32 devices in a mesh: dp: 2 (over x), ctx: 16 (over z, y, core).
Axes of the slice: x: 2, y: 2, z: 4, core: 2. Of those that a mesh axis runs over, the one named last changes fastest.
Arguments:
- pre_gate: bfloat16 [2048, 4096], P('dp', 'ctx'), may hold values from -6 to 6
- values: bfloat16 [2048, 4096], P('dp', 'ctx'), may hold values from -6 to 6
- post_gate: bfloat16 [2048, 4096], P('dp', 'ctx'), may hold values from -6 to 6
- filters: float32 [256, 4096], P('ctx', 'dp'), may hold values from -0.09375 to 0.09375
- cotangent: bfloat16 [2048, 4096], P('dp', 'ctx'), may hold values from -6 to 6
Outputs:
- mixed: bfloat16 [2048, 4096], P('dp', 'ctx')
- pre_grad: bfloat16 [2048, 4096], P('dp', 'ctx')
- value_grad: bfloat16 [2048, 4096], P('dp', 'ctx')
- post_grad: bfloat16 [2048, 4096], P('dp', 'ctx')
- filter_grad: float32 [256, 4096], P('ctx', 'dp')
The draws below stay inside these ranges and needn't reach their ends.
All inputs are finite; a program needn't handle non-finite values.
Results may differ from the reference program's by a relative error of at most 0.014.
Values may be sent and summed in bfloat16 or wider, within the bound.
No kernel may reach another device: no remote copies, remote signals or barrier semaphores. Data moves between devices by JAX's collectives and lax.ppermute only.
A program may use at most 64 MiB of HBM per device.

```python
import jax
import jax.numpy as jnp
from jax import lax

D = 2048
FG = 256
L = 4096


def levels(stream_key, shape, split, smallest, top_value):
    gain, own = 1.0, jax.random.fold_in(stream_key, 6)
    for axis_at, parts in split:
        draws = jnp.exp(jax.random.uniform(jax.random.fold_in(own, axis_at), (parts,), jnp.float32, smallest / len(split), top_value / len(split)))
        gain = gain * jnp.repeat(draws, shape[axis_at] // parts).reshape([-1 if axis == axis_at else 1 for axis in range(len(shape))])
    return gain


def gaussian(key, extent, spread, most, pieces=(), kind=jnp.bfloat16):
    result = jax.random.normal(key, extent, jnp.float32) * spread
    if len(pieces) > 0:
        result = levels(key, extent, pieces, -0.22, 0.18) * result
    return jnp.clip(result, min=-most, max=most).astype(kind)


def setup_inputs(seed: int = 0) -> dict:
    key_of = jax.random.split(jax.random.key(seed), 6)
    pre_gate = gaussian(key_of[0], (D, L), 1.0, 6.0, ((0, 2), (1, 16)))
    values = gaussian(key_of[1], (D, L), 1.0, 6.0, ((0, 2), (1, 16)))
    post_gate = gaussian(key_of[2], (D, L), 1.0, 6.0, ((0, 2), (1, 16)))
    filters = gaussian(key_of[3], (FG, L), L ** -0.5, 0.09375, ((0, 16), (1, 2)), jnp.float32)
    cotangent = gaussian(key_of[4], (D, L), 1.0, 6.0, ((0, 2), (1, 16)))
    return dict(pre_gate=pre_gate, values=values, post_gate=post_gate, filters=filters, cotangent=cotangent)


def reference(pre_gate, values, post_gate, filters, cotangent):
    count = filters.shape[0]
    length = filters.shape[1]
    points = 2 * length
    repeats = pre_gate.shape[0] // count
    filter_spec = jnp.fft.rfft(filters, n=points, axis=-1)

    def split_rows(array):
        return array.reshape(repeats, count, length)

    def one_group(carry, items):
        pre_row, value_row, post_row, cot_row = items
        gated = (pre_row.astype(jnp.float32) * value_row.astype(jnp.float32)).astype(jnp.bfloat16)
        gated_spec = jnp.fft.rfft(gated.astype(jnp.float32), n=points, axis=-1)
        conv = jnp.fft.irfft(gated_spec * filter_spec, n=points, axis=-1)[:, :length].astype(jnp.bfloat16)
        mixed = (post_row.astype(jnp.float32) * conv.astype(jnp.float32)).astype(jnp.bfloat16)
        post_grad = (cot_row.astype(jnp.float32) * conv.astype(jnp.float32)).astype(jnp.bfloat16)
        conv_grad = (cot_row.astype(jnp.float32) * post_row.astype(jnp.float32)).astype(jnp.bfloat16)
        grad_spec = jnp.fft.rfft(conv_grad.astype(jnp.float32), n=points, axis=-1)
        gated_grad = jnp.fft.irfft(jnp.conj(filter_spec) * grad_spec, n=points, axis=-1)[:, :length].astype(jnp.bfloat16)
        pre_grad = (gated_grad.astype(jnp.float32) * value_row.astype(jnp.float32)).astype(jnp.bfloat16)
        value_grad = (gated_grad.astype(jnp.float32) * pre_row.astype(jnp.float32)).astype(jnp.bfloat16)
        filter_term = jnp.fft.irfft(jnp.conj(gated_spec) * grad_spec, n=points, axis=-1)[:, :length]
        return carry + filter_term, (mixed, pre_grad, value_grad, post_grad)

    start = jnp.zeros(filters.shape, jnp.float32)
    total, outputs = lax.scan(one_group, start, (split_rows(pre_gate), split_rows(values), split_rows(post_gate), split_rows(cotangent)))
    shape = pre_gate.shape
    return outputs[0].reshape(shape), outputs[1].reshape(shape), outputs[2].reshape(shape), outputs[3].reshape(shape), total
```

```python
import math

import jax
import jax.numpy as jnp
import numpy as np
from jax import lax
from jax.experimental import pallas as pl
from jax.experimental.pallas import tpu as pltpu
from jax.sharding import PartitionSpec as P

LANES = 128
SUBLANES = 8


def dft_tables(tokens):
    angle = np.arange(tokens)[:, None] * (2.0 * np.arange(tokens)[None, :] + 1.0) * (math.pi / (2 * tokens))
    forward = np.concatenate([np.cos(angle), -np.sin(angle)], axis=1)
    inverse = np.concatenate([np.cos(angle).T, -np.sin(angle).T], axis=0) / tokens
    sign = np.where(np.arange(tokens) % 2 == 0, 1.0, -1.0)[None, :]
    return (
        jnp.asarray(forward, jnp.bfloat16),
        jnp.asarray(inverse, jnp.bfloat16),
        jnp.asarray(sign, jnp.float32),
    )


def dot(left, right):
    return jnp.dot(left, right, preferred_element_type=jnp.float32)


def gate_kernel(pre_ref, value_ref, post_ref, cot_ref, out_ref):
    blocks, _, _, rows, tokens = out_ref.shape
    gated = pre_ref[...].astype(jnp.float32) * value_ref[...].astype(jnp.float32)
    grad = cot_ref[...].astype(jnp.float32) * post_ref[...].astype(jnp.float32)
    out_ref[:, 0, 0] = gated.astype(jnp.bfloat16).reshape(blocks, rows, tokens)
    out_ref[:, 1, 0] = grad.astype(jnp.bfloat16).reshape(blocks, rows, tokens)


def gate(pre_gate, values, post_gate, cotangent, repeats, blocks):
    rows_all, tokens = pre_gate.shape
    rows = rows_all // (repeats * blocks)
    spec = pl.BlockSpec((blocks * rows, tokens), lambda r: (r, 0))
    return pl.pallas_call(
        gate_kernel,
        grid=(repeats,),
        in_specs=[spec] * 4,
        out_specs=pl.BlockSpec((blocks, 2, 1, rows, tokens), lambda r: (0, 0, r, 0, 0)),
        out_shape=jax.ShapeDtypeStruct((blocks, 2, repeats, rows, tokens), jnp.bfloat16),
        name="gate",
    )(pre_gate, values, post_gate, cotangent)


def finish_kernel(recv_ref, pre_ref, value_ref, post_ref, cot_ref, mixed_ref, pre_grad_ref, value_grad_ref, post_grad_ref):
    shape = pre_ref.shape
    conv = recv_ref[:, 0, 0].reshape(shape).astype(jnp.float32)
    grad = recv_ref[:, 1, 0].reshape(shape).astype(jnp.float32)
    mixed_ref[...] = (post_ref[...].astype(jnp.float32) * conv).astype(jnp.bfloat16)
    post_grad_ref[...] = (cot_ref[...].astype(jnp.float32) * conv).astype(jnp.bfloat16)
    pre_grad_ref[...] = (grad * value_ref[...].astype(jnp.float32)).astype(jnp.bfloat16)
    value_grad_ref[...] = (grad * pre_ref[...].astype(jnp.float32)).astype(jnp.bfloat16)


def finish(received, pre_gate, values, post_gate, cotangent):
    blocks, _, repeats, rows, tokens = received.shape
    spec = pl.BlockSpec((blocks * rows, tokens), lambda r: (r, 0))
    return pl.pallas_call(
        finish_kernel,
        grid=(repeats,),
        in_specs=[pl.BlockSpec((blocks, 2, 1, rows, tokens), lambda r: (0, 0, r, 0, 0))] + [spec] * 4,
        out_specs=[spec] * 4,
        out_shape=[jax.ShapeDtypeStruct(pre_gate.shape, jnp.bfloat16)] * 4,
        name="finish",
    )(received, pre_gate, values, post_gate, cotangent)


def transform_rows(source, table_ref, target_ref, blocks, group):
    @pl.loop(0, blocks // group)
    def _(step):
        at = step * group
        piece = source(at, group)
        count, rows, tokens = piece.shape
        result = dot(piece.reshape(count * rows, tokens), table_ref[...])
        target_ref[pl.ds(at, group)] = result.reshape(count, rows, result.shape[1])


def convolve_kernel(recv_ref, tap_ref, forward_ref, inverse_ref, sign_ref, out_ref, spec_ref, prod_ref, filt_ref):
    blocks, _, rows, tokens = out_ref.shape
    filters = tap_ref.shape[1]
    taps = dot(tap_ref[...].reshape(blocks * filters, tokens), forward_ref[...])
    taps = taps.reshape(blocks, filters, 2 * tokens)
    sign = sign_ref[...]
    filt_ref[0] = taps[0]
    for k in range(1, blocks):
        filt_ref[k, :, :tokens] = taps[k, :, :tokens] - sign * taps[k - 1, :, tokens:]
        filt_ref[k, :, tokens:] = taps[k, :, tokens:] + sign * taps[k - 1, :, :tokens]

    strips = tokens // LANES
    halves = filters // SUBLANES

    def one_side(which):
        def source(at, count):
            return recv_ref[pl.ds(at, count), which]

        transform_rows(source, forward_ref, spec_ref, blocks, 4)

        @pl.loop(0, rows // SUBLANES)
        def _(tile):
            row = pl.multiple_of(tile * SUBLANES, SUBLANES)
            tap_row = pl.multiple_of(lax.rem(tile, halves) * SUBLANES, SUBLANES)
            for strip in range(strips):
                real = pl.ds(strip * LANES, LANES)
                imag = pl.ds(tokens + strip * LANES, LANES)
                spans = [
                    (spec_ref[j, pl.ds(row, SUBLANES), real], spec_ref[j, pl.ds(row, SUBLANES), imag])
                    for j in range(blocks)
                ]
                for out in range(blocks):
                    total_real = total_imag = None
                    for lag in range(out + 1 if which == 0 else blocks - out):
                        tap_real = filt_ref[lag, pl.ds(tap_row, SUBLANES), real]
                        tap_imag = filt_ref[lag, pl.ds(tap_row, SUBLANES), imag]
                        if which == 0:
                            in_real, in_imag = spans[out - lag]
                            term_real = in_real * tap_real - in_imag * tap_imag
                            term_imag = in_real * tap_imag + in_imag * tap_real
                        else:
                            in_real, in_imag = spans[out + lag]
                            term_real = in_real * tap_real + in_imag * tap_imag
                            term_imag = in_imag * tap_real - in_real * tap_imag
                        total_real = term_real if total_real is None else total_real + term_real
                        total_imag = term_imag if total_imag is None else total_imag + term_imag
                    prod_ref[out, pl.ds(row, SUBLANES), real] = total_real
                    prod_ref[out, pl.ds(row, SUBLANES), imag] = total_imag

        group = 4

        @pl.loop(0, blocks // group)
        def _(step):
            at = step * group
            piece = prod_ref[pl.ds(at, group)].astype(jnp.bfloat16)
            result = dot(piece.reshape(group * rows, 2 * tokens), inverse_ref[...])
            out_ref[pl.ds(at, group), which] = result.astype(jnp.bfloat16).reshape(group, rows, tokens)

    one_side(0)
    one_side(1)


def convolve(received, taps, tables):
    blocks, _, rows, tokens = received.shape
    forward, inverse, sign = tables
    pairs = blocks * (blocks + 1) // 2
    return pl.pallas_call(
        convolve_kernel,
        out_shape=jax.ShapeDtypeStruct((blocks, 2, rows, tokens), jnp.bfloat16),
        scratch_shapes=[
            pltpu.VMEM((blocks, rows, 2 * tokens), jnp.float32),
            pltpu.VMEM((blocks, rows, 2 * tokens), jnp.float32),
            pltpu.VMEM((blocks, taps.shape[1], 2 * tokens), jnp.float32),
        ],
        compiler_params=pltpu.CompilerParams(vmem_limit_bytes=32 * 1024 * 1024),
        cost_estimate=pl.CostEstimate(
            flops=16 * blocks * rows * tokens * tokens + 16 * pairs * rows * tokens,
            bytes_accessed=8 * blocks * rows * tokens,
            transcendentals=0,
        ),
        name="convolve",
    )(received, taps, forward, inverse, sign)


def correlate_kernel(recv_ref, forward_ref, inverse_ref, sign_ref, out_ref, gated_ref, grad_ref, cross_ref):
    blocks, _, rows, tokens = recv_ref.shape
    filters = out_ref.shape[1]
    for which, target_ref in ((0, gated_ref), (1, grad_ref)):
        def source(at, count, which=which):
            return recv_ref[pl.ds(at, count), which]

        transform_rows(source, forward_ref, target_ref, blocks, 4)

    strips = tokens // LANES
    halves = filters // SUBLANES
    repeats = rows // filters

    @pl.loop(0, halves)
    def _(half):
        tap_row = pl.multiple_of(half * SUBLANES, SUBLANES)
        for strip in range(strips):
            real = pl.ds(strip * LANES, LANES)
            imag = pl.ds(tokens + strip * LANES, LANES)

            @pl.loop(0, repeats)
            def _(repeat):
                row = pl.multiple_of(repeat * filters + half * SUBLANES, SUBLANES)
                spans = [
                    (grad_ref[j, pl.ds(row, SUBLANES), real], grad_ref[j, pl.ds(row, SUBLANES), imag])
                    for j in range(blocks)
                ]
                for lag in range(blocks):
                    total_real = total_imag = None
                    for at in range(blocks - lag):
                        in_real = gated_ref[at, pl.ds(row, SUBLANES), real]
                        in_imag = gated_ref[at, pl.ds(row, SUBLANES), imag]
                        out_real, out_imag = spans[at + lag]
                        term_real = in_real * out_real + in_imag * out_imag
                        term_imag = in_real * out_imag - in_imag * out_real
                        total_real = term_real if total_real is None else total_real + term_real
                        total_imag = term_imag if total_imag is None else total_imag + term_imag
                    keep = jnp.where(repeat == 0, 0.0, 1.0)
                    cross_ref[lag, pl.ds(tap_row, SUBLANES), real] = total_real + keep * cross_ref[lag, pl.ds(tap_row, SUBLANES), real]
                    cross_ref[lag, pl.ds(tap_row, SUBLANES), imag] = total_imag + keep * cross_ref[lag, pl.ds(tap_row, SUBLANES), imag]

    sign = sign_ref[...]
    for k in range(blocks):
        cross_real = cross_ref[k, :, :tokens]
        cross_imag = cross_ref[k, :, tokens:]
        if k + 1 < blocks:
            cross_real = cross_real + sign * cross_ref[k + 1, :, tokens:]
            cross_imag = cross_imag - sign * cross_ref[k + 1, :, :tokens]
        joined = jnp.concatenate([cross_real, cross_imag], axis=1).astype(jnp.bfloat16)
        out_ref[k] = dot(joined, inverse_ref[...])


def correlate(received, filters, tables):
    blocks, _, rows, tokens = received.shape
    forward, inverse, sign = tables
    pairs = blocks * (blocks + 1) // 2
    return pl.pallas_call(
        correlate_kernel,
        out_shape=jax.ShapeDtypeStruct((blocks, filters, tokens), jnp.float32),
        scratch_shapes=[
            pltpu.VMEM((blocks, rows, 2 * tokens), jnp.float32),
            pltpu.VMEM((blocks, rows, 2 * tokens), jnp.float32),
            pltpu.VMEM((blocks, filters, 2 * tokens), jnp.float32),
        ],
        compiler_params=pltpu.CompilerParams(vmem_limit_bytes=32 * 1024 * 1024),
        cost_estimate=pl.CostEstimate(
            flops=8 * blocks * rows * tokens * tokens + 8 * pairs * rows * tokens,
            bytes_accessed=6 * blocks * rows * tokens,
            transcendentals=0,
        ),
        name="correlate",
    )(received, forward, inverse, sign)


def body(pre_gate, values, post_gate, filters, cotangent):
    blocks = lax.axis_size("ctx")
    groups = lax.axis_size("dp")
    local_rows, tokens = pre_gate.shape
    local_filters = filters.shape[0]
    repeats = local_rows // (local_filters * blocks)
    share = blocks // groups
    tables = dft_tables(tokens)
    tap_local = jnp.transpose(filters.reshape(local_filters, share, tokens), (1, 0, 2)).astype(jnp.bfloat16)
    group = lax.axis_index("dp")
    swap = [(0, 1), (1, 0)]
    tap_other = lax.ppermute(tap_local, "dp", swap)
    sent = gate(pre_gate, values, post_gate, cotangent, repeats, blocks)
    received = lax.all_to_all(sent, "ctx", split_axis=0, concat_axis=0, tiled=True)
    received = received.reshape(blocks, 2, repeats * local_filters, tokens)
    taps = jnp.where(
        group == 0,
        jnp.concatenate([tap_local, tap_other]),
        jnp.concatenate([tap_other, tap_local]),
    )
    result = convolve(received, taps, tables)
    returned = lax.all_to_all(result, "ctx", split_axis=0, concat_axis=0, tiled=True)
    term = correlate(received, local_filters, tables)
    low, high = term[:share], term[share:]
    mine = jnp.where(group == 0, low, high)
    theirs = jnp.where(group == 0, high, low).astype(jnp.bfloat16)
    summed = mine + lax.ppermute(theirs, "dp", swap).astype(jnp.float32)
    filter_grad = jnp.transpose(summed, (1, 0, 2)).reshape(local_filters, share * tokens)
    returned = returned.reshape(blocks, 2, repeats, local_filters, tokens)
    mixed, pre_grad, value_grad, post_grad = finish(returned, pre_gate, values, post_gate, cotangent)
    return (mixed, pre_grad, value_grad, post_grad, filter_grad)


def matmul(left, right):
    return jnp.dot(left, right, precision=lax.Precision.HIGHEST, preferred_element_type=jnp.float32)


def contract(form, left, right):
    return jnp.einsum(
        form, left, right, precision=lax.Precision.HIGHEST, preferred_element_type=jnp.float32
    )


def phases(height, width, modulus):
    product = lax.broadcasted_iota(jnp.int32, (height, width), 0) * lax.broadcasted_iota(
        jnp.int32, (height, width), 1
    )
    return (product % modulus).astype(jnp.float32) * (2.0 * math.pi / modulus)


def build_tables(blocks, tokens):
    factor = 1
    for candidate in range(1, tokens + 1):
        if tokens % candidate == 0 and candidate * candidate <= tokens:
            factor = candidate
    second = tokens // factor
    rows = blocks + 1
    total = 2 * blocks * tokens
    first_angle = phases(rows, blocks, 2 * blocks)
    twist_angle = phases(rows, tokens, total)
    inner_angle = phases(factor, factor, factor)
    middle_angle = phases(factor, second, tokens)
    outer_angle = phases(second, second, second)
    back_angle = phases(blocks, rows, 2 * blocks)
    column = lax.broadcasted_iota(jnp.int32, (blocks, rows), 1)
    weight = jnp.where((column == 0) | (column == blocks), 1.0, 2.0).astype(jnp.float32) / total
    return {
        "first_cos": jnp.cos(first_angle),
        "first_nsin": -jnp.sin(first_angle),
        "twist_cos": jnp.cos(twist_angle),
        "twist_sin": jnp.sin(twist_angle),
        "inner_cos": jnp.cos(inner_angle),
        "inner_sin": jnp.sin(inner_angle),
        "middle_cos": jnp.cos(middle_angle),
        "middle_sin": jnp.sin(middle_angle),
        "outer_cos": jnp.cos(outer_angle),
        "outer_sin": jnp.sin(outer_angle),
        "back_cos": weight * jnp.cos(back_angle),
        "back_sin": weight * jnp.sin(back_angle),
    }


def expand(table, ndim):
    return table.reshape((table.shape[0],) + (1,) * (ndim - 2) + (table.shape[1],))


def block_table(cos_part, sin_part):
    return jnp.stack([jnp.stack([cos_part, sin_part]), jnp.stack([-sin_part, cos_part])])


def wave(real_part, imag_part, tables, sign):
    shape = real_part.shape
    factor = tables["inner_cos"].shape[0]
    second = tables["outer_cos"].shape[0]
    stacked = jnp.stack(
        [real_part.reshape(-1, factor, second), imag_part.reshape(-1, factor, second)]
    )
    inner_table = block_table(tables["inner_cos"], sign * tables["inner_sin"])
    middle = contract("prab,pqac->qrcb", stacked, inner_table)
    middle_cos = tables["middle_cos"]
    middle_sin = sign * tables["middle_sin"]
    real_turn = middle[0] * middle_cos - middle[1] * middle_sin
    imag_turn = middle[0] * middle_sin + middle[1] * middle_cos
    turned = jnp.stack([real_turn, imag_turn])
    outer_table = block_table(tables["outer_cos"], sign * tables["outer_sin"])
    result = contract("prcb,pqbd->qrdc", turned, outer_table)
    return (result[0].reshape(shape), result[1].reshape(shape))


def finish_forward(real_first, imag_first, tables):
    ndim = real_first.ndim
    twist_cos = expand(tables["twist_cos"], ndim)
    twist_sin = expand(tables["twist_sin"], ndim)
    real_twist = real_first * twist_cos + imag_first * twist_sin
    imag_twist = imag_first * twist_cos - real_first * twist_sin
    return wave(real_twist, imag_twist, tables, -1.0)


def spectrum(signal, tables):
    flat = signal.reshape(signal.shape[0], -1)
    shape = (tables["first_cos"].shape[0],) + signal.shape[1:]
    real_first = matmul(tables["first_cos"], flat).reshape(shape)
    imag_first = matmul(tables["first_nsin"], flat).reshape(shape)
    return finish_forward(real_first, imag_first, tables)


def inverse_prepare(real_spec, imag_spec, tables):
    ndim = real_spec.ndim
    real_wave, imag_wave = wave(real_spec, imag_spec, tables, 1.0)
    twist_cos = expand(tables["twist_cos"], ndim)
    twist_sin = expand(tables["twist_sin"], ndim)
    real_twist = real_wave * twist_cos - imag_wave * twist_sin
    imag_twist = real_wave * twist_sin + imag_wave * twist_cos
    rows = real_spec.shape[0]
    return (real_twist.reshape(rows, -1), imag_twist.reshape(rows, -1))


def inverse_full(real_spec, imag_spec, tables):
    real_flat, imag_flat = inverse_prepare(real_spec, imag_spec, tables)
    signal = matmul(tables["back_cos"], real_flat) - matmul(tables["back_sin"], imag_flat)
    return signal.reshape((tables["back_cos"].shape[0],) + real_spec.shape[1:])


def plain_body(pre_gate, values, post_gate, filters, cotangent):
    blocks = lax.axis_size("ctx")
    groups = lax.axis_size("dp")
    local_rows = pre_gate.shape[0]
    tokens = pre_gate.shape[1]
    local_filters = filters.shape[0]
    repeats = local_rows // (local_filters * blocks)
    share = blocks // groups
    tables = build_tables(blocks, tokens)
    gated = (pre_gate.astype(jnp.float32) * values.astype(jnp.float32)).astype(jnp.bfloat16)
    conv_grad = (cotangent.astype(jnp.float32) * post_gate.astype(jnp.float32)).astype(jnp.bfloat16)
    gated_blocks = gated.reshape(repeats, blocks, local_filters, tokens)
    grad_blocks = conv_grad.reshape(repeats, blocks, local_filters, tokens)
    tap_local = jnp.transpose(filters.reshape(local_filters, share, tokens), (1, 0, 2))
    piece = lax.all_gather(tap_local, "dp", axis=0, tiled=True)
    count = piece.shape[0]
    flat = piece.reshape(count, -1)
    cos_cols = tables["first_cos"]
    sin_cols = tables["first_nsin"]
    real_first = matmul(cos_cols, flat)
    imag_first = matmul(sin_cols, flat)
    spec_shape = (blocks + 1, 1, local_filters, tokens)
    filt_real, filt_imag = finish_forward(
        real_first.reshape(spec_shape), imag_first.reshape(spec_shape), tables
    )

    def single_spectrum(received):
        signal = received.reshape(blocks, -1, received.shape[2], received.shape[3])
        return spectrum(signal.astype(jnp.float32), tables)

    gated_real, gated_imag = single_spectrum(
        lax.all_to_all(gated_blocks, "ctx", split_axis=1, concat_axis=0, tiled=True)
    )
    prod_real = gated_real * filt_real - gated_imag * filt_imag
    prod_imag = gated_real * filt_imag + gated_imag * filt_real
    result = inverse_full(prod_real, prod_imag, tables).astype(jnp.bfloat16)
    conv_chan = result.reshape(blocks * repeats, 1, local_filters, tokens)
    conv_seq = lax.all_to_all(conv_chan, "ctx", split_axis=0, concat_axis=1, tiled=True)
    grad_real, grad_imag = single_spectrum(
        lax.all_to_all(grad_blocks, "ctx", split_axis=1, concat_axis=0, tiled=True)
    )
    prod_real = filt_real * grad_real + filt_imag * grad_imag
    prod_imag = filt_real * grad_imag - filt_imag * grad_real
    result = inverse_full(prod_real, prod_imag, tables).astype(jnp.bfloat16)
    gated_chan_grad = result.reshape(blocks * repeats, 1, local_filters, tokens)
    gated_seq_grad = lax.all_to_all(gated_chan_grad, "ctx", split_axis=0, concat_axis=1, tiled=True)
    cross_real = jnp.sum(gated_real * grad_real + gated_imag * grad_imag, axis=1)
    cross_imag = jnp.sum(gated_real * grad_imag - gated_imag * grad_real, axis=1)
    wave_real, wave_imag = inverse_prepare(cross_real, cross_imag, tables)
    cos_rows = tables["back_cos"]
    sin_rows = tables["back_sin"]
    term = matmul(cos_rows, wave_real) - matmul(sin_rows, wave_imag)
    summed = lax.psum_scatter(
        term.reshape(lax.axis_size("dp") * share, local_filters, tokens).astype(jnp.bfloat16),
        "dp",
        scatter_dimension=0,
        tiled=True,
    ).astype(jnp.float32)
    filter_grad = jnp.transpose(summed, (1, 0, 2)).reshape(local_filters, share * tokens)
    conv_full = conv_seq.reshape(pre_gate.shape).astype(jnp.float32)
    gated_grad = gated_seq_grad.reshape(pre_gate.shape).astype(jnp.float32)
    mixed = (post_gate.astype(jnp.float32) * conv_full).astype(jnp.bfloat16)
    post_grad = (cotangent.astype(jnp.float32) * conv_full).astype(jnp.bfloat16)
    pre_grad = (gated_grad * values.astype(jnp.float32)).astype(jnp.bfloat16)
    value_grad = (gated_grad * pre_gate.astype(jnp.float32)).astype(jnp.bfloat16)
    return (mixed, pre_grad, value_grad, post_grad, filter_grad)


def solution(mesh):
    placed = (P("dp", "ctx"), P("dp", "ctx"), P("dp", "ctx"), P("ctx", "dp"), P("dp", "ctx"))

    def program(pre_gate, values, post_gate, filters, cotangent):
        kernels = mesh.shape["dp"] == 2 and mesh.shape["ctx"] <= 16 and filters.shape[0] % 16 == 0
        return (body if kernels else plain_body)(pre_gate, values, post_gate, filters, cotangent)

    return jax.shard_map(
        program,
        mesh=mesh,
        in_specs=placed,
        out_specs=(P("dp", "ctx"), P("dp", "ctx"), P("dp", "ctx"), P("dp", "ctx"), P("ctx", "dp")),
        check_vma=False,
    )
```

```python
import math

import jax
import jax.numpy as jnp
import numpy as np
from jax import lax
from jax.experimental import pallas as pl
from jax.experimental.pallas import tpu as pltpu
from jax.sharding import PartitionSpec as P


LANES = 128
SUBLANES = 8
VMEM_BYTES = 48 * 1024 * 1024


def dft_tables(size):
    angle = np.arange(size)[:, None] * (2.0 * np.arange(size)[None, :] + 1.0) * (math.pi / (2 * size))
    strips = size // LANES
    cos, sin = (part.reshape(size, strips, 1, LANES) for part in (np.cos(angle), np.sin(angle)))
    table = np.concatenate([cos, -sin], axis=2).reshape(size, 2 * size)
    return jnp.asarray(table, jnp.bfloat16), jnp.asarray(table.T / size, jnp.bfloat16)


def dot(left, right):
    return jnp.dot(left, right, preferred_element_type=jnp.float32)


def alternating():
    odd = lax.broadcasted_iota(jnp.int32, (SUBLANES, LANES), 1) % 2
    return 1.0 - 2.0 * odd.astype(jnp.float32)


def place(half_blocks):
    index = lax.axis_index("ctx")
    return index // half_blocks, lax.rem(index, half_blocks)


def real_of(strip):
    return pl.ds(2 * strip * LANES, LANES)


def imag_of(strip):
    return pl.ds((2 * strip + 1) * LANES, LANES)


def gate_kernel(near, half_blocks, pre_ref, value_ref, post_ref, cot_ref, *refs):
    out_refs, (left_ref, right_ref, result_ref, in_sems, out_sems) = refs[:-5], refs[-5:]
    repeats, rows, tokens = left_ref.shape
    share = rows // half_blocks
    half, me = place(half_blocks)
    use_gated = half == 0 if near else half != 0

    def fetch(r, left, right):
        at = pl.ds(r * rows, rows)
        return (
            pltpu.make_async_copy(left.at[at], left_ref.at[r], in_sems.at[0, r]),
            pltpu.make_async_copy(right.at[at], right_ref.at[r], in_sems.at[1, r]),
        )

    @pl.when(use_gated)
    def _():
        for r in range(repeats):
            for copy in fetch(r, pre_ref, value_ref):
                copy.start()

    @pl.when(jnp.logical_not(use_gated))
    def _():
        for r in range(repeats):
            for copy in fetch(r, cot_ref, post_ref):
                copy.start()

    pending = []
    for r in range(repeats):
        for copy in fetch(r, pre_ref, value_ref):
            copy.wait()
        product = left_ref[r].astype(jnp.float32) * right_ref[r].astype(jnp.float32)
        product = product.astype(jnp.bfloat16).reshape(half_blocks, share, tokens)
        if near:
            result_ref[r] = product
            for side in range(2):
                copy = pltpu.make_async_copy(result_ref.at[r], out_refs[0].at[side, :, r], out_sems.at[side, r])
                copy.start()
                pending.append(copy)
        else:
            result_ref[:, r] = product
    if not near:
        even_ref, odd_ref = out_refs
        for at in range(half_blocks // 2):
            slot = slot_order(half_blocks)[at]
            for side, target in ((0, even_ref), (1, odd_ref)):
                source = result_ref.at[jnp.bitwise_xor(me, slot + side)]
                copy = pltpu.make_async_copy(source, target.at[at], out_sems.at[side, at])
                copy.start()
                pending.append(copy)
    for copy in pending:
        copy.wait()


def slot_order(half_blocks):
    return [s for s in range(0, half_blocks, 2) if not s & 2] + [s for s in range(0, half_blocks, 2) if s & 2]


def gate(near, arrays, repeats, half_blocks):
    rows_all, tokens = arrays[0].shape
    rows = rows_all // repeats
    share = rows // half_blocks
    if near:
        shapes = [(2, half_blocks, repeats, share, tokens)]
        held, count = (repeats, half_blocks, share, tokens), repeats
    else:
        shapes = [(half_blocks // 2, repeats, share, tokens)] * 2
        held, count = (half_blocks, repeats, share, tokens), half_blocks // 2
    result = pl.pallas_call(
        lambda *refs: gate_kernel(near, half_blocks, *refs),
        in_specs=[pl.BlockSpec(memory_space=pl.ANY)] * 4,
        out_specs=[pl.BlockSpec(memory_space=pl.ANY)] * len(shapes),
        out_shape=[jax.ShapeDtypeStruct(shape, jnp.bfloat16) for shape in shapes],
        scratch_shapes=[
            pltpu.VMEM((repeats, rows, tokens), jnp.bfloat16),
            pltpu.VMEM((repeats, rows, tokens), jnp.bfloat16),
            pltpu.VMEM(held, jnp.bfloat16),
            pltpu.SemaphoreType.DMA((2, repeats)),
            pltpu.SemaphoreType.DMA((2, count)),
        ],
        compiler_params=pltpu.CompilerParams(vmem_limit_bytes=VMEM_BYTES),
        cost_estimate=pl.CostEstimate(flops=rows_all * tokens, bytes_accessed=8 * rows_all * tokens, transcendentals=0),
        name="gate_near" if near else "gate_own",
    )(*arrays)
    return result[0] if near else result


def finish_kernel(half_blocks, recv_ref, pre_ref, value_ref, post_ref, cot_ref, *refs):
    out_refs, (held_ref, sems) = refs[:4], refs[4:]
    repeats = recv_ref.shape[2]
    rows, tokens = held_ref.shape[2:]
    half, _ = place(half_blocks)
    pending = []
    for r in range(repeats):
        at = pl.ds(r * rows, rows)
        conv = recv_ref[:, half, r].reshape(rows, tokens).astype(jnp.float32)
        grad = recv_ref[:, 1 - half, r].reshape(rows, tokens).astype(jnp.float32)
        for which, (factor_ref, result) in enumerate(
            ((post_ref, conv), (value_ref, grad), (pre_ref, grad), (cot_ref, conv))
        ):
            held_ref[which, r] = (factor_ref[at].astype(jnp.float32) * result).astype(jnp.bfloat16)
            copy = pltpu.make_async_copy(held_ref.at[which, r], out_refs[which].at[at], sems.at[which, r])
            copy.start()
            pending.append(copy)
    for copy in pending:
        copy.wait()


def finish(received, pre_gate, values, post_gate, cotangent):
    half_blocks, _, repeats, share, tokens = received.shape
    rows = half_blocks * share
    return pl.pallas_call(
        lambda *refs: finish_kernel(half_blocks, *refs),
        in_specs=[pl.BlockSpec(memory_space=pltpu.VMEM)] * 5,
        out_specs=[pl.BlockSpec(memory_space=pl.ANY)] * 4,
        out_shape=[jax.ShapeDtypeStruct(pre_gate.shape, jnp.bfloat16)] * 4,
        scratch_shapes=[
            pltpu.VMEM((4, repeats, rows, tokens), jnp.bfloat16),
            pltpu.SemaphoreType.DMA((4, repeats)),
        ],
        compiler_params=pltpu.CompilerParams(vmem_limit_bytes=VMEM_BYTES),
        name="finish",
    )(received, pre_gate, values, post_gate, cotangent)


def taps_kernel(half_blocks, first_ref, second_ref, forward_ref, out_ref, stage_ref):
    count, rows, width = out_ref.shape
    size = width // 2
    share, tokens = first_ref.shape[1:]
    merge = size // tokens
    half, _ = place(half_blocks)
    low, high = first_ref[...], second_ref[...]
    ordered = (jnp.where(half == 0, low, high), jnp.where(half == 0, high, low))
    for part in range(2):
        for k in range(count):
            for q in range(merge):
                stage_ref[k, pl.ds(part * share, share), pl.ds(q * tokens, tokens)] = ordered[part][k * merge + q]
    spectrum = dot(stage_ref[...].reshape(count * rows, size), forward_ref[...]).reshape(count, rows, width)
    turn = jnp.where(half == 0, 1.0, -1.0).astype(jnp.float32)
    sign = alternating()[:1]
    for k in range(count):
        for strip in range(size // LANES):
            re, im = slice(2 * strip * LANES, (2 * strip + 1) * LANES), slice((2 * strip + 1) * LANES, (2 * strip + 2) * LANES)
            real, imag = spectrum[k, :, re], spectrum[k, :, im]
            if k > 0:
                real, imag = real - sign * spectrum[k - 1, :, im], imag + sign * spectrum[k - 1, :, re]
            out_ref[k, :, re] = real
            out_ref[k, :, im] = turn * imag


def transform_taps(first, second, half_blocks, size, forward):
    blocks, share, tokens = first.shape
    count = blocks * tokens // size
    return pl.pallas_call(
        lambda *refs: taps_kernel(half_blocks, *refs),
        out_shape=jax.ShapeDtypeStruct((count, 2 * share, 2 * size), jnp.float32),
        scratch_shapes=[pltpu.VMEM((count, 2 * share, size), jnp.bfloat16)],
        compiler_params=pltpu.CompilerParams(vmem_limit_bytes=VMEM_BYTES),
        name="taps",
    )(first, second, forward)


def exchange_own(even, odd, half_blocks):
    blocks = 2 * half_blocks

    def swap(array, bit):
        return lax.ppermute(array, "ctx", [(i, i ^ bit) for i in range(blocks)])

    order = slot_order(half_blocks)
    groups = [(list(order), even), ([s + 1 for s in order], swap(odd, 1))]
    bit = 2
    while bit < half_blocks:
        kept, leaving, leaving_slots = [], [], []
        for slots, array in groups:
            stays = [at for at, s in enumerate(slots) if not s & bit]
            goes = [at for at, s in enumerate(slots) if s & bit]
            kept.append(([slots[at] for at in stays], take(array, stays)))
            if goes:
                leaving.append(take(array, goes))
                leaving_slots += [slots[at] for at in goes]
        groups = [g for g in kept if g[0]] + [(leaving_slots, swap(jnp.concatenate(leaving), bit))]
        bit *= 2
    return groups


def take(array, rows):
    if not rows:
        return None
    if rows == list(range(rows[0], rows[0] + len(rows))):
        return array[rows[0] : rows[0] + len(rows)]
    return jnp.concatenate([array[at : at + 1] for at in rows])


def add(total, term):
    return term if total is None else (total[0] + term[0], total[1] + term[1])


def times(a, b):
    return a[0] * b[0] - a[1] * b[1], a[0] * b[1] + a[1] * b[0]


def conj_times(a, b):
    return a[0] * b[0] + a[1] * b[1], a[0] * b[1] - a[1] * b[0]


def convolve_kernel(half_blocks, slots, near_ref, *refs):
    own_refs = refs[: len(slots)]
    filt_ref, forward_ref, inverse_ref, out_ref, stage_ref, spec_ref, prod_ref = refs[len(slots) :]
    _, count, rows, width = spec_ref.shape
    size = width // 2
    tokens = near_ref.shape[2]
    merge = size // tokens
    filters = filt_ref.shape[1]
    half, _ = place(half_blocks)
    fill_stage(half_blocks, merge, near_ref, own_refs, slots, stage_ref)
    spec_ref[...] = dot(stage_ref[...].reshape(3 * count * rows, size), forward_ref[...]).reshape(spec_ref.shape)

    @pl.loop(0, rows // SUBLANES)
    def _(tile):
        row = pl.ds(pl.multiple_of(tile * SUBLANES, SUBLANES), SUBLANES)
        tap_row = pl.ds(pl.multiple_of(lax.rem(tile * SUBLANES, filters), SUBLANES), SUBLANES)
        for strip in range(size // LANES):
            def spectrum(which, k):
                return spec_ref[which, k, row, real_of(strip)], spec_ref[which, k, row, imag_of(strip)]

            taps = [
                (filt_ref[k, tap_row, real_of(strip)], filt_ref[k, tap_row, imag_of(strip)]) for k in range(2 * count)
            ]
            near = [spectrum(0, k) for k in range(count)]
            for out in range(count):
                total = None
                for k in range(out + 1):
                    total = add(total, times(taps[out - k], near[k]))
                prod_ref[0, out, row, real_of(strip)], prod_ref[0, out, row, imag_of(strip)] = total
            own = [spectrum(1, k) for k in range(count)]
            far = [spectrum(2, k) for k in range(count)]
            for out in range(count):
                total = None
                for k in range(out + 1):
                    total = add(total, conj_times(taps[out - k], own[k]))
                for k in range(count):
                    total = add(total, conj_times(taps[count + out - k], far[k]))
                prod_ref[1, out, row, real_of(strip)], prod_ref[1, out, row, imag_of(strip)] = total

    result = dot(prod_ref[...].astype(jnp.bfloat16).reshape(2 * count * rows, width), inverse_ref[...])
    result = result.astype(jnp.bfloat16).reshape(2, count, rows, size)
    for k in range(count):
        flipped = count - 1 - k
        outer = jnp.where(half == 0, k, flipped)
        inner = jnp.where(half == 0, flipped, k)
        for q in range(merge):
            lanes = slice(q * tokens, (q + 1) * tokens)
            out_ref[outer * merge + q, 0] = result[0, k, :, lanes]
            out_ref[inner * merge + q, 1] = result[1, k, :, lanes]


def fill_stage(half_blocks, merge, near_ref, own_refs, slots, stage_ref):
    count = half_blocks // merge
    tokens = near_ref.shape[2]
    half, me = place(half_blocks)
    for k in range(count):
        flipped = count - 1 - k
        outer = jnp.where(half == 0, k, flipped)
        inner = jnp.where(half == 0, flipped, k)
        for q in range(merge):
            lanes = pl.ds(q * tokens, tokens)
            stage_ref[0, k, :, lanes] = near_ref[half * half_blocks + outer * merge + q]
            stage_ref[2, k, :, lanes] = near_ref[(1 - half) * half_blocks + inner * merge + q]
    for group, ref in zip(slots, own_refs):
        for at, slot in enumerate(group):
            position = jnp.bitwise_xor(me, slot)
            block = position // merge
            k = jnp.where(half == 0, count - 1 - block, block)
            start = pl.multiple_of(lax.rem(position, merge) * tokens, tokens)
            stage_ref[1, k, :, pl.ds(start, tokens)] = ref[at]


def convolve(near, own, filt, half_blocks, tables):
    forward, inverse = tables
    _, rows, tokens = near.shape
    size = forward.shape[0]
    count = half_blocks * tokens // size
    slots = [group for group, _ in own]
    pairs = count * (2 * count + 1)
    return pl.pallas_call(
        lambda *refs: convolve_kernel(half_blocks, slots, *refs),
        out_shape=jax.ShapeDtypeStruct((half_blocks, 2, rows, tokens), jnp.bfloat16),
        scratch_shapes=[
            pltpu.VMEM((3, count, rows, size), jnp.bfloat16),
            pltpu.VMEM((3, count, rows, 2 * size), jnp.float32),
            pltpu.VMEM((2, count, rows, 2 * size), jnp.float32),
        ],
        compiler_params=pltpu.CompilerParams(vmem_limit_bytes=VMEM_BYTES),
        cost_estimate=pl.CostEstimate(
            flops=20 * count * rows * size * size + 8 * pairs * rows * size,
            bytes_accessed=10 * count * rows * size,
            transcendentals=0,
        ),
        name="convolve",
    )(near, *[array for _, array in own], filt, forward, inverse)


def correlate_kernel(half_blocks, slots, near_ref, *refs):
    own_refs = refs[: len(slots)]
    forward_ref, inverse_ref, keep_ref, give_ref, stage_ref, spec_ref, local_ref, cross_ref, joint_ref = refs[len(slots) :]
    _, count, rows, width = spec_ref.shape
    size = width // 2
    tokens = near_ref.shape[2]
    merge = size // tokens
    filters = local_ref.shape[1]
    repeats = rows // filters
    kept = filters // 2
    half, _ = place(half_blocks)
    turn = jnp.where(half == 0, 1.0, -1.0).astype(jnp.float32)
    fill_stage(half_blocks, merge, near_ref, own_refs, slots, stage_ref)
    spec_ref[...] = dot(stage_ref[...].reshape(3 * count * rows, size), forward_ref[...]).reshape(spec_ref.shape)

    def products(other, row_at, strip, lags):
        totals = [None] * len(lags)
        for repeat in range(repeats):
            row = pl.ds(pl.multiple_of(repeat * filters + row_at, SUBLANES), SUBLANES)

            def spectrum(which, k):
                return spec_ref[which, k, row, real_of(strip)], spec_ref[which, k, row, imag_of(strip)]

            near = [spectrum(0, k) for k in range(count)]
            far = [spectrum(other, k) for k in range(count)]
            for at, total in enumerate(lags):
                for a in range(count):
                    if 0 <= total - a < count:
                        totals[at] = add(totals[at], conj_times(near[a], far[total - a]))
        return totals

    @pl.loop(0, filters // SUBLANES)
    def _(tile):
        row = pl.multiple_of(tile * SUBLANES, SUBLANES)
        for strip in range(size // LANES):
            totals = products(1, row, strip, [count - 1 - k for k in range(count)])
            for k in range(count):
                local_ref[k, pl.ds(row, SUBLANES), real_of(strip)] = totals[k][0]
                local_ref[k, pl.ds(row, SUBLANES), imag_of(strip)] = turn * totals[k][1]

    @pl.loop(0, kept // SUBLANES)
    def _(tile):
        to = pl.multiple_of(tile * SUBLANES, SUBLANES)
        row = pl.multiple_of(half * kept + tile * SUBLANES, SUBLANES)
        for strip in range(size // LANES):
            totals = products(2, row, strip, [2 * count - 1 - k for k in range(1, 2 * count)])
            for k in range(1, 2 * count):
                real, imag = totals[k - 1]
                imag = turn * imag
                if k < count:
                    real = real + local_ref[k, pl.ds(row, SUBLANES), real_of(strip)]
                    imag = imag + local_ref[k, pl.ds(row, SUBLANES), imag_of(strip)]
                cross_ref[k, pl.ds(to, SUBLANES), real_of(strip)] = real
                cross_ref[k, pl.ds(to, SUBLANES), imag_of(strip)] = imag
            cross_ref[0, pl.ds(to, SUBLANES), real_of(strip)] = local_ref[0, pl.ds(row, SUBLANES), real_of(strip)]
            cross_ref[0, pl.ds(to, SUBLANES), imag_of(strip)] = local_ref[0, pl.ds(row, SUBLANES), imag_of(strip)]

    sign = alternating()[:1]
    other = pl.ds(pl.multiple_of((1 - half) * kept, SUBLANES), kept)

    def join(ref, row, lags, base):
        for k in range(lags):
            for strip in range(size // LANES):
                real, imag = ref[k, row, real_of(strip)], ref[k, row, imag_of(strip)]
                if k + 1 < lags:
                    real, imag = (
                        real + sign * ref[k + 1, row, imag_of(strip)],
                        imag - sign * ref[k + 1, row, real_of(strip)],
                    )
                joint_ref[base + k, :, real_of(strip)] = real.astype(jnp.bfloat16)
                joint_ref[base + k, :, imag_of(strip)] = imag.astype(jnp.bfloat16)

    join(cross_ref, pl.ds(0, kept), 2 * count, 0)
    join(local_ref, other, count, 2 * count)
    result = dot(joint_ref[...].reshape(3 * count * kept, width), inverse_ref[...]).reshape(3 * count, kept, size)
    for k in range(3 * count):
        for q in range(merge):
            piece = result[k, :, q * tokens : (q + 1) * tokens]
            if k < 2 * count:
                keep_ref[k * merge + q] = piece
            else:
                give_ref[(k - 2 * count) * merge + q] = piece.astype(jnp.bfloat16)


def correlate(near, own, filters, half_blocks, tables):
    forward, inverse = tables
    _, rows, tokens = near.shape
    size = forward.shape[0]
    count = half_blocks * tokens // size
    slots = [group for group, _ in own]
    pairs = count * (2 * count + 1)
    kept = filters // 2
    return pl.pallas_call(
        lambda *refs: correlate_kernel(half_blocks, slots, *refs),
        out_shape=[
            jax.ShapeDtypeStruct((2 * half_blocks, kept, tokens), jnp.float32),
            jax.ShapeDtypeStruct((half_blocks, kept, tokens), jnp.bfloat16),
        ],
        scratch_shapes=[
            pltpu.VMEM((3, count, rows, size), jnp.bfloat16),
            pltpu.VMEM((3, count, rows, 2 * size), jnp.float32),
            pltpu.VMEM((count, filters, 2 * size), jnp.float32),
            pltpu.VMEM((2 * count, kept, 2 * size), jnp.float32),
            pltpu.VMEM((3 * count, kept, 2 * size), jnp.bfloat16),
        ],
        compiler_params=pltpu.CompilerParams(vmem_limit_bytes=VMEM_BYTES),
        cost_estimate=pl.CostEstimate(
            flops=14 * count * rows * size * size + 4 * pairs * rows * size,
            bytes_accessed=8 * count * rows * size,
            transcendentals=0,
        ),
        name="correlate",
    )(near, *[array for _, array in own], forward, inverse)


def body(pre_gate, values, post_gate, filters, cotangent):
    blocks = lax.axis_size("ctx")
    groups = lax.axis_size("dp")
    half_blocks = blocks // 2
    local_rows, tokens = pre_gate.shape
    local_filters = filters.shape[0]
    repeats = local_rows // (local_filters * blocks)
    owned = 2 * local_filters
    lags = blocks // groups
    tables = dft_tables(2 * tokens)
    group = lax.axis_index("dp")
    half = lax.axis_index("ctx") // half_blocks
    arrays = (pre_gate, values, post_gate, cotangent)

    near = gate(True, arrays, repeats, half_blocks)
    near = lax.all_to_all(
        near.reshape(blocks, repeats * owned, tokens), "ctx", split_axis=0, concat_axis=0, tiled=True
    )

    tap_local = jnp.transpose(filters.reshape(local_filters, lags, tokens), (1, 0, 2)).astype(jnp.bfloat16)
    tap_other = lax.ppermute(tap_local, "dp", [(0, 1), (1, 0)])
    tap_all = jnp.where(
        group == 0,
        jnp.concatenate([tap_local, tap_other]),
        jnp.concatenate([tap_other, tap_local]),
    )
    first = lax.ppermute(tap_all, "ctx", [(i, i // 2 + (i % 2) * half_blocks) for i in range(blocks)])
    second = lax.ppermute(tap_all, "ctx", [(i, i // 2 + (1 - i % 2) * half_blocks) for i in range(blocks)])
    filt = transform_taps(first, second, half_blocks, 2 * tokens, tables[0])

    even, odd = gate(False, arrays, repeats, half_blocks)
    shape = (half_blocks // 2, repeats * owned, tokens)
    own = exchange_own(even.reshape(shape), odd.reshape(shape), half_blocks)

    result = convolve(near, own, filt, half_blocks, tables)
    sides = [list(range(half_blocks)), list(range(half_blocks, blocks))]
    returned = lax.all_to_all(
        result, "ctx", split_axis=0, concat_axis=0, tiled=True, axis_index_groups=sides
    )

    keep, give = correlate(near, own, owned, half_blocks, tables)
    taken = lax.ppermute(give, "ctx", [(i, (i + half_blocks) % blocks) for i in range(blocks)])
    low = keep[:half_blocks] + taken.astype(jnp.float32)
    high = keep[half_blocks:]
    mine = jnp.where(group == 0, low, high).astype(jnp.bfloat16)
    theirs = jnp.where(group == 0, high, low).astype(jnp.bfloat16)
    home = [(i, 2 * (i % half_blocks) + i // half_blocks) for i in range(blocks)]
    mine = lax.ppermute(mine, "ctx", home)
    theirs = lax.ppermute(
        theirs, ("dp", "ctx"), [(g * blocks + i, (1 - g) * blocks + j) for g in range(groups) for i, j in home]
    )
    summed = mine.astype(jnp.float32) + theirs.astype(jnp.float32)
    filter_grad = jnp.transpose(summed, (1, 0, 2)).reshape(local_filters, lags * tokens)

    returned = returned.reshape(half_blocks, 2, repeats, owned, tokens)
    mixed, pre_grad, value_grad, post_grad = finish(returned, pre_gate, values, post_gate, cotangent)
    return (mixed, pre_grad, value_grad, post_grad, filter_grad)


def matmul(left, right):
    return jnp.dot(left, right, precision=lax.Precision.HIGHEST, preferred_element_type=jnp.float32)


def contract(form, left, right):
    return jnp.einsum(
        form, left, right, precision=lax.Precision.HIGHEST, preferred_element_type=jnp.float32
    )


def phases(height, width, modulus):
    product = lax.broadcasted_iota(jnp.int32, (height, width), 0) * lax.broadcasted_iota(
        jnp.int32, (height, width), 1
    )
    return (product % modulus).astype(jnp.float32) * (2.0 * math.pi / modulus)


def build_tables(blocks, tokens):
    factor = 1
    for candidate in range(1, tokens + 1):
        if tokens % candidate == 0 and candidate * candidate <= tokens:
            factor = candidate
    second = tokens // factor
    rows = blocks + 1
    total = 2 * blocks * tokens
    first_angle = phases(rows, blocks, 2 * blocks)
    twist_angle = phases(rows, tokens, total)
    inner_angle = phases(factor, factor, factor)
    middle_angle = phases(factor, second, tokens)
    outer_angle = phases(second, second, second)
    back_angle = phases(blocks, rows, 2 * blocks)
    column = lax.broadcasted_iota(jnp.int32, (blocks, rows), 1)
    weight = jnp.where((column == 0) | (column == blocks), 1.0, 2.0).astype(jnp.float32) / total
    return {
        "first_cos": jnp.cos(first_angle),
        "first_nsin": -jnp.sin(first_angle),
        "twist_cos": jnp.cos(twist_angle),
        "twist_sin": jnp.sin(twist_angle),
        "inner_cos": jnp.cos(inner_angle),
        "inner_sin": jnp.sin(inner_angle),
        "middle_cos": jnp.cos(middle_angle),
        "middle_sin": jnp.sin(middle_angle),
        "outer_cos": jnp.cos(outer_angle),
        "outer_sin": jnp.sin(outer_angle),
        "back_cos": weight * jnp.cos(back_angle),
        "back_sin": weight * jnp.sin(back_angle),
    }


def expand(table, ndim):
    return table.reshape((table.shape[0],) + (1,) * (ndim - 2) + (table.shape[1],))


def block_table(cos_part, sin_part):
    return jnp.stack([jnp.stack([cos_part, sin_part]), jnp.stack([-sin_part, cos_part])])


def wave(real_part, imag_part, tables, sign):
    shape = real_part.shape
    factor = tables["inner_cos"].shape[0]
    second = tables["outer_cos"].shape[0]
    stacked = jnp.stack(
        [real_part.reshape(-1, factor, second), imag_part.reshape(-1, factor, second)]
    )
    inner_table = block_table(tables["inner_cos"], sign * tables["inner_sin"])
    middle = contract("prab,pqac->qrcb", stacked, inner_table)
    middle_cos = tables["middle_cos"]
    middle_sin = sign * tables["middle_sin"]
    real_turn = middle[0] * middle_cos - middle[1] * middle_sin
    imag_turn = middle[0] * middle_sin + middle[1] * middle_cos
    turned = jnp.stack([real_turn, imag_turn])
    outer_table = block_table(tables["outer_cos"], sign * tables["outer_sin"])
    result = contract("prcb,pqbd->qrdc", turned, outer_table)
    return (result[0].reshape(shape), result[1].reshape(shape))


def finish_forward(real_first, imag_first, tables):
    ndim = real_first.ndim
    twist_cos = expand(tables["twist_cos"], ndim)
    twist_sin = expand(tables["twist_sin"], ndim)
    real_twist = real_first * twist_cos + imag_first * twist_sin
    imag_twist = imag_first * twist_cos - real_first * twist_sin
    return wave(real_twist, imag_twist, tables, -1.0)


def spectrum(signal, tables):
    flat = signal.reshape(signal.shape[0], -1)
    shape = (tables["first_cos"].shape[0],) + signal.shape[1:]
    real_first = matmul(tables["first_cos"], flat).reshape(shape)
    imag_first = matmul(tables["first_nsin"], flat).reshape(shape)
    return finish_forward(real_first, imag_first, tables)


def inverse_prepare(real_spec, imag_spec, tables):
    ndim = real_spec.ndim
    real_wave, imag_wave = wave(real_spec, imag_spec, tables, 1.0)
    twist_cos = expand(tables["twist_cos"], ndim)
    twist_sin = expand(tables["twist_sin"], ndim)
    real_twist = real_wave * twist_cos - imag_wave * twist_sin
    imag_twist = real_wave * twist_sin + imag_wave * twist_cos
    rows = real_spec.shape[0]
    return (real_twist.reshape(rows, -1), imag_twist.reshape(rows, -1))


def inverse_full(real_spec, imag_spec, tables):
    real_flat, imag_flat = inverse_prepare(real_spec, imag_spec, tables)
    signal = matmul(tables["back_cos"], real_flat) - matmul(tables["back_sin"], imag_flat)
    return signal.reshape((tables["back_cos"].shape[0],) + real_spec.shape[1:])


def plain_body(pre_gate, values, post_gate, filters, cotangent):
    blocks = lax.axis_size("ctx")
    groups = lax.axis_size("dp")
    local_rows = pre_gate.shape[0]
    tokens = pre_gate.shape[1]
    local_filters = filters.shape[0]
    repeats = local_rows // (local_filters * blocks)
    share = blocks // groups
    tables = build_tables(blocks, tokens)
    gated = (pre_gate.astype(jnp.float32) * values.astype(jnp.float32)).astype(jnp.bfloat16)
    conv_grad = (cotangent.astype(jnp.float32) * post_gate.astype(jnp.float32)).astype(jnp.bfloat16)
    gated_blocks = gated.reshape(repeats, blocks, local_filters, tokens)
    grad_blocks = conv_grad.reshape(repeats, blocks, local_filters, tokens)
    tap_local = jnp.transpose(filters.reshape(local_filters, share, tokens), (1, 0, 2))
    piece = lax.all_gather(tap_local, "dp", axis=0, tiled=True)
    count = piece.shape[0]
    flat = piece.reshape(count, -1)
    cos_cols = tables["first_cos"]
    sin_cols = tables["first_nsin"]
    real_first = matmul(cos_cols, flat)
    imag_first = matmul(sin_cols, flat)
    spec_shape = (blocks + 1, 1, local_filters, tokens)
    filt_real, filt_imag = finish_forward(
        real_first.reshape(spec_shape), imag_first.reshape(spec_shape), tables
    )

    def single_spectrum(received):
        signal = received.reshape(blocks, -1, received.shape[2], received.shape[3])
        return spectrum(signal.astype(jnp.float32), tables)

    gated_real, gated_imag = single_spectrum(
        lax.all_to_all(gated_blocks, "ctx", split_axis=1, concat_axis=0, tiled=True)
    )
    prod_real = gated_real * filt_real - gated_imag * filt_imag
    prod_imag = gated_real * filt_imag + gated_imag * filt_real
    result = inverse_full(prod_real, prod_imag, tables).astype(jnp.bfloat16)
    conv_chan = result.reshape(blocks * repeats, 1, local_filters, tokens)
    conv_seq = lax.all_to_all(conv_chan, "ctx", split_axis=0, concat_axis=1, tiled=True)
    grad_real, grad_imag = single_spectrum(
        lax.all_to_all(grad_blocks, "ctx", split_axis=1, concat_axis=0, tiled=True)
    )
    prod_real = filt_real * grad_real + filt_imag * grad_imag
    prod_imag = filt_real * grad_imag - filt_imag * grad_real
    result = inverse_full(prod_real, prod_imag, tables).astype(jnp.bfloat16)
    gated_chan_grad = result.reshape(blocks * repeats, 1, local_filters, tokens)
    gated_seq_grad = lax.all_to_all(gated_chan_grad, "ctx", split_axis=0, concat_axis=1, tiled=True)
    cross_real = jnp.sum(gated_real * grad_real + gated_imag * grad_imag, axis=1)
    cross_imag = jnp.sum(gated_real * grad_imag - gated_imag * grad_real, axis=1)
    wave_real, wave_imag = inverse_prepare(cross_real, cross_imag, tables)
    cos_rows = tables["back_cos"]
    sin_rows = tables["back_sin"]
    term = matmul(cos_rows, wave_real) - matmul(sin_rows, wave_imag)
    summed = lax.psum_scatter(
        term.reshape(lax.axis_size("dp") * share, local_filters, tokens).astype(jnp.bfloat16),
        "dp",
        scatter_dimension=0,
        tiled=True,
    ).astype(jnp.float32)
    filter_grad = jnp.transpose(summed, (1, 0, 2)).reshape(local_filters, share * tokens)
    conv_full = conv_seq.reshape(pre_gate.shape).astype(jnp.float32)
    gated_grad = gated_seq_grad.reshape(pre_gate.shape).astype(jnp.float32)
    mixed = (post_gate.astype(jnp.float32) * conv_full).astype(jnp.bfloat16)
    post_grad = (cotangent.astype(jnp.float32) * conv_full).astype(jnp.bfloat16)
    pre_grad = (gated_grad * values.astype(jnp.float32)).astype(jnp.bfloat16)
    value_grad = (gated_grad * pre_gate.astype(jnp.float32)).astype(jnp.bfloat16)
    return (mixed, pre_grad, value_grad, post_grad, filter_grad)


def solution(mesh):
    placed = (P("dp", "ctx"), P("dp", "ctx"), P("dp", "ctx"), P("ctx", "dp"), P("dp", "ctx"))
    groups, blocks = mesh.shape["dp"], mesh.shape["ctx"]

    def program(pre_gate, values, post_gate, filters, cotangent):
        kernels = groups == 2 and blocks >= 8 and blocks & (blocks - 1) == 0 and filters.shape[0] % 16 == 0
        return (body if kernels else plain_body)(pre_gate, values, post_gate, filters, cotangent)

    return jax.shard_map(
        program,
        mesh=mesh,
        in_specs=placed,
        out_specs=(P("dp", "ctx"), P("dp", "ctx"), P("dp", "ctx"), P("dp", "ctx"), P("ctx", "dp")),
        check_vma=False,
    )
```

```python
import math

import jax
import jax.numpy as jnp
import numpy as np
from jax import lax
from jax.experimental import pallas as pl
from jax.experimental.pallas import tpu as pltpu
from jax.sharding import PartitionSpec as P


LANES = 128
SUBLANES = 8
MEBI = 1024 * 1024


def dft_tables(size):
    angle = np.arange(size)[:, None] * (2.0 * np.arange(size)[None, :] + 1.0) * (math.pi / (2 * size))
    strips = size // LANES
    cos, sin = (part.reshape(size, strips, 1, LANES) for part in (np.cos(angle), np.sin(angle)))
    table = np.concatenate([cos, -sin], axis=2).reshape(size, 2 * size)
    return jnp.asarray(table, jnp.bfloat16), jnp.asarray(table.T / size, jnp.bfloat16)


def dot(left, right):
    return jnp.dot(left, right, preferred_element_type=jnp.float32)


def alternating():
    odd = lax.broadcasted_iota(jnp.int32, (SUBLANES, LANES), 1) % 2
    return 1.0 - 2.0 * odd.astype(jnp.float32)


def place(half_blocks):
    index = lax.axis_index("ctx")
    return index // half_blocks, lax.rem(index, half_blocks)


def real_of(strip):
    return pl.ds(2 * strip * LANES, LANES)


def imag_of(strip):
    return pl.ds((2 * strip + 1) * LANES, LANES)


def gate_kernel(near, half_blocks, pre_ref, value_ref, post_ref, cot_ref, *refs):
    out_refs, (left_ref, right_ref, result_ref, in_sems, out_sems) = refs[:-5], refs[-5:]
    repeats, rows, tokens = left_ref.shape
    share = rows // (2 * half_blocks)
    half, me = place(half_blocks)
    use_gated = half == 0 if near else half != 0

    def fetch(r, left, right):
        at = pl.ds(r * rows, rows)
        return (
            pltpu.make_async_copy(left.at[at], left_ref.at[r], in_sems.at[0, r]),
            pltpu.make_async_copy(right.at[at], right_ref.at[r], in_sems.at[1, r]),
        )

    @pl.when(use_gated)
    def _():
        for r in range(repeats):
            for copy in fetch(r, pre_ref, value_ref):
                copy.start()

    @pl.when(jnp.logical_not(use_gated))
    def _():
        for r in range(repeats):
            for copy in fetch(r, cot_ref, post_ref):
                copy.start()

    pending = []
    for r in range(repeats):
        for copy in fetch(r, pre_ref, value_ref):
            copy.wait()
        product = left_ref[r].astype(jnp.float32) * right_ref[r].astype(jnp.float32)
        product = product.astype(jnp.bfloat16).reshape(2, half_blocks, share, tokens)
        for side in range(2):
            if near:
                result_ref[r, :, side] = product[side]
            else:
                result_ref[:, r, side] = product[side]
        if near:
            for copy_at in range(2):
                copy = pltpu.make_async_copy(result_ref.at[r], out_refs[0].at[copy_at, :, r], out_sems.at[copy_at, r])
                copy.start()
                pending.append(copy)
    if not near:
        for slot in range(half_blocks):
            source = result_ref.at[jnp.bitwise_xor(me, slot)]
            copy = pltpu.make_async_copy(source, out_refs[slot], out_sems.at[slot])
            copy.start()
            pending.append(copy)
    for copy in pending:
        copy.wait()


def gate(near, arrays, repeats, half_blocks):
    rows_all, tokens = arrays[0].shape
    rows = rows_all // repeats
    share = rows // (2 * half_blocks)
    if near:
        shapes = [(2, half_blocks, repeats, 2, share, tokens)]
        held, sems = (repeats, half_blocks, 2, share, tokens), (2, repeats)
    else:
        shapes = [(repeats, 2, share, tokens)] * half_blocks
        held, sems = (half_blocks, repeats, 2, share, tokens), (half_blocks,)
    return pl.pallas_call(
        lambda *refs: gate_kernel(near, half_blocks, *refs),
        in_specs=[pl.BlockSpec(memory_space=pltpu.HBM)] * 4,
        out_specs=[pl.BlockSpec(memory_space=pltpu.HBM)] * len(shapes),
        out_shape=[jax.ShapeDtypeStruct(shape, jnp.bfloat16) for shape in shapes],
        scratch_shapes=[
            pltpu.VMEM((repeats, rows, tokens), jnp.bfloat16),
            pltpu.VMEM((repeats, rows, tokens), jnp.bfloat16),
            pltpu.VMEM(held, jnp.bfloat16),
            pltpu.SemaphoreType.DMA((2, repeats)),
            pltpu.SemaphoreType.DMA(sems),
        ],
        compiler_params=pltpu.CompilerParams(vmem_limit_bytes=6 * MEBI),
        cost_estimate=pl.CostEstimate(flops=rows_all * tokens, bytes_accessed=8 * rows_all * tokens, transcendentals=0),
        name="gate_near" if near else "gate_own",
    )(*arrays)


def finish_kernel(half_blocks, recv_ref, pre_ref, value_ref, post_ref, cot_ref, *refs):
    out_refs, (held_ref, sems) = refs[:4], refs[4:]
    repeats, sides = recv_ref.shape[2:4]
    rows, tokens = held_ref.shape[2:]
    half, _ = place(half_blocks)
    pending = []
    for part in range(repeats * sides):
        r, side = part // sides, part % sides
        at = pl.ds(part * rows, rows)
        conv = recv_ref[:, half, r, side].reshape(rows, tokens).astype(jnp.float32)
        grad = recv_ref[:, 1 - half, r, side].reshape(rows, tokens).astype(jnp.float32)
        for which, (factor_ref, result) in enumerate(
            ((post_ref, conv), (value_ref, grad), (pre_ref, grad), (cot_ref, conv))
        ):
            held_ref[which, part] = (factor_ref[at].astype(jnp.float32) * result).astype(jnp.bfloat16)
            copy = pltpu.make_async_copy(held_ref.at[which, part], out_refs[which].at[at], sems.at[which, part])
            copy.start()
            pending.append(copy)
    for copy in pending:
        copy.wait()


def finish(received, pre_gate, values, post_gate, cotangent):
    half_blocks, _, repeats, sides, share, tokens = received.shape
    parts, rows = repeats * sides, half_blocks * share
    return pl.pallas_call(
        lambda *refs: finish_kernel(half_blocks, *refs),
        in_specs=[pl.BlockSpec(memory_space=pltpu.VMEM)] * 5,
        out_specs=[pl.BlockSpec(memory_space=pltpu.HBM)] * 4,
        out_shape=[jax.ShapeDtypeStruct(pre_gate.shape, jnp.bfloat16)] * 4,
        scratch_shapes=[
            pltpu.VMEM((4, parts, rows, tokens), jnp.bfloat16),
            pltpu.SemaphoreType.DMA((4, parts)),
        ],
        compiler_params=pltpu.CompilerParams(vmem_limit_bytes=8 * MEBI),
        name="finish",
    )(received, pre_gate, values, post_gate, cotangent)


def taps_kernel(half_blocks, groups, *refs):
    piece_refs, (forward_ref, out_ref, stage_ref) = refs[:-3], refs[-3:]
    count, rows, width = out_ref.shape
    size = width // 2
    share, lags = piece_refs[0].shape
    half, _ = place(half_blocks)
    group = lax.axis_index("dp")
    for at, ref in enumerate(piece_refs):
        side = half if at < 2 else 1 - half
        first = (group if at % 2 == 0 else 1 - group) * (lags // size)
        for k in range(lags // size):
            stage_ref[first + k, pl.ds(pl.multiple_of(side * share, share), share)] = ref[:, k * size : (k + 1) * size]
    spectrum = dot(stage_ref[...].reshape(count * rows, size), forward_ref[...]).reshape(count, rows, width)
    turn = jnp.where(half == 0, 1.0, -1.0).astype(jnp.float32)
    sign = alternating()[:1]
    for k in range(count):
        for strip in range(size // LANES):
            re = slice(2 * strip * LANES, (2 * strip + 1) * LANES)
            im = slice((2 * strip + 1) * LANES, (2 * strip + 2) * LANES)
            real, imag = spectrum[k, :, re], spectrum[k, :, im]
            if k > 0:
                real, imag = real - sign * spectrum[k - 1, :, im], imag + sign * spectrum[k - 1, :, re]
            out_ref[k, :, re] = real
            out_ref[k, :, im] = turn * imag


def transform_taps(pieces, half_blocks, groups, forward):
    share, lags = pieces[0].shape
    size = forward.shape[0]
    count = groups * lags // size
    return pl.pallas_call(
        lambda *refs: taps_kernel(half_blocks, groups, *refs),
        out_shape=jax.ShapeDtypeStruct((count, 2 * share, 2 * size), jnp.float32),
        scratch_shapes=[pltpu.VMEM((count, 2 * share, size), jnp.bfloat16)],
        compiler_params=pltpu.CompilerParams(vmem_limit_bytes=8 * MEBI),
        name="taps",
    )(*pieces, forward)


def add(total, term):
    return term if total is None else (total[0] + term[0], total[1] + term[1])


def times(a, b):
    return a[0] * b[0] - a[1] * b[1], a[0] * b[1] + a[1] * b[0]


def conj_times(a, b):
    return a[0] * b[0] + a[1] * b[1], a[0] * b[1] - a[1] * b[0]


def transform(stage_ref, forward_ref, spec_ref):
    width = spec_ref.shape[-1]
    staged = stage_ref[...].reshape(-1, stage_ref.shape[-1])
    for strip in range(width // (2 * LANES)):
        columns = slice(2 * strip * LANES, 2 * (strip + 1) * LANES)
        result = dot(staged, forward_ref[:, columns])
        spec_ref[:, :, :, columns] = result.reshape(spec_ref.shape[:-1] + (2 * LANES,))


def convolve_kernel(half_blocks, near_ref, *refs):
    own_refs = refs[:half_blocks]
    filt_ref, forward_ref, inverse_ref, out_ref, stage_ref, spec_ref, prod_ref, held_ref, sems = refs[half_blocks:]
    _, count, rows, width = spec_ref.shape
    size = width // 2
    tokens = near_ref.shape[2]
    merge = size // tokens
    filters = filt_ref.shape[1]
    half, _ = place(half_blocks)
    fill_stage(half_blocks, merge, near_ref, own_refs, stage_ref)
    transform(stage_ref, forward_ref, spec_ref)

    @pl.loop(0, rows // SUBLANES)
    def _(tile):
        row = pl.ds(pl.multiple_of(tile * SUBLANES, SUBLANES), SUBLANES)
        tap_row = pl.ds(pl.multiple_of(lax.rem(tile * SUBLANES, filters), SUBLANES), SUBLANES)
        for strip in range(size // LANES):
            def spectrum(which, k):
                return spec_ref[which, k, row, real_of(strip)], spec_ref[which, k, row, imag_of(strip)]

            taps = [
                (filt_ref[k, tap_row, real_of(strip)], filt_ref[k, tap_row, imag_of(strip)]) for k in range(2 * count)
            ]
            near = [spectrum(0, k) for k in range(count)]
            for out in range(count):
                total = None
                for k in range(out + 1):
                    total = add(total, times(taps[out - k], near[k]))
                prod_ref[0, out, row, real_of(strip)], prod_ref[0, out, row, imag_of(strip)] = total
            own = [spectrum(1, k) for k in range(count)]
            far = [spectrum(2, k) for k in range(count)]
            for out in range(count):
                total = None
                for k in range(out + 1):
                    total = add(total, conj_times(taps[out - k], own[k]))
                for k in range(count):
                    total = add(total, conj_times(taps[count + out - k], far[k]))
                prod_ref[1, out, row, real_of(strip)], prod_ref[1, out, row, imag_of(strip)] = total

    pending = []
    for which in range(2):
        result = dot(prod_ref[which].astype(jnp.bfloat16).reshape(count * rows, width), inverse_ref[...])
        result = result.astype(jnp.bfloat16).reshape(count, rows, size)
        for k in range(count):
            flipped = count - 1 - k
            block = jnp.where(half == which, k, flipped)
            for q in range(merge):
                held_ref[which, k, q] = result[k, :, q * tokens : (q + 1) * tokens]
                copy = pltpu.make_async_copy(
                    held_ref.at[which, k, q], out_ref.at[block * merge + q, which], sems.at[which, k, q]
                )
                copy.start()
                pending.append(copy)
    for copy in pending:
        copy.wait()


def fill_stage(half_blocks, merge, near_ref, own_refs, stage_ref):
    count = half_blocks // merge
    tokens = near_ref.shape[2]
    half, me = place(half_blocks)
    for k in range(count):
        flipped = count - 1 - k
        outer = jnp.where(half == 0, k, flipped)
        inner = jnp.where(half == 0, flipped, k)
        for q in range(merge):
            lanes = pl.ds(q * tokens, tokens)
            stage_ref[0, k, :, lanes] = near_ref[half * half_blocks + outer * merge + q]
            stage_ref[2, k, :, lanes] = near_ref[(1 - half) * half_blocks + inner * merge + q]
    for slot, ref in enumerate(own_refs):
        position = jnp.bitwise_xor(me, slot)
        block = position // merge
        k = jnp.where(half == 0, count - 1 - block, block)
        start = pl.multiple_of(lax.rem(position, merge) * tokens, tokens)
        stage_ref[1, k, :, pl.ds(start, tokens)] = ref[...]


def convolve(near, own, filt, half_blocks, tables):
    forward, inverse = tables
    _, rows, tokens = near.shape
    size = forward.shape[0]
    merge = size // tokens
    count = half_blocks // merge
    pairs = count * (2 * count + 1)
    return pl.pallas_call(
        lambda *refs: convolve_kernel(half_blocks, *refs),
        out_specs=pl.BlockSpec(memory_space=pltpu.HBM),
        out_shape=jax.ShapeDtypeStruct((half_blocks, 2, rows, tokens), jnp.bfloat16),
        scratch_shapes=[
            pltpu.VMEM((3, count, rows, size), jnp.bfloat16),
            pltpu.VMEM((3, count, rows, 2 * size), jnp.float32),
            pltpu.VMEM((2, count, rows, 2 * size), jnp.float32),
            pltpu.VMEM((2, count, merge, rows, tokens), jnp.bfloat16),
            pltpu.SemaphoreType.DMA((2, count, merge)),
        ],
        compiler_params=pltpu.CompilerParams(vmem_limit_bytes=28 * MEBI),
        cost_estimate=pl.CostEstimate(
            flops=20 * count * rows * size * size + 8 * pairs * rows * size,
            bytes_accessed=10 * count * rows * size,
            transcendentals=0,
        ),
        name="convolve",
    )(near, *own, filt, forward, inverse)


def correlate_kernel(half_blocks, near_ref, *refs):
    own_refs = refs[:half_blocks]
    forward_ref, inverse_ref, mine_ref, theirs_ref, give_ref = refs[half_blocks : half_blocks + 5]
    stage_ref, spec_ref, local_ref, cross_ref, joint_ref, held_ref = refs[half_blocks + 5 :]
    _, count, rows, width = spec_ref.shape
    size = width // 2
    tokens = near_ref.shape[2]
    merge = size // tokens
    filters = local_ref.shape[1]
    repeats = rows // filters
    kept = filters // 2
    half, _ = place(half_blocks)
    turn = jnp.where(half == 0, 1.0, -1.0).astype(jnp.float32)
    fill_stage(half_blocks, merge, near_ref, own_refs, stage_ref)
    transform(stage_ref, forward_ref, spec_ref)

    def products(other, row_at, strip, lags):
        totals = [None] * len(lags)
        for repeat in range(repeats):
            row = pl.ds(pl.multiple_of(repeat * filters + row_at, SUBLANES), SUBLANES)

            def spectrum(which, k):
                return spec_ref[which, k, row, real_of(strip)], spec_ref[which, k, row, imag_of(strip)]

            near = [spectrum(0, k) for k in range(count)]
            far = [spectrum(other, k) for k in range(count)]
            for at, total in enumerate(lags):
                for a in range(count):
                    if 0 <= total - a < count:
                        totals[at] = add(totals[at], conj_times(near[a], far[total - a]))
        return totals

    @pl.loop(0, filters // SUBLANES)
    def _(tile):
        row = pl.multiple_of(tile * SUBLANES, SUBLANES)
        for strip in range(size // LANES):
            totals = products(1, row, strip, [count - 1 - k for k in range(count)])
            for k in range(count):
                local_ref[k, pl.ds(row, SUBLANES), real_of(strip)] = totals[k][0]
                local_ref[k, pl.ds(row, SUBLANES), imag_of(strip)] = turn * totals[k][1]

    @pl.loop(0, kept // SUBLANES)
    def _(tile):
        to = pl.multiple_of(tile * SUBLANES, SUBLANES)
        row = pl.multiple_of(half * kept + tile * SUBLANES, SUBLANES)
        for strip in range(size // LANES):
            totals = products(2, row, strip, [2 * count - 1 - k for k in range(1, 2 * count)])
            for k in range(1, 2 * count):
                real, imag = totals[k - 1]
                imag = turn * imag
                if k < count:
                    real = real + local_ref[k, pl.ds(row, SUBLANES), real_of(strip)]
                    imag = imag + local_ref[k, pl.ds(row, SUBLANES), imag_of(strip)]
                cross_ref[k, pl.ds(to, SUBLANES), real_of(strip)] = real
                cross_ref[k, pl.ds(to, SUBLANES), imag_of(strip)] = imag
            cross_ref[0, pl.ds(to, SUBLANES), real_of(strip)] = local_ref[0, pl.ds(row, SUBLANES), real_of(strip)]
            cross_ref[0, pl.ds(to, SUBLANES), imag_of(strip)] = local_ref[0, pl.ds(row, SUBLANES), imag_of(strip)]

    sign = alternating()[:1]
    other = pl.ds(pl.multiple_of((1 - half) * kept, SUBLANES), kept)

    def join(ref, row, lags, base):
        for k in range(lags):
            for strip in range(size // LANES):
                real, imag = ref[k, row, real_of(strip)], ref[k, row, imag_of(strip)]
                if k + 1 < lags:
                    real, imag = (
                        real + sign * ref[k + 1, row, imag_of(strip)],
                        imag - sign * ref[k + 1, row, real_of(strip)],
                    )
                joint_ref[base + k, :, real_of(strip)] = real.astype(jnp.bfloat16)
                joint_ref[base + k, :, imag_of(strip)] = imag.astype(jnp.bfloat16)

    join(cross_ref, pl.ds(0, kept), 2 * count, 0)
    join(local_ref, other, count, 2 * count)
    result = dot(joint_ref[...].reshape(3 * count * kept, width), inverse_ref[...]).reshape(3 * count, kept, size)
    held_ref[...] = result[: 2 * count].reshape(2, count, kept, size)
    group = lax.axis_index("dp")
    for k in range(count):
        columns = slice(k * size, (k + 1) * size)
        mine_ref[:, columns] = held_ref[group, k]
        theirs_ref[:, columns] = held_ref[1 - group, k].astype(jnp.bfloat16)
        give_ref[:, columns] = result[2 * count + k].astype(jnp.bfloat16)


def correlate(near, own, filters, half_blocks, tables):
    forward, inverse = tables
    _, rows, tokens = near.shape
    size = forward.shape[0]
    count = half_blocks * tokens // size
    pairs = count * (2 * count + 1)
    kept = filters // 2
    return pl.pallas_call(
        lambda *refs: correlate_kernel(half_blocks, *refs),
        out_shape=[
            jax.ShapeDtypeStruct((kept, count * size), jnp.float32),
            jax.ShapeDtypeStruct((kept, count * size), jnp.bfloat16),
            jax.ShapeDtypeStruct((kept, count * size), jnp.bfloat16),
        ],
        scratch_shapes=[
            pltpu.VMEM((3, count, rows, size), jnp.bfloat16),
            pltpu.VMEM((3, count, rows, 2 * size), jnp.float32),
            pltpu.VMEM((count, filters, 2 * size), jnp.float32),
            pltpu.VMEM((2 * count, kept, 2 * size), jnp.float32),
            pltpu.VMEM((3 * count, kept, 2 * size), jnp.bfloat16),
            pltpu.VMEM((2, count, kept, size), jnp.float32),
        ],
        compiler_params=pltpu.CompilerParams(vmem_limit_bytes=28 * MEBI),
        cost_estimate=pl.CostEstimate(
            flops=14 * count * rows * size * size + 4 * pairs * rows * size,
            bytes_accessed=8 * count * rows * size,
            transcendentals=0,
        ),
        name="correlate",
    )(near, *own, forward, inverse)


def body(pre_gate, values, post_gate, filters, cotangent):
    blocks = lax.axis_size("ctx")
    groups = lax.axis_size("dp")
    half_blocks = blocks // 2
    local_rows, tokens = pre_gate.shape
    local_filters = filters.shape[0]
    repeats = local_rows // (local_filters * blocks)
    owned = 2 * local_filters
    tables = dft_tables(2 * tokens)
    arrays = (pre_gate, values, post_gate, cotangent)

    def swap(array, bit):
        return array if bit == 0 else lax.ppermute(array, "ctx", [(i, i ^ bit) for i in range(blocks)])

    (near,) = gate(True, arrays, repeats, half_blocks)
    near = lax.all_to_all(
        near.reshape(blocks, repeats * owned, tokens), "ctx", split_axis=0, concat_axis=0, tiled=True
    )

    taps = filters.astype(jnp.bfloat16)
    across = [(i, blocks + (i ^ half_blocks)) for i in range(blocks)]
    across = across + [(b, a) for a, b in across]
    pieces = (
        taps,
        lax.ppermute(taps, "dp", [(0, 1), (1, 0)]),
        swap(taps, half_blocks),
        lax.ppermute(taps, ("dp", "ctx"), across),
    )
    filt = transform_taps(pieces, half_blocks, groups, tables[0])

    own = gate(False, arrays, repeats, half_blocks)
    own = [swap(piece.reshape(repeats * owned, tokens), slot) for slot, piece in enumerate(own)]

    result = convolve(near, own, filt, half_blocks, tables)
    sides = [list(range(half_blocks)), list(range(half_blocks, blocks))]
    returned = lax.all_to_all(
        result, "ctx", split_axis=0, concat_axis=0, tiled=True, axis_index_groups=sides
    )

    mine, theirs, give = correlate(near, own, owned, half_blocks, tables)
    terms = (
        lax.ppermute(theirs, "dp", [(0, 1), (1, 0)]),
        lax.ppermute(give, ("dp", "ctx"), [(i, i ^ half_blocks) for i in range(blocks)]),
        lax.ppermute(give, ("dp", "ctx"), [(blocks + i, i ^ half_blocks) for i in range(blocks)]),
    )
    filter_grad = mine
    for term in terms:
        filter_grad = filter_grad + term.astype(jnp.float32)

    returned = returned.reshape(half_blocks, 2, repeats, 2, local_filters, tokens)
    mixed, pre_grad, value_grad, post_grad = finish(returned, pre_gate, values, post_gate, cotangent)
    return (mixed, pre_grad, value_grad, post_grad, filter_grad)


def matmul(left, right):
    return jnp.dot(left, right, precision=lax.Precision.HIGHEST, preferred_element_type=jnp.float32)


def contract(form, left, right):
    return jnp.einsum(
        form, left, right, precision=lax.Precision.HIGHEST, preferred_element_type=jnp.float32
    )


def phases(height, width, modulus):
    product = lax.broadcasted_iota(jnp.int32, (height, width), 0) * lax.broadcasted_iota(
        jnp.int32, (height, width), 1
    )
    return (product % modulus).astype(jnp.float32) * (2.0 * math.pi / modulus)


def build_tables(blocks, tokens):
    factor = 1
    for candidate in range(1, tokens + 1):
        if tokens % candidate == 0 and candidate * candidate <= tokens:
            factor = candidate
    second = tokens // factor
    rows = blocks + 1
    total = 2 * blocks * tokens
    first_angle = phases(rows, blocks, 2 * blocks)
    twist_angle = phases(rows, tokens, total)
    inner_angle = phases(factor, factor, factor)
    middle_angle = phases(factor, second, tokens)
    outer_angle = phases(second, second, second)
    back_angle = phases(blocks, rows, 2 * blocks)
    column = lax.broadcasted_iota(jnp.int32, (blocks, rows), 1)
    weight = jnp.where((column == 0) | (column == blocks), 1.0, 2.0).astype(jnp.float32) / total
    return {
        "first_cos": jnp.cos(first_angle),
        "first_nsin": -jnp.sin(first_angle),
        "twist_cos": jnp.cos(twist_angle),
        "twist_sin": jnp.sin(twist_angle),
        "inner_cos": jnp.cos(inner_angle),
        "inner_sin": jnp.sin(inner_angle),
        "middle_cos": jnp.cos(middle_angle),
        "middle_sin": jnp.sin(middle_angle),
        "outer_cos": jnp.cos(outer_angle),
        "outer_sin": jnp.sin(outer_angle),
        "back_cos": weight * jnp.cos(back_angle),
        "back_sin": weight * jnp.sin(back_angle),
    }


def expand(table, ndim):
    return table.reshape((table.shape[0],) + (1,) * (ndim - 2) + (table.shape[1],))


def block_table(cos_part, sin_part):
    return jnp.stack([jnp.stack([cos_part, sin_part]), jnp.stack([-sin_part, cos_part])])


def wave(real_part, imag_part, tables, sign):
    shape = real_part.shape
    factor = tables["inner_cos"].shape[0]
    second = tables["outer_cos"].shape[0]
    stacked = jnp.stack(
        [real_part.reshape(-1, factor, second), imag_part.reshape(-1, factor, second)]
    )
    inner_table = block_table(tables["inner_cos"], sign * tables["inner_sin"])
    middle = contract("prab,pqac->qrcb", stacked, inner_table)
    middle_cos = tables["middle_cos"]
    middle_sin = sign * tables["middle_sin"]
    real_turn = middle[0] * middle_cos - middle[1] * middle_sin
    imag_turn = middle[0] * middle_sin + middle[1] * middle_cos
    turned = jnp.stack([real_turn, imag_turn])
    outer_table = block_table(tables["outer_cos"], sign * tables["outer_sin"])
    result = contract("prcb,pqbd->qrdc", turned, outer_table)
    return (result[0].reshape(shape), result[1].reshape(shape))


def finish_forward(real_first, imag_first, tables):
    ndim = real_first.ndim
    twist_cos = expand(tables["twist_cos"], ndim)
    twist_sin = expand(tables["twist_sin"], ndim)
    real_twist = real_first * twist_cos + imag_first * twist_sin
    imag_twist = imag_first * twist_cos - real_first * twist_sin
    return wave(real_twist, imag_twist, tables, -1.0)


def spectrum(signal, tables):
    flat = signal.reshape(signal.shape[0], -1)
    shape = (tables["first_cos"].shape[0],) + signal.shape[1:]
    real_first = matmul(tables["first_cos"], flat).reshape(shape)
    imag_first = matmul(tables["first_nsin"], flat).reshape(shape)
    return finish_forward(real_first, imag_first, tables)


def inverse_prepare(real_spec, imag_spec, tables):
    ndim = real_spec.ndim
    real_wave, imag_wave = wave(real_spec, imag_spec, tables, 1.0)
    twist_cos = expand(tables["twist_cos"], ndim)
    twist_sin = expand(tables["twist_sin"], ndim)
    real_twist = real_wave * twist_cos - imag_wave * twist_sin
    imag_twist = real_wave * twist_sin + imag_wave * twist_cos
    rows = real_spec.shape[0]
    return (real_twist.reshape(rows, -1), imag_twist.reshape(rows, -1))


def inverse_full(real_spec, imag_spec, tables):
    real_flat, imag_flat = inverse_prepare(real_spec, imag_spec, tables)
    signal = matmul(tables["back_cos"], real_flat) - matmul(tables["back_sin"], imag_flat)
    return signal.reshape((tables["back_cos"].shape[0],) + real_spec.shape[1:])


def plain_body(pre_gate, values, post_gate, filters, cotangent):
    blocks = lax.axis_size("ctx")
    groups = lax.axis_size("dp")
    local_rows = pre_gate.shape[0]
    tokens = pre_gate.shape[1]
    local_filters = filters.shape[0]
    repeats = local_rows // (local_filters * blocks)
    share = blocks // groups
    tables = build_tables(blocks, tokens)
    gated = (pre_gate.astype(jnp.float32) * values.astype(jnp.float32)).astype(jnp.bfloat16)
    conv_grad = (cotangent.astype(jnp.float32) * post_gate.astype(jnp.float32)).astype(jnp.bfloat16)
    gated_blocks = gated.reshape(repeats, blocks, local_filters, tokens)
    grad_blocks = conv_grad.reshape(repeats, blocks, local_filters, tokens)
    tap_local = jnp.transpose(filters.reshape(local_filters, share, tokens), (1, 0, 2))
    piece = lax.all_gather(tap_local, "dp", axis=0, tiled=True)
    count = piece.shape[0]
    flat = piece.reshape(count, -1)
    cos_cols = tables["first_cos"]
    sin_cols = tables["first_nsin"]
    real_first = matmul(cos_cols, flat)
    imag_first = matmul(sin_cols, flat)
    spec_shape = (blocks + 1, 1, local_filters, tokens)
    filt_real, filt_imag = finish_forward(
        real_first.reshape(spec_shape), imag_first.reshape(spec_shape), tables
    )

    def single_spectrum(received):
        signal = received.reshape(blocks, -1, received.shape[2], received.shape[3])
        return spectrum(signal.astype(jnp.float32), tables)

    gated_real, gated_imag = single_spectrum(
        lax.all_to_all(gated_blocks, "ctx", split_axis=1, concat_axis=0, tiled=True)
    )
    prod_real = gated_real * filt_real - gated_imag * filt_imag
    prod_imag = gated_real * filt_imag + gated_imag * filt_real
    result = inverse_full(prod_real, prod_imag, tables).astype(jnp.bfloat16)
    conv_chan = result.reshape(blocks * repeats, 1, local_filters, tokens)
    conv_seq = lax.all_to_all(conv_chan, "ctx", split_axis=0, concat_axis=1, tiled=True)
    grad_real, grad_imag = single_spectrum(
        lax.all_to_all(grad_blocks, "ctx", split_axis=1, concat_axis=0, tiled=True)
    )
    prod_real = filt_real * grad_real + filt_imag * grad_imag
    prod_imag = filt_real * grad_imag - filt_imag * grad_real
    result = inverse_full(prod_real, prod_imag, tables).astype(jnp.bfloat16)
    gated_chan_grad = result.reshape(blocks * repeats, 1, local_filters, tokens)
    gated_seq_grad = lax.all_to_all(gated_chan_grad, "ctx", split_axis=0, concat_axis=1, tiled=True)
    cross_real = jnp.sum(gated_real * grad_real + gated_imag * grad_imag, axis=1)
    cross_imag = jnp.sum(gated_real * grad_imag - gated_imag * grad_real, axis=1)
    wave_real, wave_imag = inverse_prepare(cross_real, cross_imag, tables)
    cos_rows = tables["back_cos"]
    sin_rows = tables["back_sin"]
    term = matmul(cos_rows, wave_real) - matmul(sin_rows, wave_imag)
    summed = lax.psum_scatter(
        term.reshape(lax.axis_size("dp") * share, local_filters, tokens).astype(jnp.bfloat16),
        "dp",
        scatter_dimension=0,
        tiled=True,
    ).astype(jnp.float32)
    filter_grad = jnp.transpose(summed, (1, 0, 2)).reshape(local_filters, share * tokens)
    conv_full = conv_seq.reshape(pre_gate.shape).astype(jnp.float32)
    gated_grad = gated_seq_grad.reshape(pre_gate.shape).astype(jnp.float32)
    mixed = (post_gate.astype(jnp.float32) * conv_full).astype(jnp.bfloat16)
    post_grad = (cotangent.astype(jnp.float32) * conv_full).astype(jnp.bfloat16)
    pre_grad = (gated_grad * values.astype(jnp.float32)).astype(jnp.bfloat16)
    value_grad = (gated_grad * pre_gate.astype(jnp.float32)).astype(jnp.bfloat16)
    return (mixed, pre_grad, value_grad, post_grad, filter_grad)


def solution(mesh):
    placed = (P("dp", "ctx"), P("dp", "ctx"), P("dp", "ctx"), P("ctx", "dp"), P("dp", "ctx"))
    groups, blocks = mesh.shape["dp"], mesh.shape["ctx"]

    def program(pre_gate, values, post_gate, filters, cotangent):
        kernels = groups == 2 and blocks >= 8 and blocks & (blocks - 1) == 0 and filters.shape[0] % 16 == 0
        return (body if kernels else plain_body)(pre_gate, values, post_gate, filters, cotangent)

    return jax.shard_map(
        program,
        mesh=mesh,
        in_specs=placed,
        out_specs=(P("dp", "ctx"), P("dp", "ctx"), P("dp", "ctx"), P("dp", "ctx"), P("ctx", "dp")),
        check_vma=False,
    )
```

```python
import math

import jax
import jax.numpy as jnp
import numpy as np
from jax import lax
from jax.experimental import pallas as pl
from jax.experimental.pallas import tpu as pltpu
from jax.sharding import PartitionSpec as P


LANES = 128
SUBLANES = 8
VMEM_BYTES = 60 * 1024 * 1024
HEAVY = 1 << 37


def dft_tables(size):
    angle = np.arange(size)[:, None] * (2.0 * np.arange(size)[None, :] + 1.0) * (math.pi / (2 * size))
    strips = size // LANES
    cos, sin = (part.reshape(size, strips, 1, LANES) for part in (np.cos(angle), np.sin(angle)))
    table = np.concatenate([cos, -sin], axis=2).reshape(size, 2 * size)
    return jnp.asarray(table, jnp.bfloat16), jnp.asarray(table.T / size, jnp.bfloat16)


def dot(left, right):
    return jnp.dot(left, right, preferred_element_type=jnp.float32)


def alternating():
    odd = lax.broadcasted_iota(jnp.int32, (SUBLANES, LANES), 1) % 2
    return 1.0 - 2.0 * odd.astype(jnp.float32)


def place(half_blocks):
    index = lax.axis_index("ctx")
    return index // half_blocks, lax.rem(index, half_blocks)


def real_of(strip):
    return pl.ds(2 * strip * LANES, LANES)


def imag_of(strip):
    return pl.ds((2 * strip + 1) * LANES, LANES)


def begin(copies):
    for copy in copies:
        copy.start()
    return copies


def end(copies):
    for copy in copies:
        copy.wait()


def call(kernel, name, operands, outputs, scratch, weight=1, vmem=VMEM_BYTES):
    hbm = pl.BlockSpec(memory_space=pltpu.HBM)
    return pl.pallas_call(
        kernel,
        in_specs=[hbm] * len(operands),
        out_specs=[hbm] * len(outputs),
        out_shape=outputs,
        scratch_shapes=scratch,
        compiler_params=pltpu.CompilerParams(vmem_limit_bytes=vmem),
        cost_estimate=pl.CostEstimate(flops=weight, bytes_accessed=weight, transcendentals=0),
        name=name,
    )(*operands)


def gate(near, arrays, repeats, half_blocks):
    rows_all, tokens = arrays[0].shape
    rows = rows_all // repeats
    share = rows // (2 * half_blocks)

    def kernel(pre_ref, value_ref, post_ref, cot_ref, out_ref, left_ref, right_ref, result_ref, in_sems, out_sems):
        half, _ = place(half_blocks)
        use_gated = half == 0 if near else half != 0

        def fetch(r, left, right):
            at = pl.ds(r * rows, rows)
            return (
                pltpu.make_async_copy(left.at[at], left_ref.at[r], in_sems.at[0, r]),
                pltpu.make_async_copy(right.at[at], right_ref.at[r], in_sems.at[1, r]),
            )

        @pl.when(use_gated)
        def _():
            for r in range(repeats):
                begin(fetch(r, pre_ref, value_ref))

        @pl.when(jnp.logical_not(use_gated))
        def _():
            for r in range(repeats):
                begin(fetch(r, cot_ref, post_ref))

        sent = []
        for r in range(repeats):
            end(fetch(r, pre_ref, value_ref))
            product = left_ref[r].astype(jnp.float32) * right_ref[r].astype(jnp.float32)
            product = product.astype(jnp.bfloat16).reshape(2, half_blocks, share, tokens)
            for side in range(2):
                result_ref[r, :, side] = product[side]
            sent += begin([pltpu.make_async_copy(result_ref.at[r], out_ref.at[:, r], out_sems.at[r])])
        end(sent)

    return call(
        kernel,
        "gate_near" if near else "gate_own",
        arrays,
        [jax.ShapeDtypeStruct((half_blocks, repeats, 2, share, tokens), jnp.bfloat16)],
        [
            pltpu.VMEM((repeats, rows, tokens), jnp.bfloat16),
            pltpu.VMEM((repeats, rows, tokens), jnp.bfloat16),
            pltpu.VMEM((repeats, half_blocks, 2, share, tokens), jnp.bfloat16),
            pltpu.SemaphoreType.DMA((2, repeats)),
            pltpu.SemaphoreType.DMA((repeats,)),
        ],
        weight=1 if near else HEAVY,
    )[0]


def finish(early, late, arrays, terms):
    half_blocks, repeats, sides, share, tokens = early.shape
    count, rows = repeats * sides, half_blocks * share

    def kernel(early_ref, late_ref, pre_ref, value_ref, post_ref, cot_ref, mine_ref, theirs_ref, *refs):
        out_refs, (held_ref, total_ref, sems, total_sem) = refs[:5], refs[5:]
        half, _ = place(half_blocks)
        sent = []
        for part in range(count):
            r, side = part // sides, part % sides
            at = pl.ds(part * rows, rows)
            first = early_ref[:, r, side].reshape(rows, tokens).astype(jnp.float32)
            second = late_ref[:, r, side].reshape(rows, tokens).astype(jnp.float32)
            conv = jnp.where(half == 0, first, second)
            grad = jnp.where(half == 0, second, first)
            for which, (factor_ref, result) in enumerate(
                ((post_ref, conv), (value_ref, grad), (pre_ref, grad), (cot_ref, conv))
            ):
                held_ref[which, part] = (factor_ref[at].astype(jnp.float32) * result).astype(jnp.bfloat16)
                sent += begin(
                    [pltpu.make_async_copy(held_ref.at[which, part], out_refs[which].at[at], sems.at[which, part])]
                )
        total_ref[...] = mine_ref[...] + theirs_ref[...].astype(jnp.float32)
        sent += begin([pltpu.make_async_copy(total_ref, out_refs[4], total_sem)])
        end(sent)

    shapes = [jax.ShapeDtypeStruct(arrays[0].shape, jnp.bfloat16)] * 4
    return pl.pallas_call(
        kernel,
        in_specs=[pl.BlockSpec(memory_space=pltpu.VMEM)] * 8,
        out_specs=[pl.BlockSpec(memory_space=pltpu.HBM)] * 5,
        out_shape=shapes + [jax.ShapeDtypeStruct(terms[0].shape, jnp.float32)],
        scratch_shapes=[
            pltpu.VMEM((4, count, rows, tokens), jnp.bfloat16),
            pltpu.VMEM(terms[0].shape, jnp.float32),
            pltpu.SemaphoreType.DMA((4, count)),
            pltpu.SemaphoreType.DMA,
        ],
        compiler_params=pltpu.CompilerParams(vmem_limit_bytes=VMEM_BYTES // 6),
        name="finish",
    )(early, late, *arrays, *terms)


def transform_taps(pieces, half_blocks, groups, forward):
    share, lags = pieces[0].shape
    size = forward.shape[0]
    count = groups * lags // size
    rows, width = 2 * share, 2 * size

    def kernel(own_ref, group_ref, half_ref, both_ref, forward_hbm, out_hbm, piece_ref, forward_ref, stage_ref, out_ref, sems):
        sources = (own_ref, group_ref, half_ref, both_ref)
        loads = begin([pltpu.make_async_copy(ref, piece_ref.at[at], sems.at[at]) for at, ref in enumerate(sources)])
        table = begin([pltpu.make_async_copy(forward_hbm, forward_ref, sems.at[4])])
        half, _ = place(half_blocks)
        group = lax.axis_index("dp")
        end(loads)
        for at in range(4):
            side = half if at < 2 else 1 - half
            first = (group if at % 2 == 0 else 1 - group) * (lags // size)
            target = pl.ds(pl.multiple_of(side * share, share), share)
            for k in range(lags // size):
                stage_ref[first + k, target] = piece_ref[at, :, k * size : (k + 1) * size]
        end(table)
        spectrum = dot(stage_ref[...].reshape(count * rows, size), forward_ref[...]).reshape(count, rows, width)
        turn = jnp.where(half == 0, 1.0, -1.0).astype(jnp.float32)
        sign = alternating()[:1]
        sent = []
        for k in range(count):
            for strip in range(size // LANES):
                re = slice(2 * strip * LANES, (2 * strip + 1) * LANES)
                im = slice((2 * strip + 1) * LANES, (2 * strip + 2) * LANES)
                real, imag = spectrum[k, :, re], spectrum[k, :, im]
                if k > 0:
                    real, imag = real - sign * spectrum[k - 1, :, im], imag + sign * spectrum[k - 1, :, re]
                out_ref[k, :, re] = real
                out_ref[k, :, im] = turn * imag
            sent += begin([pltpu.make_async_copy(out_ref.at[k], out_hbm.at[k], sems.at[5 + k])])
        end(sent)

    return call(
        kernel,
        "taps",
        (*pieces, forward),
        [jax.ShapeDtypeStruct((count, rows, width), jnp.float32)],
        [
            pltpu.VMEM((4, share, lags), jnp.bfloat16),
            pltpu.VMEM((size, width), jnp.bfloat16),
            pltpu.VMEM((count, rows, size), jnp.bfloat16),
            pltpu.VMEM((count, rows, width), jnp.float32),
            pltpu.SemaphoreType.DMA((5 + count,)),
        ],
    )[0]


def add(total, term):
    return term if total is None else (total[0] + term[0], total[1] + term[1])


def times(a, b):
    return a[0] * b[0] - a[1] * b[1], a[0] * b[1] + a[1] * b[0]


def conj_times(a, b):
    return a[0] * b[0] + a[1] * b[1], a[0] * b[1] - a[1] * b[0]


def transform(stage_ref, forward_ref, spec_ref):
    width = spec_ref.shape[-1]
    staged = stage_ref[...].reshape(-1, stage_ref.shape[-1])
    for strip in range(width // (2 * LANES)):
        columns = slice(2 * strip * LANES, 2 * (strip + 1) * LANES)
        spec_ref[..., columns] = dot(staged, forward_ref[:, columns]).reshape(spec_ref.shape[:-1] + (2 * LANES,))


def stage_copies(source, stage_ref, sems, outer, half_blocks):
    count, _, size = stage_ref.shape
    tokens = source.shape[2]
    merge = size // tokens
    half, _ = place(half_blocks)
    copies = []
    for k in range(count):
        block = order(k, count, half, outer)
        for q in range(merge):
            target = stage_ref.at[k, :, pl.ds(q * tokens, tokens)]
            copies.append(pltpu.make_async_copy(source.at[block * merge + q], target, sems.at[k, q]))
    return copies


def order(k, count, half, outer):
    return jnp.where(half == (0 if outer else 1), k, count - 1 - k)


def tile_loop(rows, body):
    @pl.loop(0, rows // SUBLANES)
    def _(tile):
        body(pl.multiple_of(tile * SUBLANES, SUBLANES))


def parts(ref, k, row, strip):
    return ref[k, row, real_of(strip)], ref[k, row, imag_of(strip)]


def keep(ref, k, row, strip, value):
    ref[k, row, real_of(strip)], ref[k, row, imag_of(strip)] = value


def give_back(prod_ref, inverse_ref, held_ref, out_ref, sems, outer, half_blocks):
    count, rows, width = prod_ref.shape
    merge, tokens = held_ref.shape[1], held_ref.shape[3]
    half, _ = place(half_blocks)
    sent = []
    result = dot(prod_ref[...].astype(jnp.bfloat16).reshape(count * rows, width), inverse_ref[...])
    result = result.astype(jnp.bfloat16).reshape(count, rows, width // 2)
    for k in range(count):
        block = order(k, count, half, outer)
        for q in range(merge):
            held_ref[k, q] = result[k, :, q * tokens : (q + 1) * tokens]
            sent += begin(
                [pltpu.make_async_copy(held_ref.at[k, q], out_ref.at[block * merge + q], sems.at[k, q])]
            )
    end(sent)


def early_result(near, filt, half_blocks, tables):
    forward, inverse = tables
    _, rows, tokens = near.shape
    size, width = forward.shape
    merge = size // tokens
    count = half_blocks // merge
    filters = filt.shape[1]

    def kernel(near_hbm, filt_hbm, forward_hbm, inverse_hbm, out_hbm, stage_ref, filt_ref, forward_ref, inverse_ref, spec_ref, prod_ref, held_ref, sems, stage_sems, out_sems):
        staged = begin(stage_copies(near_hbm, stage_ref, stage_sems, True, half_blocks))
        table = begin([pltpu.make_async_copy(forward_hbm, forward_ref, sems.at[0])])
        rest = begin(
            [
                pltpu.make_async_copy(filt_hbm.at[pl.ds(0, count)], filt_ref, sems.at[1]),
                pltpu.make_async_copy(inverse_hbm, inverse_ref, sems.at[2]),
            ]
        )
        end(staged)
        end(table)
        transform(stage_ref, forward_ref, spec_ref)
        end(rest)

        def tile(first):
            row = pl.ds(first, SUBLANES)
            tap_row = pl.ds(pl.multiple_of(lax.rem(first, filters), SUBLANES), SUBLANES)
            for strip in range(size // LANES):
                taps = [parts(filt_ref, k, tap_row, strip) for k in range(count)]
                spans = [parts(spec_ref, k, row, strip) for k in range(count)]
                for out in range(count):
                    total = None
                    for k in range(out + 1):
                        total = add(total, times(taps[out - k], spans[k]))
                    keep(prod_ref, out, row, strip, total)

        tile_loop(rows, tile)
        give_back(prod_ref, inverse_ref, held_ref, out_hbm, out_sems, True, half_blocks)

    return call(
        kernel,
        "early",
        (near, filt, forward, inverse),
        [jax.ShapeDtypeStruct((half_blocks, rows, tokens), jnp.bfloat16)],
        [
            pltpu.VMEM((count, rows, size), jnp.bfloat16),
            pltpu.VMEM((count, filters, width), jnp.float32),
            pltpu.VMEM(forward.shape, jnp.bfloat16),
            pltpu.VMEM(inverse.shape, jnp.bfloat16),
            pltpu.VMEM((count, rows, width), jnp.float32),
            pltpu.VMEM((count, rows, width), jnp.float32),
            pltpu.VMEM((count, merge, rows, tokens), jnp.bfloat16),
            pltpu.SemaphoreType.DMA((3,)),
            pltpu.SemaphoreType.DMA((count, merge)),
            pltpu.SemaphoreType.DMA((count, merge)),
        ],
    )[0]


def late_result(far, filt, partial, half_blocks, tables):
    forward, inverse = tables
    _, rows, tokens = far.shape
    size, width = forward.shape
    merge = size // tokens
    count = half_blocks // merge
    filters = filt.shape[1]

    def kernel(far_hbm, filt_hbm, partial_hbm, forward_hbm, inverse_hbm, out_hbm, stage_ref, filt_ref, forward_ref, inverse_ref, spec_ref, prod_ref, held_ref, sems, stage_sems, out_sems):
        staged = begin(stage_copies(far_hbm, stage_ref, stage_sems, False, half_blocks))
        table = begin([pltpu.make_async_copy(forward_hbm, forward_ref, sems.at[0])])
        rest = begin(
            [
                pltpu.make_async_copy(filt_hbm, filt_ref, sems.at[1]),
                pltpu.make_async_copy(partial_hbm, prod_ref, sems.at[2]),
            ]
        )
        last = begin([pltpu.make_async_copy(inverse_hbm, inverse_ref, sems.at[3])])
        end(staged)
        end(table)
        transform(stage_ref, forward_ref, spec_ref)
        end(rest)

        def tile(first):
            row = pl.ds(first, SUBLANES)
            tap_row = pl.ds(pl.multiple_of(lax.rem(first, filters), SUBLANES), SUBLANES)
            for strip in range(size // LANES):
                taps = [parts(filt_ref, k, tap_row, strip) for k in range(2 * count)]
                spans = [parts(spec_ref, k, row, strip) for k in range(count)]
                for out in range(count):
                    total = parts(prod_ref, out, row, strip)
                    for k in range(count):
                        total = add(total, conj_times(taps[count + out - k], spans[k]))
                    keep(prod_ref, out, row, strip, total)

        tile_loop(rows, tile)
        end(last)
        give_back(prod_ref, inverse_ref, held_ref, out_hbm, out_sems, False, half_blocks)

    return call(
        kernel,
        "late",
        (far, filt, partial, forward, inverse),
        [jax.ShapeDtypeStruct((half_blocks, rows, tokens), jnp.bfloat16)],
        [
            pltpu.VMEM((count, rows, size), jnp.bfloat16),
            pltpu.VMEM((2 * count, filters, width), jnp.float32),
            pltpu.VMEM(forward.shape, jnp.bfloat16),
            pltpu.VMEM(inverse.shape, jnp.bfloat16),
            pltpu.VMEM((count, rows, width), jnp.float32),
            pltpu.VMEM((count, rows, width), jnp.float32),
            pltpu.VMEM((count, merge, rows, tokens), jnp.bfloat16),
            pltpu.SemaphoreType.DMA((4,)),
            pltpu.SemaphoreType.DMA((count, merge)),
            pltpu.SemaphoreType.DMA((count, merge)),
        ],
        weight=HEAVY,
        vmem=VMEM_BYTES - (2 << 20),
    )[0]


def lag_products(near_ref, other_ref, row_at, strip, repeats, filters, totals):
    count = near_ref.shape[0]
    sums = [None] * len(totals)
    for repeat in range(repeats):
        row = pl.ds(pl.multiple_of(repeat * filters + row_at, SUBLANES), SUBLANES)
        near = [parts(near_ref, k, row, strip) for k in range(count)]
        other = [parts(other_ref, k, row, strip) for k in range(count)]
        for at, total in enumerate(totals):
            for a in range(count):
                if 0 <= total - a < count:
                    sums[at] = add(sums[at], conj_times(near[a], other[total - a]))
    return sums


def join_lags(ref, row, joint_ref, base):
    lags, size = ref.shape[0], ref.shape[2] // 2
    sign = alternating()[:1]
    for k in range(lags):
        for strip in range(size // LANES):
            real, imag = parts(ref, k, row, strip)
            if k + 1 < lags:
                next_real, next_imag = parts(ref, k + 1, row, strip)
                real, imag = real + sign * next_imag, imag - sign * next_real
            keep(joint_ref, base + k, slice(None), strip, (real.astype(jnp.bfloat16), imag.astype(jnp.bfloat16)))


def local_terms(near, own, filt, half_blocks, tables):
    forward, inverse = tables
    _, rows, tokens = near.shape
    size, width = forward.shape
    merge = size // tokens
    count = half_blocks // merge
    filters = filt.shape[1]
    kept, lags = filters // 2, count * size
    repeats = rows // filters

    def kernel(near_hbm, own_hbm, filt_hbm, forward_hbm, inverse_hbm, partial_hbm, mine_hbm, give_hbm, stage_ref, filt_ref, forward_ref, inverse_ref, near_ref, own_ref, prod_ref, local_ref, joint_ref, mine_ref, give_ref, sems, stage_sems, own_sems):
        staged = begin(stage_copies(own_hbm, stage_ref.at[1], own_sems, False, half_blocks))
        staged += begin(stage_copies(near_hbm, stage_ref.at[0], stage_sems, True, half_blocks))
        table = begin([pltpu.make_async_copy(forward_hbm, forward_ref, sems.at[0])])
        rest = begin(
            [
                pltpu.make_async_copy(filt_hbm.at[pl.ds(0, count)], filt_ref, sems.at[1]),
                pltpu.make_async_copy(inverse_hbm, inverse_ref, sems.at[2]),
            ]
        )
        half, _ = place(half_blocks)
        turn = jnp.where(half == 0, 1.0, -1.0).astype(jnp.float32)
        end(staged)
        end(table)
        transform(stage_ref.at[1], forward_ref, own_ref)
        transform(stage_ref.at[0], forward_ref, near_ref)
        end(rest)

        def tile(first):
            row = pl.ds(first, SUBLANES)
            tap_row = pl.ds(pl.multiple_of(lax.rem(first, filters), SUBLANES), SUBLANES)
            for strip in range(size // LANES):
                taps = [parts(filt_ref, k, tap_row, strip) for k in range(count)]
                spans = [parts(own_ref, k, row, strip) for k in range(count)]
                for out in range(count):
                    total = None
                    for k in range(out + 1):
                        total = add(total, conj_times(taps[out - k], spans[k]))
                    keep(prod_ref, out, row, strip, total)

        tile_loop(rows, tile)
        sent = begin([pltpu.make_async_copy(prod_ref, partial_hbm, sems.at[3])])

        def lag_tile(first):
            for strip in range(size // LANES):
                sums = lag_products(near_ref, own_ref, first, strip, repeats, filters, [count - 1 - k for k in range(count)])
                for k, (real, imag) in enumerate(sums):
                    keep(local_ref, k, pl.ds(first, SUBLANES), strip, (real, turn * imag))

        tile_loop(filters, lag_tile)
        for at in range(2):
            side = pl.ds(pl.multiple_of((half if at == 0 else 1 - half) * kept, SUBLANES), kept)
            join_lags(local_ref, side, joint_ref, at * count)
        result = dot(joint_ref[...].reshape(2 * count * kept, width), inverse_ref[...]).reshape(2 * count, kept, size)
        for k in range(count):
            columns = slice(k * size, (k + 1) * size)
            mine_ref[:, columns] = result[k]
            give_ref[:, columns] = result[count + k].astype(jnp.bfloat16)
        sent += begin(
            [
                pltpu.make_async_copy(mine_ref, mine_hbm, sems.at[4]),
                pltpu.make_async_copy(give_ref, give_hbm, sems.at[5]),
            ]
        )
        end(sent)

    return call(
        kernel,
        "local",
        (near, own, filt, forward, inverse),
        [
            jax.ShapeDtypeStruct((count, rows, width), jnp.float32),
            jax.ShapeDtypeStruct((kept, lags), jnp.float32),
            jax.ShapeDtypeStruct((kept, lags), jnp.bfloat16),
        ],
        [
            pltpu.VMEM((2, count, rows, size), jnp.bfloat16),
            pltpu.VMEM((count, filters, width), jnp.float32),
            pltpu.VMEM(forward.shape, jnp.bfloat16),
            pltpu.VMEM(inverse.shape, jnp.bfloat16),
            pltpu.VMEM((count, rows, width), jnp.float32),
            pltpu.VMEM((count, rows, width), jnp.float32),
            pltpu.VMEM((count, rows, width), jnp.float32),
            pltpu.VMEM((count, filters, width), jnp.float32),
            pltpu.VMEM((2 * count, kept, width), jnp.bfloat16),
            pltpu.VMEM((kept, lags), jnp.float32),
            pltpu.VMEM((kept, lags), jnp.bfloat16),
            pltpu.SemaphoreType.DMA((6,)),
            pltpu.SemaphoreType.DMA((count, merge)),
            pltpu.SemaphoreType.DMA((count, merge)),
        ],
    )


def cross_terms(near, far, local, given, half_blocks, tables):
    forward, inverse = tables
    _, rows, tokens = near.shape
    size, width = forward.shape
    merge = size // tokens
    count = half_blocks // merge
    kept, lags = local.shape
    filters = 2 * kept
    repeats = rows // filters

    def kernel(near_hbm, far_hbm, local_hbm, given_hbm, forward_hbm, inverse_hbm, mine_hbm, theirs_hbm, stage_ref, local_ref, given_ref, forward_ref, inverse_ref, near_ref, far_ref, cross_ref, joint_ref, held_ref, mine_ref, theirs_ref, sems, stage_sems, far_sems):
        staged = begin(stage_copies(near_hbm, stage_ref.at[0], stage_sems, True, half_blocks))
        staged += begin(stage_copies(far_hbm, stage_ref.at[1], far_sems, False, half_blocks))
        table = begin([pltpu.make_async_copy(forward_hbm, forward_ref, sems.at[0])])
        rest = begin(
            [
                pltpu.make_async_copy(inverse_hbm, inverse_ref, sems.at[1]),
                pltpu.make_async_copy(local_hbm, local_ref, sems.at[2]),
                pltpu.make_async_copy(given_hbm, given_ref, sems.at[5]),
            ]
        )
        half, _ = place(half_blocks)
        group = lax.axis_index("dp")
        turn = jnp.where(half == 0, 1.0, -1.0).astype(jnp.float32)
        end(staged)
        end(table)
        transform(stage_ref.at[0], forward_ref, near_ref)
        transform(stage_ref.at[1], forward_ref, far_ref)

        def lag_tile(first):
            row = pl.ds(first, SUBLANES)
            for strip in range(size // LANES):
                totals = [2 * count - 1 - k for k in range(1, 2 * count)]
                sums = lag_products(near_ref, far_ref, half * kept + first, strip, repeats, filters, totals)
                for k, (real, imag) in enumerate(sums):
                    keep(cross_ref, k + 1, row, strip, (real, turn * imag))
                keep(cross_ref, 0, row, strip, (jnp.zeros_like(real), jnp.zeros_like(real)))

        tile_loop(kept, lag_tile)
        join_lags(cross_ref, slice(None), joint_ref, 0)
        end(rest)
        result = dot(joint_ref[...].reshape(2 * count * kept, width), inverse_ref[...])
        result = result.reshape(2, count, kept, size)
        for k in range(count):
            columns = slice(k * size, (k + 1) * size)
            held_ref[0, k] = result[0, k] + local_ref[:, columns] + given_ref[:, columns].astype(jnp.float32)
        held_ref[1] = result[1]
        for k in range(count):
            columns = slice(k * size, (k + 1) * size)
            mine_ref[:, columns] = held_ref[group, k]
            theirs_ref[:, columns] = held_ref[1 - group, k].astype(jnp.bfloat16)
        end(
            begin(
                [
                    pltpu.make_async_copy(theirs_ref, theirs_hbm, sems.at[3]),
                    pltpu.make_async_copy(mine_ref, mine_hbm, sems.at[4]),
                ]
            )
        )

    return call(
        kernel,
        "cross",
        (near, far, local, given, forward, inverse),
        [jax.ShapeDtypeStruct((kept, lags), jnp.float32), jax.ShapeDtypeStruct((kept, lags), jnp.bfloat16)],
        [
            pltpu.VMEM((2, count, rows, size), jnp.bfloat16),
            pltpu.VMEM((kept, lags), jnp.float32),
            pltpu.VMEM((kept, lags), jnp.bfloat16),
            pltpu.VMEM(forward.shape, jnp.bfloat16),
            pltpu.VMEM(inverse.shape, jnp.bfloat16),
            pltpu.VMEM((count, rows, width), jnp.float32),
            pltpu.VMEM((count, rows, width), jnp.float32),
            pltpu.VMEM((2 * count, kept, width), jnp.float32),
            pltpu.VMEM((2 * count, kept, width), jnp.bfloat16),
            pltpu.VMEM((2, count, kept, size), jnp.float32),
            pltpu.VMEM((kept, lags), jnp.float32),
            pltpu.VMEM((kept, lags), jnp.bfloat16),
            pltpu.SemaphoreType.DMA((6,)),
            pltpu.SemaphoreType.DMA((count, merge)),
            pltpu.SemaphoreType.DMA((count, merge)),
        ],
    )


def body(pre_gate, values, post_gate, filters, cotangent):
    blocks = lax.axis_size("ctx")
    groups = lax.axis_size("dp")
    half_blocks = blocks // 2
    local_rows, tokens = pre_gate.shape
    local_filters = filters.shape[0]
    repeats = local_rows // (local_filters * blocks)
    rows = 2 * local_filters * repeats
    tables = dft_tables(2 * tokens)
    arrays = (pre_gate, values, post_gate, cotangent)
    sides = [list(range(half_blocks)), list(range(half_blocks, blocks))]
    across = [(i, blocks + (i ^ half_blocks)) for i in range(blocks)]
    across = across + [(b, a) for a, b in across]

    def spread(array):
        return lax.all_to_all(array, "ctx", split_axis=0, concat_axis=0, tiled=True, axis_index_groups=sides)

    def swap(array):
        return lax.ppermute(array, "ctx", [(i, i ^ half_blocks) for i in range(blocks)])

    near = spread(gate(True, arrays, repeats, half_blocks).reshape(half_blocks, rows, tokens))
    own = gate(False, arrays, repeats, half_blocks).reshape(half_blocks, rows, tokens)
    taps = filters.astype(jnp.bfloat16)
    pieces = (
        taps,
        lax.ppermute(taps, "dp", [(0, 1), (1, 0)]),
        swap(taps),
        lax.ppermute(taps, ("dp", "ctx"), across),
    )
    near, own, *pieces = lax.optimization_barrier((near, own, *pieces))
    far = swap(near)
    own = spread(own)
    filt = transform_taps(pieces, half_blocks, groups, tables[0])
    early = early_result(near, filt, half_blocks, tables)
    early, own = lax.optimization_barrier((early, own))
    early = spread(early)
    partial, local, give = local_terms(near, own, filt, half_blocks, tables)
    far, given = lax.optimization_barrier((far, swap(give)))
    late = late_result(far, filt, partial, half_blocks, tables)
    late, near, far = lax.optimization_barrier((late, near, far))
    late = spread(late)
    mine, theirs = cross_terms(near, far, local, given, half_blocks, tables)
    theirs = lax.ppermute(theirs, "dp", [(0, 1), (1, 0)])

    shape = (half_blocks, repeats, 2, local_filters, tokens)
    mixed, pre_grad, value_grad, post_grad, filter_grad = finish(
        early.reshape(shape), late.reshape(shape), arrays, (mine, theirs)
    )
    return (mixed, pre_grad, value_grad, post_grad, filter_grad)


def matmul(left, right):
    return jnp.dot(left, right, precision=lax.Precision.HIGHEST, preferred_element_type=jnp.float32)


def contract(form, left, right):
    return jnp.einsum(
        form, left, right, precision=lax.Precision.HIGHEST, preferred_element_type=jnp.float32
    )


def phases(height, width, modulus):
    product = lax.broadcasted_iota(jnp.int32, (height, width), 0) * lax.broadcasted_iota(
        jnp.int32, (height, width), 1
    )
    return (product % modulus).astype(jnp.float32) * (2.0 * math.pi / modulus)


def build_tables(blocks, tokens):
    factor = 1
    for candidate in range(1, tokens + 1):
        if tokens % candidate == 0 and candidate * candidate <= tokens:
            factor = candidate
    second = tokens // factor
    rows = blocks + 1
    total = 2 * blocks * tokens
    first_angle = phases(rows, blocks, 2 * blocks)
    twist_angle = phases(rows, tokens, total)
    inner_angle = phases(factor, factor, factor)
    middle_angle = phases(factor, second, tokens)
    outer_angle = phases(second, second, second)
    back_angle = phases(blocks, rows, 2 * blocks)
    column = lax.broadcasted_iota(jnp.int32, (blocks, rows), 1)
    weight = jnp.where((column == 0) | (column == blocks), 1.0, 2.0).astype(jnp.float32) / total
    return {
        "first_cos": jnp.cos(first_angle),
        "first_nsin": -jnp.sin(first_angle),
        "twist_cos": jnp.cos(twist_angle),
        "twist_sin": jnp.sin(twist_angle),
        "inner_cos": jnp.cos(inner_angle),
        "inner_sin": jnp.sin(inner_angle),
        "middle_cos": jnp.cos(middle_angle),
        "middle_sin": jnp.sin(middle_angle),
        "outer_cos": jnp.cos(outer_angle),
        "outer_sin": jnp.sin(outer_angle),
        "back_cos": weight * jnp.cos(back_angle),
        "back_sin": weight * jnp.sin(back_angle),
    }


def expand(table, ndim):
    return table.reshape((table.shape[0],) + (1,) * (ndim - 2) + (table.shape[1],))


def block_table(cos_part, sin_part):
    return jnp.stack([jnp.stack([cos_part, sin_part]), jnp.stack([-sin_part, cos_part])])


def wave(real_part, imag_part, tables, sign):
    shape = real_part.shape
    factor = tables["inner_cos"].shape[0]
    second = tables["outer_cos"].shape[0]
    stacked = jnp.stack(
        [real_part.reshape(-1, factor, second), imag_part.reshape(-1, factor, second)]
    )
    inner_table = block_table(tables["inner_cos"], sign * tables["inner_sin"])
    middle = contract("prab,pqac->qrcb", stacked, inner_table)
    middle_cos = tables["middle_cos"]
    middle_sin = sign * tables["middle_sin"]
    real_turn = middle[0] * middle_cos - middle[1] * middle_sin
    imag_turn = middle[0] * middle_sin + middle[1] * middle_cos
    turned = jnp.stack([real_turn, imag_turn])
    outer_table = block_table(tables["outer_cos"], sign * tables["outer_sin"])
    result = contract("prcb,pqbd->qrdc", turned, outer_table)
    return (result[0].reshape(shape), result[1].reshape(shape))


def finish_forward(real_first, imag_first, tables):
    ndim = real_first.ndim
    twist_cos = expand(tables["twist_cos"], ndim)
    twist_sin = expand(tables["twist_sin"], ndim)
    real_twist = real_first * twist_cos + imag_first * twist_sin
    imag_twist = imag_first * twist_cos - real_first * twist_sin
    return wave(real_twist, imag_twist, tables, -1.0)


def spectrum(signal, tables):
    flat = signal.reshape(signal.shape[0], -1)
    shape = (tables["first_cos"].shape[0],) + signal.shape[1:]
    real_first = matmul(tables["first_cos"], flat).reshape(shape)
    imag_first = matmul(tables["first_nsin"], flat).reshape(shape)
    return finish_forward(real_first, imag_first, tables)


def inverse_prepare(real_spec, imag_spec, tables):
    ndim = real_spec.ndim
    real_wave, imag_wave = wave(real_spec, imag_spec, tables, 1.0)
    twist_cos = expand(tables["twist_cos"], ndim)
    twist_sin = expand(tables["twist_sin"], ndim)
    real_twist = real_wave * twist_cos - imag_wave * twist_sin
    imag_twist = real_wave * twist_sin + imag_wave * twist_cos
    rows = real_spec.shape[0]
    return (real_twist.reshape(rows, -1), imag_twist.reshape(rows, -1))


def inverse_full(real_spec, imag_spec, tables):
    real_flat, imag_flat = inverse_prepare(real_spec, imag_spec, tables)
    signal = matmul(tables["back_cos"], real_flat) - matmul(tables["back_sin"], imag_flat)
    return signal.reshape((tables["back_cos"].shape[0],) + real_spec.shape[1:])


def plain_body(pre_gate, values, post_gate, filters, cotangent):
    blocks = lax.axis_size("ctx")
    groups = lax.axis_size("dp")
    local_rows = pre_gate.shape[0]
    tokens = pre_gate.shape[1]
    local_filters = filters.shape[0]
    repeats = local_rows // (local_filters * blocks)
    share = blocks // groups
    tables = build_tables(blocks, tokens)
    gated = (pre_gate.astype(jnp.float32) * values.astype(jnp.float32)).astype(jnp.bfloat16)
    conv_grad = (cotangent.astype(jnp.float32) * post_gate.astype(jnp.float32)).astype(jnp.bfloat16)
    gated_blocks = gated.reshape(repeats, blocks, local_filters, tokens)
    grad_blocks = conv_grad.reshape(repeats, blocks, local_filters, tokens)
    tap_local = jnp.transpose(filters.reshape(local_filters, share, tokens), (1, 0, 2))
    piece = lax.all_gather(tap_local, "dp", axis=0, tiled=True)
    count = piece.shape[0]
    flat = piece.reshape(count, -1)
    cos_cols = tables["first_cos"]
    sin_cols = tables["first_nsin"]
    real_first = matmul(cos_cols, flat)
    imag_first = matmul(sin_cols, flat)
    spec_shape = (blocks + 1, 1, local_filters, tokens)
    filt_real, filt_imag = finish_forward(
        real_first.reshape(spec_shape), imag_first.reshape(spec_shape), tables
    )

    def single_spectrum(received):
        signal = received.reshape(blocks, -1, received.shape[2], received.shape[3])
        return spectrum(signal.astype(jnp.float32), tables)

    gated_real, gated_imag = single_spectrum(
        lax.all_to_all(gated_blocks, "ctx", split_axis=1, concat_axis=0, tiled=True)
    )
    prod_real = gated_real * filt_real - gated_imag * filt_imag
    prod_imag = gated_real * filt_imag + gated_imag * filt_real
    result = inverse_full(prod_real, prod_imag, tables).astype(jnp.bfloat16)
    conv_chan = result.reshape(blocks * repeats, 1, local_filters, tokens)
    conv_seq = lax.all_to_all(conv_chan, "ctx", split_axis=0, concat_axis=1, tiled=True)
    grad_real, grad_imag = single_spectrum(
        lax.all_to_all(grad_blocks, "ctx", split_axis=1, concat_axis=0, tiled=True)
    )
    prod_real = filt_real * grad_real + filt_imag * grad_imag
    prod_imag = filt_real * grad_imag - filt_imag * grad_real
    result = inverse_full(prod_real, prod_imag, tables).astype(jnp.bfloat16)
    gated_chan_grad = result.reshape(blocks * repeats, 1, local_filters, tokens)
    gated_seq_grad = lax.all_to_all(gated_chan_grad, "ctx", split_axis=0, concat_axis=1, tiled=True)
    cross_real = jnp.sum(gated_real * grad_real + gated_imag * grad_imag, axis=1)
    cross_imag = jnp.sum(gated_real * grad_imag - gated_imag * grad_real, axis=1)
    wave_real, wave_imag = inverse_prepare(cross_real, cross_imag, tables)
    cos_rows = tables["back_cos"]
    sin_rows = tables["back_sin"]
    term = matmul(cos_rows, wave_real) - matmul(sin_rows, wave_imag)
    summed = lax.psum_scatter(
        term.reshape(lax.axis_size("dp") * share, local_filters, tokens).astype(jnp.bfloat16),
        "dp",
        scatter_dimension=0,
        tiled=True,
    ).astype(jnp.float32)
    filter_grad = jnp.transpose(summed, (1, 0, 2)).reshape(local_filters, share * tokens)
    conv_full = conv_seq.reshape(pre_gate.shape).astype(jnp.float32)
    gated_grad = gated_seq_grad.reshape(pre_gate.shape).astype(jnp.float32)
    mixed = (post_gate.astype(jnp.float32) * conv_full).astype(jnp.bfloat16)
    post_grad = (cotangent.astype(jnp.float32) * conv_full).astype(jnp.bfloat16)
    pre_grad = (gated_grad * values.astype(jnp.float32)).astype(jnp.bfloat16)
    value_grad = (gated_grad * pre_gate.astype(jnp.float32)).astype(jnp.bfloat16)
    return (mixed, pre_grad, value_grad, post_grad, filter_grad)


def solution(mesh):
    placed = (P("dp", "ctx"), P("dp", "ctx"), P("dp", "ctx"), P("ctx", "dp"), P("dp", "ctx"))
    groups, blocks = mesh.shape["dp"], mesh.shape["ctx"]

    def program(pre_gate, values, post_gate, filters, cotangent):
        kernels = groups == 2 and blocks >= 8 and blocks & (blocks - 1) == 0 and filters.shape[0] % 16 == 0
        return (body if kernels else plain_body)(pre_gate, values, post_gate, filters, cotangent)

    return jax.shard_map(
        program,
        mesh=mesh,
        in_specs=placed,
        out_specs=(P("dp", "ctx"), P("dp", "ctx"), P("dp", "ctx"), P("dp", "ctx"), P("ctx", "dp")),
        check_vma=False,
    )
```

```python
import math

import jax
import jax.numpy as jnp
import numpy as np
from jax import lax
from jax.experimental import pallas as pl
from jax.experimental.pallas import tpu as pltpu
from jax.sharding import PartitionSpec as P


LANES = 128
SUBLANES = 8
VMEM_BYTES = 60 * 1024 * 1024
HEAVY = 1 << 37


def dft_table(size):
    angle = np.arange(size)[:, None] * (2.0 * np.arange(size)[None, :] + 1.0) * (math.pi / (2 * size))
    strips = size // LANES
    cos, sin = (part.reshape(size, strips, 1, LANES) for part in (np.cos(angle), np.sin(angle)))
    return jnp.asarray(np.concatenate([cos, -sin], axis=2).reshape(size, 2 * size), jnp.bfloat16)


def dot(left, right):
    return jnp.dot(left, right, preferred_element_type=jnp.float32)


def back(spectrum, table):
    result = lax.dot_general(spectrum, table, (((1,), (1,)), ((), ())), preferred_element_type=jnp.float32)
    return result * (2.0 / table.shape[1])


def alternating():
    odd = lax.broadcasted_iota(jnp.int32, (SUBLANES, LANES), 1) % 2
    return 1.0 - 2.0 * odd.astype(jnp.float32)


def place(half_blocks):
    index = lax.axis_index("ctx")
    return index // half_blocks, lax.rem(index, half_blocks)


def real_of(strip):
    return pl.ds(2 * strip * LANES, LANES)


def imag_of(strip):
    return pl.ds((2 * strip + 1) * LANES, LANES)


def begin(copies):
    for copy in copies:
        copy.start()
    return copies


def end(copies):
    for copy in copies:
        copy.wait()


def call(kernel, name, operands, outputs, scratch, weight=1, vmem=VMEM_BYTES):
    hbm = pl.BlockSpec(memory_space=pltpu.HBM)
    return pl.pallas_call(
        kernel,
        in_specs=[hbm] * len(operands),
        out_specs=[hbm] * len(outputs),
        out_shape=outputs,
        scratch_shapes=scratch,
        compiler_params=pltpu.CompilerParams(vmem_limit_bytes=vmem),
        cost_estimate=pl.CostEstimate(flops=weight, bytes_accessed=weight, transcendentals=0),
        name=name,
    )(*operands)


def gate(arrays, filters, repeats, half_blocks):
    rows_all, tokens = arrays[0].shape
    rows = rows_all // repeats
    share = rows // (2 * half_blocks)
    piece = (repeats, 2, share, tokens)

    def kernel(pre_ref, value_ref, post_ref, cot_ref, filt_ref, out_ref, even_ref, odd_ref, taps_ref, in_ref, result_ref, filt_in, taps_out, in_sems, out_sems, own_sems, taps_sems):
        half, me = place(half_blocks)
        sources = (pre_ref, value_ref, cot_ref, post_ref)

        def fetch(r):
            at = pl.ds(r * rows, rows)
            return [
                pltpu.make_async_copy(ref.at[at], in_ref.at[which, r], in_sems.at[which, r])
                for which, ref in enumerate(sources)
            ]

        for r in range(repeats):
            begin(fetch(r))
        loaded = begin([pltpu.make_async_copy(filt_ref, filt_in, taps_sems.at[0])])
        sent = []
        for r in range(repeats):
            end(fetch(r))
            for which in range(2):
                product = in_ref[2 * which, r].astype(jnp.float32) * in_ref[2 * which + 1, r].astype(jnp.float32)
                product = product.astype(jnp.bfloat16).reshape(2, half_blocks, share, tokens)
                at = half if which == 0 else 1 - half
                for side in range(2):
                    result_ref[at, :, r, side] = product[side]
            for to in range(2):
                copy = pltpu.make_async_copy(result_ref.at[0, :, r], out_ref.at[to, :, r], out_sems.at[to, r])
                sent += begin([copy])
        for at in range(half_blocks // 2):
            for odd, target in enumerate((even_ref, odd_ref)):
                source = result_ref.at[1, jnp.bitwise_xor(me, 2 * at + odd)]
                sent += begin([pltpu.make_async_copy(source, target.at[at], own_sems.at[odd, at])])
        end(loaded)
        taps_out[...] = filt_in[...].astype(jnp.bfloat16)
        sent += begin([pltpu.make_async_copy(taps_out, taps_ref, taps_sems.at[1])])
        end(sent)

    own_shape = jax.ShapeDtypeStruct((half_blocks // 2, *piece), jnp.bfloat16)
    return call(
        kernel,
        "gate",
        (*arrays, filters),
        [
            jax.ShapeDtypeStruct((2, half_blocks, *piece), jnp.bfloat16),
            own_shape,
            own_shape,
            jax.ShapeDtypeStruct(filters.shape, jnp.bfloat16),
        ],
        [
            pltpu.VMEM((4, repeats, rows, tokens), jnp.bfloat16),
            pltpu.VMEM((2, half_blocks, *piece), jnp.bfloat16),
            pltpu.VMEM(filters.shape, filters.dtype),
            pltpu.VMEM(filters.shape, jnp.bfloat16),
            pltpu.SemaphoreType.DMA((4, repeats)),
            pltpu.SemaphoreType.DMA((2, repeats)),
            pltpu.SemaphoreType.DMA((2, half_blocks // 2)),
            pltpu.SemaphoreType.DMA((2,)),
        ],
    )


def exchange_own(even, odd, half_blocks):
    def swap(array, slot):
        return lax.ppermute(array, "ctx", [(i, i ^ slot) for i in range(2 * half_blocks)])

    odd = swap(odd, 1)
    groups = [([0], even[:1]), ([1], odd[:1])]
    for at in range(1, half_blocks // 2):
        pair = jnp.concatenate([even[at : at + 1], odd[at : at + 1]])
        groups.append(([2 * at, 2 * at + 1], swap(pair, 2 * at)))
    return groups


def finish(returned, arrays, terms):
    half_blocks, _, repeats, sides, share, tokens = returned.shape
    count, rows = repeats * sides, half_blocks * share

    def kernel(recv_ref, pre_ref, value_ref, post_ref, cot_ref, mine_ref, theirs_ref, *refs):
        out_refs, (held_ref, total_ref, sems, total_sem) = refs[:5], refs[5:]
        half, _ = place(half_blocks)
        sent = []
        for part in range(count):
            r, side = part // sides, part % sides
            at = pl.ds(part * rows, rows)
            conv = recv_ref[:, half, r, side].reshape(rows, tokens).astype(jnp.float32)
            grad = recv_ref[:, 1 - half, r, side].reshape(rows, tokens).astype(jnp.float32)
            for which, (factor_ref, result) in enumerate(
                ((post_ref, conv), (value_ref, grad), (pre_ref, grad), (cot_ref, conv))
            ):
                held_ref[which, part] = (factor_ref[at].astype(jnp.float32) * result).astype(jnp.bfloat16)
                sent += begin(
                    [pltpu.make_async_copy(held_ref.at[which, part], out_refs[which].at[at], sems.at[which, part])]
                )
        total_ref[...] = mine_ref[...] + theirs_ref[...].astype(jnp.float32)
        sent += begin([pltpu.make_async_copy(total_ref, out_refs[4], total_sem)])
        end(sent)

    shapes = [jax.ShapeDtypeStruct(arrays[0].shape, jnp.bfloat16)] * 4
    return pl.pallas_call(
        kernel,
        in_specs=[pl.BlockSpec(memory_space=pltpu.VMEM)] * 7,
        out_specs=[pl.BlockSpec(memory_space=pltpu.HBM)] * 5,
        out_shape=shapes + [jax.ShapeDtypeStruct(terms[0].shape, jnp.float32)],
        scratch_shapes=[
            pltpu.VMEM((4, count, rows, tokens), jnp.bfloat16),
            pltpu.VMEM(terms[0].shape, jnp.float32),
            pltpu.SemaphoreType.DMA((4, count)),
            pltpu.SemaphoreType.DMA,
        ],
        compiler_params=pltpu.CompilerParams(vmem_limit_bytes=VMEM_BYTES // 6),
        name="finish",
    )(returned, *arrays, *terms)


def pack_taps(taps, pair, half_blocks):
    share, lags = taps.shape

    def kernel(taps_ref, pair_ref, out_ref, held_ref, sems):
        half, _ = place(half_blocks)
        end(
            begin(
                [
                    pltpu.make_async_copy(taps_ref, held_ref.at[half], sems.at[0]),
                    pltpu.make_async_copy(pair_ref, held_ref.at[1 - half], sems.at[1]),
                ]
            )
        )
        end(begin([pltpu.make_async_copy(held_ref, out_ref, sems.at[2])]))

    return call(
        kernel,
        "pack_taps",
        (taps, pair),
        [jax.ShapeDtypeStruct((2, share, lags), jnp.bfloat16)],
        [pltpu.VMEM((2, share, lags), jnp.bfloat16), pltpu.SemaphoreType.DMA((3,))],
        weight=HEAVY,
    )[0]


def transform_taps(here, there, half_blocks, groups, table):
    sides, share, lags = here.shape
    size = table.shape[0]
    count = groups * lags // size
    rows, width = sides * share, 2 * size

    def kernel(here_ref, there_ref, table_hbm, out_hbm, piece_ref, table_ref, stage_ref, out_ref, sems):
        sources = (here_ref, there_ref)
        loads = begin([pltpu.make_async_copy(ref, piece_ref.at[at], sems.at[at]) for at, ref in enumerate(sources)])
        tabled = begin([pltpu.make_async_copy(table_hbm, table_ref, sems.at[2])])
        half, _ = place(half_blocks)
        group = lax.axis_index("dp")
        end(loads)
        for at in range(2):
            first = (group if at == 0 else 1 - group) * (lags // size)
            for side in range(sides):
                for k in range(lags // size):
                    piece = piece_ref[at, side, :, k * size : (k + 1) * size]
                    stage_ref[first + k, side * share : (side + 1) * share] = piece
        end(tabled)
        spectrum = dot(stage_ref[...].reshape(count * rows, size), table_ref[...]).reshape(count, rows, width)
        turn = jnp.where(half == 0, 1.0, -1.0).astype(jnp.float32)
        sign = alternating()[:1]
        sent = []
        for k in range(count):
            for strip in range(size // LANES):
                re = slice(2 * strip * LANES, (2 * strip + 1) * LANES)
                im = slice((2 * strip + 1) * LANES, (2 * strip + 2) * LANES)
                real, imag = spectrum[k, :, re], spectrum[k, :, im]
                if k > 0:
                    real, imag = real - sign * spectrum[k - 1, :, im], imag + sign * spectrum[k - 1, :, re]
                out_ref[k, :, re] = real.astype(jnp.bfloat16)
                out_ref[k, :, im] = (turn * imag).astype(jnp.bfloat16)
            sent += begin([pltpu.make_async_copy(out_ref.at[k], out_hbm.at[k], sems.at[3 + k])])
        end(sent)

    return call(
        kernel,
        "taps",
        (here, there, table),
        [jax.ShapeDtypeStruct((count, rows, width), jnp.bfloat16)],
        [
            pltpu.VMEM((2, sides, share, lags), jnp.bfloat16),
            pltpu.VMEM((size, width), jnp.bfloat16),
            pltpu.VMEM((count, rows, size), jnp.bfloat16),
            pltpu.VMEM((count, rows, width), jnp.bfloat16),
            pltpu.SemaphoreType.DMA((3 + count,)),
        ],
    )[0]


def add(total, term):
    return term if total is None else (total[0] + term[0], total[1] + term[1])


def times(a, b):
    return a[0] * b[0] - a[1] * b[1], a[0] * b[1] + a[1] * b[0]


def conj_times(a, b):
    return a[0] * b[0] + a[1] * b[1], a[0] * b[1] - a[1] * b[0]


def transform(stage_ref, table_ref, spec_ref):
    width = spec_ref.shape[-1]
    staged = stage_ref[...].reshape(-1, stage_ref.shape[-1])
    for strip in range(width // (2 * LANES)):
        columns = slice(2 * strip * LANES, 2 * (strip + 1) * LANES)
        spec_ref[..., columns] = dot(staged, table_ref[:, columns]).reshape(spec_ref.shape[:-1] + (2 * LANES,))


def stage_copies(source, base, stage_ref, sems, outer, half_blocks):
    count, _, size = stage_ref.shape
    tokens = source.shape[2]
    merge = size // tokens
    half, _ = place(half_blocks)
    copies = []
    for k in range(count):
        block = order(k, count, half, outer)
        for q in range(merge):
            target = stage_ref.at[k, :, pl.ds(q * tokens, tokens)]
            copies.append(pltpu.make_async_copy(source.at[base + block * merge + q], target, sems.at[k, q]))
    return copies


def stage_all(near_hbm, own_refs, slots, stage_ref, sems, half_blocks):
    _, count, _, size = stage_ref.shape
    tokens = near_hbm.shape[2]
    merge = size // tokens
    half, me = place(half_blocks)
    near = stage_copies(near_hbm, half * half_blocks, stage_ref.at[0], sems.at[0], True, half_blocks)
    far = stage_copies(near_hbm, (1 - half) * half_blocks, stage_ref.at[1], sems.at[1], False, half_blocks)
    own = []
    for group, ref in zip(slots, own_refs):
        for at, slot in enumerate(group):
            position = jnp.bitwise_xor(me, slot)
            k = order(position // merge, count, half, False)
            start = pl.multiple_of(lax.rem(position, merge) * tokens, tokens)
            target = stage_ref.at[2, k, :, pl.ds(start, tokens)]
            own.append(pltpu.make_async_copy(ref.at[at], target, sems.at[2, slot // merge, slot % merge]))
    return begin(near) + begin(far), begin(own)


def order(k, count, half, outer):
    return jnp.where(half == (0 if outer else 1), k, count - 1 - k)


def tile_loop(rows, body):
    @pl.loop(0, rows // SUBLANES)
    def _(tile):
        body(pl.multiple_of(tile * SUBLANES, SUBLANES))


def parts(ref, k, row, strip):
    return ref[k, row, real_of(strip)], ref[k, row, imag_of(strip)]


def keep(ref, k, row, strip, value):
    ref[k, row, real_of(strip)], ref[k, row, imag_of(strip)] = value


def give_back(prod_ref, table_ref, held_ref, out_ref, sems, outer, half_blocks):
    count, rows, width = prod_ref.shape
    merge, tokens = held_ref.shape[1], held_ref.shape[3]
    half, _ = place(half_blocks)
    sent = []
    spectrum = prod_ref[...].astype(jnp.bfloat16).reshape(count * rows, width)
    for q in range(merge):
        result = back(spectrum, table_ref[q * tokens : (q + 1) * tokens])
        held_ref[:, q] = result.astype(jnp.bfloat16).reshape(count, rows, tokens)
        for k in range(count):
            block = order(k, count, half, outer)
            sent += begin(
                [pltpu.make_async_copy(held_ref.at[k, q], out_ref.at[block * merge + q], sems.at[k, q])]
            )
    end(sent)


def results(near, own, filt, half_blocks, table):
    slots = [group for group, _ in own]
    _, rows, tokens = near.shape
    size, width = table.shape
    merge = size // tokens
    count = half_blocks // merge
    filters = filt.shape[1]

    def kernel(near_hbm, *refs):
        own_hbm, (filt_hbm, table_hbm, out_hbm) = refs[: len(own)], refs[len(own) : len(own) + 3]
        stage_ref, filt_in, filt_ref, table_ref, spec_ref, prod_ref, held_ref, sems, stage_sems, out_sems = refs[len(own) + 3 :]
        tabled = begin([pltpu.make_async_copy(table_hbm, table_ref, sems.at[0])])
        staged, later = stage_all(near_hbm, own_hbm, slots, stage_ref, stage_sems, half_blocks)
        rest = begin([pltpu.make_async_copy(filt_hbm, filt_in, sems.at[1])])
        end(staged)
        end(tabled)
        end(later)
        transform(stage_ref, table_ref, spec_ref)
        end(rest)
        filt_ref[...] = filt_in[...].astype(jnp.float32)

        def tile(first):
            row = pl.ds(first, SUBLANES)
            tap_row = pl.ds(pl.multiple_of(lax.rem(first, filters), SUBLANES), SUBLANES)
            for strip in range(size // LANES):
                taps = [parts(filt_ref, k, tap_row, strip) for k in range(2 * count)]
                near, far, own = ([parts(spec_ref.at[which], k, row, strip) for k in range(count)] for which in range(3))
                for out in range(count):
                    total = None
                    for k in range(out + 1):
                        total = add(total, times(taps[out - k], near[k]))
                    keep(prod_ref.at[0], out, row, strip, total)
                for out in range(count):
                    total = None
                    for k in range(out + 1):
                        total = add(total, conj_times(taps[out - k], own[k]))
                    for k in range(count):
                        total = add(total, conj_times(taps[count + out - k], far[k]))
                    keep(prod_ref.at[1], out, row, strip, total)

        tile_loop(rows, tile)
        half, _ = place(half_blocks)
        spectrum = prod_ref[...].astype(jnp.bfloat16).reshape(2 * count * rows, width)
        sent = []
        for q in range(merge):
            result = back(spectrum, table_ref[q * tokens : (q + 1) * tokens]).astype(jnp.bfloat16)
            held_ref[:, :, q] = result.reshape(2, count, rows, tokens)
            for which in range(2):
                for k in range(count):
                    position = order(k, count, half, which == 0) * merge + q
                    copy = pltpu.make_async_copy(
                        held_ref.at[which, k, q], out_hbm.at[position, which], out_sems.at[which, k, q]
                    )
                    sent += begin([copy])
        end(sent)

    return call(
        kernel,
        "results",
        (near, *[array for _, array in own], filt, table),
        [jax.ShapeDtypeStruct((half_blocks, 2, rows, tokens), jnp.bfloat16)],
        [
            pltpu.VMEM((3, count, rows, size), jnp.bfloat16),
            pltpu.VMEM((2 * count, filters, width), jnp.bfloat16),
            pltpu.VMEM((2 * count, filters, width), jnp.float32),
            pltpu.VMEM(table.shape, jnp.bfloat16),
            pltpu.VMEM((3, count, rows, width), jnp.float32),
            pltpu.VMEM((2, count, rows, width), jnp.float32),
            pltpu.VMEM((2, count, merge, rows, tokens), jnp.bfloat16),
            pltpu.SemaphoreType.DMA((2,)),
            pltpu.SemaphoreType.DMA((3, count, merge)),
            pltpu.SemaphoreType.DMA((2, count, merge)),
        ],
        weight=HEAVY,
    )[0]


def lag_products(near_ref, other_ref, row_at, strip, repeats, filters, totals):
    count = near_ref.shape[0]
    sums = [None] * len(totals)
    for repeat in range(repeats):
        row = pl.ds(pl.multiple_of(repeat * filters + row_at, SUBLANES), SUBLANES)
        near = [parts(near_ref, k, row, strip) for k in range(count)]
        other = [parts(other_ref, k, row, strip) for k in range(count)]
        for at, total in enumerate(totals):
            for a in range(count):
                if 0 <= total - a < count:
                    sums[at] = add(sums[at], conj_times(near[a], other[total - a]))
    return sums


def join_lags(ref, row, joint_ref, base):
    lags, size = ref.shape[0], ref.shape[2] // 2
    sign = alternating()[:1]
    for k in range(lags):
        for strip in range(size // LANES):
            real, imag = parts(ref, k, row, strip)
            if k + 1 < lags:
                next_real, next_imag = parts(ref, k + 1, row, strip)
                real, imag = real + sign * next_imag, imag - sign * next_real
            keep(joint_ref, base + k, slice(None), strip, (real.astype(jnp.bfloat16), imag.astype(jnp.bfloat16)))


def filter_terms(near, own, filters, half_blocks, table):
    slots = [group for group, _ in own]
    _, rows, tokens = near.shape
    size, width = table.shape
    merge = size // tokens
    count = half_blocks // merge
    kept, lags = filters // 2, count * size
    repeats = rows // filters

    def kernel(near_hbm, *refs):
        own_hbm, refs = refs[: len(own)], refs[len(own) :]
        table_hbm, give_hbm, mine_hbm, theirs_hbm, stage_ref, table_ref, spec_ref, local_ref, cross_ref, joint_ref, held_ref = refs[:11]
        give_ref, mine_ref, theirs_ref, sems, stage_sems = refs[11:]
        tabled = begin([pltpu.make_async_copy(table_hbm, table_ref, sems.at[0])])
        staged, later = stage_all(near_hbm, own_hbm, slots, stage_ref, stage_sems, half_blocks)
        half, _ = place(half_blocks)
        group = lax.axis_index("dp")
        turn = jnp.where(half == 0, 1.0, -1.0).astype(jnp.float32)
        end(tabled)
        end(staged)
        end(later)
        transform(stage_ref, table_ref, spec_ref)
        near_ref, far_ref, own_ref = (spec_ref.at[which] for which in range(3))

        def local_tile(first):
            for strip in range(size // LANES):
                sums = lag_products(near_ref, own_ref, first, strip, repeats, filters, [count - 1 - k for k in range(count)])
                for k, (real, imag) in enumerate(sums):
                    keep(local_ref, k, pl.ds(first, SUBLANES), strip, (real, turn * imag))

        tile_loop(filters, local_tile)
        mine = pl.multiple_of(half * kept, SUBLANES)
        other = pl.multiple_of((1 - half) * kept, SUBLANES)
        join_lags(local_ref, pl.ds(other, kept), joint_ref, 0)
        result = back(joint_ref[:count].reshape(count * kept, width), table_ref[...]).reshape(count, kept, size)
        for k in range(count):
            give_ref[:, k * size : (k + 1) * size] = result[k].astype(jnp.bfloat16)
        sent = begin([pltpu.make_async_copy(give_ref, give_hbm, sems.at[1])])

        def cross_tile(first):
            row = pl.ds(first, SUBLANES)
            at = pl.ds(pl.multiple_of(mine + first, SUBLANES), SUBLANES)
            for strip in range(size // LANES):
                totals = [2 * count - 1 - k for k in range(1, 2 * count)]
                sums = lag_products(near_ref, far_ref, mine + first, strip, repeats, filters, totals)
                keep(cross_ref, 0, row, strip, parts(local_ref, 0, at, strip))
                for k, (real, imag) in enumerate(sums, 1):
                    value = (real, turn * imag)
                    keep(cross_ref, k, row, strip, add(value, parts(local_ref, k, at, strip)) if k < count else value)

        tile_loop(kept, cross_tile)
        join_lags(cross_ref, slice(None), joint_ref, 0)
        result = back(joint_ref[...].reshape(2 * count * kept, width), table_ref[...])
        held_ref[...] = result.reshape(2, count, kept, size)
        for k in range(count):
            columns = slice(k * size, (k + 1) * size)
            mine_ref[:, columns] = held_ref[group, k]
            theirs_ref[:, columns] = held_ref[1 - group, k].astype(jnp.bfloat16)
        sent += begin(
            [
                pltpu.make_async_copy(theirs_ref, theirs_hbm, sems.at[2]),
                pltpu.make_async_copy(mine_ref, mine_hbm, sems.at[3]),
            ]
        )
        end(sent)

    return call(
        kernel,
        "filter_terms",
        (near, *[array for _, array in own], table),
        [
            jax.ShapeDtypeStruct((kept, lags), jnp.bfloat16),
            jax.ShapeDtypeStruct((kept, lags), jnp.float32),
            jax.ShapeDtypeStruct((kept, lags), jnp.bfloat16),
        ],
        [
            pltpu.VMEM((3, count, rows, size), jnp.bfloat16),
            pltpu.VMEM(table.shape, jnp.bfloat16),
            pltpu.VMEM((3, count, rows, width), jnp.float32),
            pltpu.VMEM((count, filters, width), jnp.float32),
            pltpu.VMEM((2 * count, kept, width), jnp.float32),
            pltpu.VMEM((2 * count, kept, width), jnp.bfloat16),
            pltpu.VMEM((2, count, kept, size), jnp.float32),
            pltpu.VMEM((kept, lags), jnp.bfloat16),
            pltpu.VMEM((kept, lags), jnp.float32),
            pltpu.VMEM((kept, lags), jnp.bfloat16),
            pltpu.SemaphoreType.DMA((4,)),
            pltpu.SemaphoreType.DMA((3, count, merge)),
        ],
    )


def body(pre_gate, values, post_gate, filters, cotangent):
    blocks = lax.axis_size("ctx")
    groups = lax.axis_size("dp")
    half_blocks = blocks // 2
    local_rows, tokens = pre_gate.shape
    local_filters = filters.shape[0]
    repeats = local_rows // (local_filters * blocks)
    rows = 2 * local_filters * repeats
    table = dft_table(2 * tokens)
    arrays = (pre_gate, values, post_gate, cotangent)
    sides = [list(range(half_blocks)), list(range(half_blocks, blocks))]

    def swap(array):
        return lax.ppermute(array, "ctx", [(i, i ^ half_blocks) for i in range(blocks)])

    def other_group(array):
        return lax.ppermute(array, "dp", [(0, 1), (1, 0)])

    near, even, odd, taps = gate(arrays, filters, repeats, half_blocks)
    here = pack_taps(taps, swap(taps), half_blocks)
    odd, here = lax.optimization_barrier((odd, here))
    near = lax.all_to_all(near.reshape(blocks, rows, tokens), "ctx", split_axis=0, concat_axis=0, tiled=True)
    shape = (half_blocks // 2, rows, tokens)
    own = exchange_own(even.reshape(shape), odd.reshape(shape), half_blocks)
    filt = transform_taps(here, other_group(here), half_blocks, groups, table)

    result = results(near, own, filt, half_blocks, table)
    result, near = lax.optimization_barrier((result, near))
    returned = lax.all_to_all(
        result, "ctx", split_axis=0, concat_axis=0, tiled=True, axis_index_groups=sides
    )
    give, mine, theirs = filter_terms(near, own, 2 * local_filters, half_blocks, table)
    given = swap(give)
    to_first = lax.ppermute(give, ("dp", "ctx"), [(blocks + i, i ^ half_blocks) for i in range(blocks)])
    first = jnp.where(lax.axis_index("dp") == 0, given.astype(jnp.float32), 0.0) + to_first.astype(jnp.float32)
    terms = (mine + first, other_group(theirs))
    mixed, pre_grad, value_grad, post_grad, filter_grad = finish(
        returned.reshape(half_blocks, 2, repeats, 2, local_filters, tokens), arrays, terms
    )
    return (mixed, pre_grad, value_grad, post_grad, filter_grad)


def matmul(left, right):
    return jnp.dot(left, right, precision=lax.Precision.HIGHEST, preferred_element_type=jnp.float32)


def contract(form, left, right):
    return jnp.einsum(
        form, left, right, precision=lax.Precision.HIGHEST, preferred_element_type=jnp.float32
    )


def phases(height, width, modulus):
    product = lax.broadcasted_iota(jnp.int32, (height, width), 0) * lax.broadcasted_iota(
        jnp.int32, (height, width), 1
    )
    return (product % modulus).astype(jnp.float32) * (2.0 * math.pi / modulus)


def build_tables(blocks, tokens):
    factor = 1
    for candidate in range(1, tokens + 1):
        if tokens % candidate == 0 and candidate * candidate <= tokens:
            factor = candidate
    second = tokens // factor
    rows = blocks + 1
    total = 2 * blocks * tokens
    first_angle = phases(rows, blocks, 2 * blocks)
    twist_angle = phases(rows, tokens, total)
    inner_angle = phases(factor, factor, factor)
    middle_angle = phases(factor, second, tokens)
    outer_angle = phases(second, second, second)
    back_angle = phases(blocks, rows, 2 * blocks)
    column = lax.broadcasted_iota(jnp.int32, (blocks, rows), 1)
    weight = jnp.where((column == 0) | (column == blocks), 1.0, 2.0).astype(jnp.float32) / total
    return {
        "first_cos": jnp.cos(first_angle),
        "first_nsin": -jnp.sin(first_angle),
        "twist_cos": jnp.cos(twist_angle),
        "twist_sin": jnp.sin(twist_angle),
        "inner_cos": jnp.cos(inner_angle),
        "inner_sin": jnp.sin(inner_angle),
        "middle_cos": jnp.cos(middle_angle),
        "middle_sin": jnp.sin(middle_angle),
        "outer_cos": jnp.cos(outer_angle),
        "outer_sin": jnp.sin(outer_angle),
        "back_cos": weight * jnp.cos(back_angle),
        "back_sin": weight * jnp.sin(back_angle),
    }


def expand(table, ndim):
    return table.reshape((table.shape[0],) + (1,) * (ndim - 2) + (table.shape[1],))


def block_table(cos_part, sin_part):
    return jnp.stack([jnp.stack([cos_part, sin_part]), jnp.stack([-sin_part, cos_part])])


def wave(real_part, imag_part, tables, sign):
    shape = real_part.shape
    factor = tables["inner_cos"].shape[0]
    second = tables["outer_cos"].shape[0]
    stacked = jnp.stack(
        [real_part.reshape(-1, factor, second), imag_part.reshape(-1, factor, second)]
    )
    inner_table = block_table(tables["inner_cos"], sign * tables["inner_sin"])
    middle = contract("prab,pqac->qrcb", stacked, inner_table)
    middle_cos = tables["middle_cos"]
    middle_sin = sign * tables["middle_sin"]
    real_turn = middle[0] * middle_cos - middle[1] * middle_sin
    imag_turn = middle[0] * middle_sin + middle[1] * middle_cos
    turned = jnp.stack([real_turn, imag_turn])
    outer_table = block_table(tables["outer_cos"], sign * tables["outer_sin"])
    result = contract("prcb,pqbd->qrdc", turned, outer_table)
    return (result[0].reshape(shape), result[1].reshape(shape))


def finish_forward(real_first, imag_first, tables):
    ndim = real_first.ndim
    twist_cos = expand(tables["twist_cos"], ndim)
    twist_sin = expand(tables["twist_sin"], ndim)
    real_twist = real_first * twist_cos + imag_first * twist_sin
    imag_twist = imag_first * twist_cos - real_first * twist_sin
    return wave(real_twist, imag_twist, tables, -1.0)


def spectrum(signal, tables):
    flat = signal.reshape(signal.shape[0], -1)
    shape = (tables["first_cos"].shape[0],) + signal.shape[1:]
    real_first = matmul(tables["first_cos"], flat).reshape(shape)
    imag_first = matmul(tables["first_nsin"], flat).reshape(shape)
    return finish_forward(real_first, imag_first, tables)


def inverse_prepare(real_spec, imag_spec, tables):
    ndim = real_spec.ndim
    real_wave, imag_wave = wave(real_spec, imag_spec, tables, 1.0)
    twist_cos = expand(tables["twist_cos"], ndim)
    twist_sin = expand(tables["twist_sin"], ndim)
    real_twist = real_wave * twist_cos - imag_wave * twist_sin
    imag_twist = real_wave * twist_sin + imag_wave * twist_cos
    rows = real_spec.shape[0]
    return (real_twist.reshape(rows, -1), imag_twist.reshape(rows, -1))


def inverse_full(real_spec, imag_spec, tables):
    real_flat, imag_flat = inverse_prepare(real_spec, imag_spec, tables)
    signal = matmul(tables["back_cos"], real_flat) - matmul(tables["back_sin"], imag_flat)
    return signal.reshape((tables["back_cos"].shape[0],) + real_spec.shape[1:])


def plain_body(pre_gate, values, post_gate, filters, cotangent):
    blocks = lax.axis_size("ctx")
    groups = lax.axis_size("dp")
    local_rows = pre_gate.shape[0]
    tokens = pre_gate.shape[1]
    local_filters = filters.shape[0]
    repeats = local_rows // (local_filters * blocks)
    share = blocks // groups
    tables = build_tables(blocks, tokens)
    gated = (pre_gate.astype(jnp.float32) * values.astype(jnp.float32)).astype(jnp.bfloat16)
    conv_grad = (cotangent.astype(jnp.float32) * post_gate.astype(jnp.float32)).astype(jnp.bfloat16)
    gated_blocks = gated.reshape(repeats, blocks, local_filters, tokens)
    grad_blocks = conv_grad.reshape(repeats, blocks, local_filters, tokens)
    tap_local = jnp.transpose(filters.reshape(local_filters, share, tokens), (1, 0, 2))
    piece = lax.all_gather(tap_local, "dp", axis=0, tiled=True)
    count = piece.shape[0]
    flat = piece.reshape(count, -1)
    cos_cols = tables["first_cos"]
    sin_cols = tables["first_nsin"]
    real_first = matmul(cos_cols, flat)
    imag_first = matmul(sin_cols, flat)
    spec_shape = (blocks + 1, 1, local_filters, tokens)
    filt_real, filt_imag = finish_forward(
        real_first.reshape(spec_shape), imag_first.reshape(spec_shape), tables
    )

    def single_spectrum(received):
        signal = received.reshape(blocks, -1, received.shape[2], received.shape[3])
        return spectrum(signal.astype(jnp.float32), tables)

    gated_real, gated_imag = single_spectrum(
        lax.all_to_all(gated_blocks, "ctx", split_axis=1, concat_axis=0, tiled=True)
    )
    prod_real = gated_real * filt_real - gated_imag * filt_imag
    prod_imag = gated_real * filt_imag + gated_imag * filt_real
    result = inverse_full(prod_real, prod_imag, tables).astype(jnp.bfloat16)
    conv_chan = result.reshape(blocks * repeats, 1, local_filters, tokens)
    conv_seq = lax.all_to_all(conv_chan, "ctx", split_axis=0, concat_axis=1, tiled=True)
    grad_real, grad_imag = single_spectrum(
        lax.all_to_all(grad_blocks, "ctx", split_axis=1, concat_axis=0, tiled=True)
    )
    prod_real = filt_real * grad_real + filt_imag * grad_imag
    prod_imag = filt_real * grad_imag - filt_imag * grad_real
    result = inverse_full(prod_real, prod_imag, tables).astype(jnp.bfloat16)
    gated_chan_grad = result.reshape(blocks * repeats, 1, local_filters, tokens)
    gated_seq_grad = lax.all_to_all(gated_chan_grad, "ctx", split_axis=0, concat_axis=1, tiled=True)
    cross_real = jnp.sum(gated_real * grad_real + gated_imag * grad_imag, axis=1)
    cross_imag = jnp.sum(gated_real * grad_imag - gated_imag * grad_real, axis=1)
    wave_real, wave_imag = inverse_prepare(cross_real, cross_imag, tables)
    cos_rows = tables["back_cos"]
    sin_rows = tables["back_sin"]
    term = matmul(cos_rows, wave_real) - matmul(sin_rows, wave_imag)
    summed = lax.psum_scatter(
        term.reshape(lax.axis_size("dp") * share, local_filters, tokens).astype(jnp.bfloat16),
        "dp",
        scatter_dimension=0,
        tiled=True,
    ).astype(jnp.float32)
    filter_grad = jnp.transpose(summed, (1, 0, 2)).reshape(local_filters, share * tokens)
    conv_full = conv_seq.reshape(pre_gate.shape).astype(jnp.float32)
    gated_grad = gated_seq_grad.reshape(pre_gate.shape).astype(jnp.float32)
    mixed = (post_gate.astype(jnp.float32) * conv_full).astype(jnp.bfloat16)
    post_grad = (cotangent.astype(jnp.float32) * conv_full).astype(jnp.bfloat16)
    pre_grad = (gated_grad * values.astype(jnp.float32)).astype(jnp.bfloat16)
    value_grad = (gated_grad * pre_gate.astype(jnp.float32)).astype(jnp.bfloat16)
    return (mixed, pre_grad, value_grad, post_grad, filter_grad)


def solution(mesh):
    placed = (P("dp", "ctx"), P("dp", "ctx"), P("dp", "ctx"), P("ctx", "dp"), P("dp", "ctx"))
    groups, blocks = mesh.shape["dp"], mesh.shape["ctx"]

    def program(pre_gate, values, post_gate, filters, cotangent):
        kernels = groups == 2 and blocks >= 8 and blocks & (blocks - 1) == 0 and filters.shape[0] % 16 == 0
        return (body if kernels else plain_body)(pre_gate, values, post_gate, filters, cotangent)

    return jax.shard_map(
        program,
        mesh=mesh,
        in_specs=placed,
        out_specs=(P("dp", "ctx"), P("dp", "ctx"), P("dp", "ctx"), P("dp", "ctx"), P("ctx", "dp")),
        check_vma=False,
    )
```

```python
import math

import jax
import jax.numpy as jnp
import numpy as np
from jax import lax
from jax.experimental import pallas as pl
from jax.experimental.pallas import tpu as pltpu
from jax.sharding import PartitionSpec as P


LANES = 128
SUBLANES = 8
VMEM_BYTES = 60 * 1024 * 1024
HEAVY = 1 << 37


def dft_table(size):
    angle = np.arange(size)[:, None] * (2.0 * np.arange(size)[None, :] + 1.0) * (math.pi / (2 * size))
    strips = size // LANES
    cos, sin = (part.reshape(size, strips, 1, LANES) for part in (np.cos(angle), np.sin(angle)))
    return jnp.asarray(np.concatenate([cos, -sin], axis=2).reshape(size, 2 * size), jnp.bfloat16)


def dot(left, right):
    return jnp.dot(left, right, preferred_element_type=jnp.float32)


def back(spectrum, table):
    result = lax.dot_general(spectrum, table, (((1,), (1,)), ((), ())), preferred_element_type=jnp.float32)
    return result * (2.0 / table.shape[1])


def alternating():
    odd = lax.broadcasted_iota(jnp.int32, (SUBLANES, LANES), 1) % 2
    return 1.0 - 2.0 * odd.astype(jnp.float32)


def place(half_blocks):
    index = lax.axis_index("ctx")
    return index // half_blocks, lax.rem(index, half_blocks)


def real_of(strip):
    return pl.ds(2 * strip * LANES, LANES)


def imag_of(strip):
    return pl.ds((2 * strip + 1) * LANES, LANES)


def begin(copies):
    for copy in copies:
        copy.start()
    return copies


def end(copies):
    for copy in copies:
        copy.wait()


def call(kernel, name, operands, outputs, scratch, weight=1, vmem=VMEM_BYTES):
    hbm = pl.BlockSpec(memory_space=pltpu.HBM)
    return pl.pallas_call(
        kernel,
        in_specs=[hbm] * len(operands),
        out_specs=[hbm] * len(outputs),
        out_shape=outputs,
        scratch_shapes=scratch,
        compiler_params=pltpu.CompilerParams(vmem_limit_bytes=vmem),
        cost_estimate=pl.CostEstimate(flops=weight, bytes_accessed=weight, transcendentals=0),
        name=name,
    )(*operands)


def gate(arrays, filters, repeats, half_blocks):
    rows_all, tokens = arrays[0].shape
    rows = rows_all // repeats
    share = rows // (2 * half_blocks)
    piece = (repeats, 2, share, tokens)

    def kernel(pre_ref, value_ref, post_ref, cot_ref, filt_ref, out_ref, even_ref, odd_ref, taps_ref, in_ref, result_ref, filt_in, taps_out, in_sems, out_sems, own_sems, taps_sems):
        half, me = place(half_blocks)
        sources = (pre_ref, value_ref, cot_ref, post_ref)

        def fetch(r):
            at = pl.ds(r * rows, rows)
            return [
                pltpu.make_async_copy(ref.at[at], in_ref.at[which, r], in_sems.at[which, r])
                for which, ref in enumerate(sources)
            ]

        for r in range(repeats):
            begin(fetch(r))
        loaded = begin([pltpu.make_async_copy(filt_ref, filt_in, taps_sems.at[0])])
        sent = []
        for r in range(repeats):
            end(fetch(r))
            for which in range(2):
                product = in_ref[2 * which, r].astype(jnp.float32) * in_ref[2 * which + 1, r].astype(jnp.float32)
                product = product.astype(jnp.bfloat16).reshape(2, half_blocks, share, tokens)
                at = half if which == 0 else 1 - half
                for side in range(2):
                    result_ref[at, :, r, side] = product[side]
            for to in range(2):
                copy = pltpu.make_async_copy(result_ref.at[0, :, r], out_ref.at[to, :, r], out_sems.at[to, r])
                sent += begin([copy])
        for at in range(half_blocks // 2):
            for odd, target in enumerate((even_ref, odd_ref)):
                source = result_ref.at[1, jnp.bitwise_xor(me, 2 * at + odd)]
                sent += begin([pltpu.make_async_copy(source, target.at[at], own_sems.at[odd, at])])
        end(loaded)
        taps_out[...] = filt_in[...].astype(jnp.bfloat16)
        sent += begin([pltpu.make_async_copy(taps_out, taps_ref, taps_sems.at[1])])
        end(sent)

    own_shape = jax.ShapeDtypeStruct((half_blocks // 2, *piece), jnp.bfloat16)
    return call(
        kernel,
        "gate",
        (*arrays, filters),
        [
            jax.ShapeDtypeStruct((2, half_blocks, *piece), jnp.bfloat16),
            own_shape,
            own_shape,
            jax.ShapeDtypeStruct(filters.shape, jnp.bfloat16),
        ],
        [
            pltpu.VMEM((4, repeats, rows, tokens), jnp.bfloat16),
            pltpu.VMEM((2, half_blocks, *piece), jnp.bfloat16),
            pltpu.VMEM(filters.shape, filters.dtype),
            pltpu.VMEM(filters.shape, jnp.bfloat16),
            pltpu.SemaphoreType.DMA((4, repeats)),
            pltpu.SemaphoreType.DMA((2, repeats)),
            pltpu.SemaphoreType.DMA((2, half_blocks // 2)),
            pltpu.SemaphoreType.DMA((2,)),
        ],
    )


def exchange_own(even, odd, half_blocks):
    def swap(array, slot):
        return lax.ppermute(array, "ctx", [(i, i ^ slot) for i in range(2 * half_blocks)])

    odd = swap(odd, 1)
    groups = [([0], even[:1]), ([1], odd[:1])]
    for at in range(1, half_blocks // 2):
        pair = jnp.concatenate([even[at : at + 1], odd[at : at + 1]])
        groups.append(([2 * at, 2 * at + 1], swap(pair, 2 * at)))
    return groups


def finish(returned, arrays):
    half_blocks, _, repeats, sides, share, tokens = returned.shape
    count, rows = repeats * sides, half_blocks * share

    def kernel(recv_ref, pre_ref, value_ref, post_ref, cot_ref, *refs):
        out_refs, (held_ref, sems) = refs[:4], refs[4:]
        half, _ = place(half_blocks)
        sent = []
        for part in range(count):
            r, side = part // sides, part % sides
            at = pl.ds(part * rows, rows)
            conv = recv_ref[:, half, r, side].reshape(rows, tokens).astype(jnp.float32)
            grad = recv_ref[:, 1 - half, r, side].reshape(rows, tokens).astype(jnp.float32)
            for which, (factor_ref, result) in enumerate(
                ((post_ref, conv), (value_ref, grad), (pre_ref, grad), (cot_ref, conv))
            ):
                held_ref[which, part] = (factor_ref[at].astype(jnp.float32) * result).astype(jnp.bfloat16)
                sent += begin(
                    [pltpu.make_async_copy(held_ref.at[which, part], out_refs[which].at[at], sems.at[which, part])]
                )
        end(sent)

    shapes = [jax.ShapeDtypeStruct(arrays[0].shape, jnp.bfloat16)] * 4
    return pl.pallas_call(
        kernel,
        in_specs=[pl.BlockSpec(memory_space=pltpu.VMEM)] * 5,
        out_specs=[pl.BlockSpec(memory_space=pltpu.HBM)] * 4,
        out_shape=shapes,
        scratch_shapes=[
            pltpu.VMEM((4, count, rows, tokens), jnp.bfloat16),
            pltpu.SemaphoreType.DMA((4, count)),
        ],
        compiler_params=pltpu.CompilerParams(vmem_limit_bytes=VMEM_BYTES // 6),
        name="finish",
    )(returned, *arrays)


def pack_taps(taps, pair, half_blocks):
    share, lags = taps.shape

    def kernel(taps_ref, pair_ref, out_ref, held_ref, sems):
        half, _ = place(half_blocks)
        end(
            begin(
                [
                    pltpu.make_async_copy(taps_ref, held_ref.at[half], sems.at[0]),
                    pltpu.make_async_copy(pair_ref, held_ref.at[1 - half], sems.at[1]),
                ]
            )
        )
        end(begin([pltpu.make_async_copy(held_ref, out_ref, sems.at[2])]))

    return call(
        kernel,
        "pack_taps",
        (taps, pair),
        [jax.ShapeDtypeStruct((2, share, lags), jnp.bfloat16)],
        [pltpu.VMEM((2, share, lags), jnp.bfloat16), pltpu.SemaphoreType.DMA((3,))],
        weight=HEAVY,
    )[0]


def transform_taps(here, there, half_blocks, groups, table):
    sides, share, lags = here.shape
    size = table.shape[0]
    count = groups * lags // size
    rows, width = sides * share, 2 * size

    def kernel(here_ref, there_ref, table_hbm, out_hbm, piece_ref, table_ref, stage_ref, out_ref, sems):
        sources = (here_ref, there_ref)
        loads = begin([pltpu.make_async_copy(ref, piece_ref.at[at], sems.at[at]) for at, ref in enumerate(sources)])
        tabled = begin([pltpu.make_async_copy(table_hbm, table_ref, sems.at[2])])
        half, _ = place(half_blocks)
        group = lax.axis_index("dp")
        end(loads)
        for at in range(2):
            first = (group if at == 0 else 1 - group) * (lags // size)
            for side in range(sides):
                for k in range(lags // size):
                    piece = piece_ref[at, side, :, k * size : (k + 1) * size]
                    stage_ref[first + k, side * share : (side + 1) * share] = piece
        end(tabled)
        spectrum = dot(stage_ref[...].reshape(count * rows, size), table_ref[...]).reshape(count, rows, width)
        turn = jnp.where(half == 0, 1.0, -1.0).astype(jnp.float32)
        sign = alternating()[:1]
        sent = []
        for k in range(count):
            for strip in range(size // LANES):
                re = slice(2 * strip * LANES, (2 * strip + 1) * LANES)
                im = slice((2 * strip + 1) * LANES, (2 * strip + 2) * LANES)
                real, imag = spectrum[k, :, re], spectrum[k, :, im]
                if k > 0:
                    real, imag = real - sign * spectrum[k - 1, :, im], imag + sign * spectrum[k - 1, :, re]
                out_ref[k, :, re] = real.astype(jnp.bfloat16)
                out_ref[k, :, im] = (turn * imag).astype(jnp.bfloat16)
            sent += begin([pltpu.make_async_copy(out_ref.at[k], out_hbm.at[k], sems.at[3 + k])])
        end(sent)

    return call(
        kernel,
        "taps",
        (here, there, table),
        [jax.ShapeDtypeStruct((count, rows, width), jnp.bfloat16)],
        [
            pltpu.VMEM((2, sides, share, lags), jnp.bfloat16),
            pltpu.VMEM((size, width), jnp.bfloat16),
            pltpu.VMEM((count, rows, size), jnp.bfloat16),
            pltpu.VMEM((count, rows, width), jnp.bfloat16),
            pltpu.SemaphoreType.DMA((3 + count,)),
        ],
    )[0]


def add(total, term):
    return term if total is None else (total[0] + term[0], total[1] + term[1])


def times(a, b):
    return a[0] * b[0] - a[1] * b[1], a[0] * b[1] + a[1] * b[0]


def conj_times(a, b):
    return a[0] * b[0] + a[1] * b[1], a[0] * b[1] - a[1] * b[0]


def transform(stage_ref, table_ref, spec_ref):
    width = spec_ref.shape[-1]
    staged = stage_ref[...].reshape(-1, stage_ref.shape[-1])
    for strip in range(width // (2 * LANES)):
        columns = slice(2 * strip * LANES, 2 * (strip + 1) * LANES)
        spec_ref[..., columns] = dot(staged, table_ref[:, columns]).reshape(spec_ref.shape[:-1] + (2 * LANES,))


def stage_copies(source, base, stage_ref, sems, outer, half_blocks):
    count, _, size = stage_ref.shape
    tokens = source.shape[2]
    merge = size // tokens
    half, _ = place(half_blocks)
    copies = []
    for k in range(count):
        block = order(k, count, half, outer)
        for q in range(merge):
            target = stage_ref.at[k, :, pl.ds(q * tokens, tokens)]
            copies.append(pltpu.make_async_copy(source.at[base + block * merge + q], target, sems.at[k, q]))
    return copies


def stage_all(near_hbm, own_refs, slots, stage_ref, sems, half_blocks):
    _, count, _, size = stage_ref.shape
    tokens = near_hbm.shape[2]
    merge = size // tokens
    half, me = place(half_blocks)
    near = stage_copies(near_hbm, half * half_blocks, stage_ref.at[0], sems.at[0], True, half_blocks)
    far = stage_copies(near_hbm, (1 - half) * half_blocks, stage_ref.at[1], sems.at[1], False, half_blocks)
    own = []
    for group, ref in zip(slots, own_refs):
        for at, slot in enumerate(group):
            position = jnp.bitwise_xor(me, slot)
            k = order(position // merge, count, half, False)
            start = pl.multiple_of(lax.rem(position, merge) * tokens, tokens)
            target = stage_ref.at[2, k, :, pl.ds(start, tokens)]
            own.append(pltpu.make_async_copy(ref.at[at], target, sems.at[2, slot // merge, slot % merge]))
    return begin(near) + begin(far), begin(own)


def order(k, count, half, outer):
    return jnp.where(half == (0 if outer else 1), k, count - 1 - k)


def tile_loop(rows, body):
    @pl.loop(0, rows // SUBLANES)
    def _(tile):
        body(pl.multiple_of(tile * SUBLANES, SUBLANES))


def parts(ref, k, row, strip):
    return ref[k, row, real_of(strip)], ref[k, row, imag_of(strip)]


def keep(ref, k, row, strip, value):
    ref[k, row, real_of(strip)], ref[k, row, imag_of(strip)] = value


def give_back(prod_ref, table_ref, held_ref, out_ref, sems, outer, half_blocks):
    count, rows, width = prod_ref.shape
    merge, tokens = held_ref.shape[1], held_ref.shape[3]
    half, _ = place(half_blocks)
    sent = []
    spectrum = prod_ref[...].astype(jnp.bfloat16).reshape(count * rows, width)
    for q in range(merge):
        result = back(spectrum, table_ref[q * tokens : (q + 1) * tokens])
        held_ref[:, q] = result.astype(jnp.bfloat16).reshape(count, rows, tokens)
        for k in range(count):
            block = order(k, count, half, outer)
            sent += begin(
                [pltpu.make_async_copy(held_ref.at[k, q], out_ref.at[block * merge + q], sems.at[k, q])]
            )
    end(sent)


def results(near, own, filt, half_blocks, table):
    slots = [group for group, _ in own]
    _, rows, tokens = near.shape
    size, width = table.shape
    merge = size // tokens
    count = half_blocks // merge
    filters = filt.shape[1]

    def kernel(near_hbm, *refs):
        own_hbm, (filt_hbm, table_hbm, out_hbm) = refs[: len(own)], refs[len(own) : len(own) + 3]
        stage_ref, filt_in, filt_ref, table_ref, spec_ref, prod_ref, held_ref, sems, stage_sems, out_sems = refs[len(own) + 3 :]
        tabled = begin([pltpu.make_async_copy(table_hbm, table_ref, sems.at[0])])
        staged, later = stage_all(near_hbm, own_hbm, slots, stage_ref, stage_sems, half_blocks)
        rest = begin([pltpu.make_async_copy(filt_hbm, filt_in, sems.at[1])])
        end(staged)
        end(tabled)
        end(later)
        transform(stage_ref, table_ref, spec_ref)
        end(rest)
        filt_ref[...] = filt_in[...].astype(jnp.float32)

        def tile(first):
            row = pl.ds(first, SUBLANES)
            tap_row = pl.ds(pl.multiple_of(lax.rem(first, filters), SUBLANES), SUBLANES)
            for strip in range(size // LANES):
                taps = [parts(filt_ref, k, tap_row, strip) for k in range(2 * count)]
                near, far, own = ([parts(spec_ref.at[which], k, row, strip) for k in range(count)] for which in range(3))
                for out in range(count):
                    total = None
                    for k in range(out + 1):
                        total = add(total, times(taps[out - k], near[k]))
                    keep(prod_ref.at[0], out, row, strip, total)
                for out in range(count):
                    total = None
                    for k in range(out + 1):
                        total = add(total, conj_times(taps[out - k], own[k]))
                    for k in range(count):
                        total = add(total, conj_times(taps[count + out - k], far[k]))
                    keep(prod_ref.at[1], out, row, strip, total)

        tile_loop(rows, tile)
        half, _ = place(half_blocks)
        spectrum = prod_ref[...].astype(jnp.bfloat16).reshape(2 * count * rows, width)
        sent = []
        for q in range(merge):
            result = back(spectrum, table_ref[q * tokens : (q + 1) * tokens]).astype(jnp.bfloat16)
            held_ref[:, :, q] = result.reshape(2, count, rows, tokens)
            for which in range(2):
                for k in range(count):
                    position = order(k, count, half, which == 0) * merge + q
                    copy = pltpu.make_async_copy(
                        held_ref.at[which, k, q], out_hbm.at[position, which], out_sems.at[which, k, q]
                    )
                    sent += begin([copy])
        end(sent)

    return call(
        kernel,
        "results",
        (near, *[array for _, array in own], filt, table),
        [jax.ShapeDtypeStruct((half_blocks, 2, rows, tokens), jnp.bfloat16)],
        [
            pltpu.VMEM((3, count, rows, size), jnp.bfloat16),
            pltpu.VMEM((2 * count, filters, width), jnp.bfloat16),
            pltpu.VMEM((2 * count, filters, width), jnp.float32),
            pltpu.VMEM(table.shape, jnp.bfloat16),
            pltpu.VMEM((3, count, rows, width), jnp.float32),
            pltpu.VMEM((2, count, rows, width), jnp.float32),
            pltpu.VMEM((2, count, merge, rows, tokens), jnp.bfloat16),
            pltpu.SemaphoreType.DMA((2,)),
            pltpu.SemaphoreType.DMA((3, count, merge)),
            pltpu.SemaphoreType.DMA((2, count, merge)),
        ],
        vmem=VMEM_BYTES // 2,
        weight=HEAVY,
    )[0]


def lag_products(near_ref, other_ref, row_at, strip, repeats, filters, totals):
    count = near_ref.shape[0]
    sums = [None] * len(totals)
    for repeat in range(repeats):
        row = pl.ds(pl.multiple_of(repeat * filters + row_at, SUBLANES), SUBLANES)
        near = [parts(near_ref, k, row, strip) for k in range(count)]
        other = [parts(other_ref, k, row, strip) for k in range(count)]
        for at, total in enumerate(totals):
            for a in range(count):
                if 0 <= total - a < count:
                    sums[at] = add(sums[at], conj_times(near[a], other[total - a]))
    return sums


def join_lags(ref, row, joint_ref, base):
    lags, size = ref.shape[0], ref.shape[2] // 2
    sign = alternating()[:1]
    for k in range(lags):
        for strip in range(size // LANES):
            real, imag = parts(ref, k, row, strip)
            if k + 1 < lags:
                next_real, next_imag = parts(ref, k + 1, row, strip)
                real, imag = real + sign * next_imag, imag - sign * next_real
            keep(joint_ref, base + k, slice(None), strip, (real.astype(jnp.bfloat16), imag.astype(jnp.bfloat16)))


def filter_terms(near, own, filters, half_blocks, table):
    slots = [group for group, _ in own]
    _, rows, tokens = near.shape
    size, width = table.shape
    merge = size // tokens
    count = half_blocks // merge
    kept, lags = filters // 2, count * size
    repeats = rows // filters

    def kernel(near_hbm, *refs):
        own_hbm, refs = refs[: len(own)], refs[len(own) :]
        table_hbm, give_hbm, mine_hbm, upper_hbm, lower_hbm, stage_ref, table_ref, spec_ref, local_ref, cross_ref, joint_ref = refs[:11]
        held_ref, give_ref, mine_ref, theirs_ref, sems, stage_sems = refs[11:]
        tabled = begin([pltpu.make_async_copy(table_hbm, table_ref, sems.at[0])])
        staged, later = stage_all(near_hbm, own_hbm, slots, stage_ref, stage_sems, half_blocks)
        half, _ = place(half_blocks)
        group = lax.axis_index("dp")
        turn = jnp.where(half == 0, 1.0, -1.0).astype(jnp.float32)
        end(tabled)
        end(staged)
        end(later)
        transform(stage_ref, table_ref, spec_ref)
        near_ref, far_ref, own_ref = (spec_ref.at[which] for which in range(3))

        def local_tile(first):
            for strip in range(size // LANES):
                sums = lag_products(near_ref, own_ref, first, strip, repeats, filters, [count - 1 - k for k in range(count)])
                for k, (real, imag) in enumerate(sums):
                    keep(local_ref, k, pl.ds(first, SUBLANES), strip, (real, turn * imag))

        tile_loop(filters, local_tile)
        mine = pl.multiple_of(half * kept, SUBLANES)
        other = pl.multiple_of((1 - half) * kept, SUBLANES)
        join_lags(local_ref, pl.ds(other, kept), joint_ref, 0)
        result = back(joint_ref[:count].reshape(count * kept, width), table_ref[...]).reshape(count, kept, size)
        for k in range(count):
            give_ref[:, k * size : (k + 1) * size] = result[k].astype(jnp.bfloat16)
        sent = begin([pltpu.make_async_copy(give_ref, give_hbm, sems.at[1])])

        def cross_tile(first):
            row = pl.ds(first, SUBLANES)
            at = pl.ds(pl.multiple_of(mine + first, SUBLANES), SUBLANES)
            for strip in range(size // LANES):
                totals = [2 * count - 1 - k for k in range(1, 2 * count)]
                sums = lag_products(near_ref, far_ref, mine + first, strip, repeats, filters, totals)
                keep(cross_ref, 0, row, strip, parts(local_ref, 0, at, strip))
                for k, (real, imag) in enumerate(sums, 1):
                    value = (real, turn * imag)
                    keep(cross_ref, k, row, strip, add(value, parts(local_ref, k, at, strip)) if k < count else value)

        tile_loop(kept, cross_tile)
        join_lags(cross_ref, slice(None), joint_ref, 0)
        result = back(joint_ref[...].reshape(2 * count * kept, width), table_ref[...])
        held_ref[...] = result.reshape(2, count, kept, size)
        for k in range(count):
            columns = slice(k * size, (k + 1) * size)
            mine_ref[:, columns] = held_ref[group, k]
            theirs_ref[:, columns] = held_ref[1 - group, k].astype(jnp.bfloat16)
        sent += begin(
            [
                pltpu.make_async_copy(theirs_ref.at[pl.ds(0, kept // 2)], upper_hbm, sems.at[2]),
                pltpu.make_async_copy(theirs_ref.at[pl.ds(kept // 2, kept // 2)], lower_hbm, sems.at[3]),
                pltpu.make_async_copy(mine_ref, mine_hbm, sems.at[4]),
            ]
        )
        end(sent)

    return call(
        kernel,
        "filter_terms",
        (near, *[array for _, array in own], table),
        [
            jax.ShapeDtypeStruct((kept, lags), jnp.bfloat16),
            jax.ShapeDtypeStruct((kept, lags), jnp.float32),
            jax.ShapeDtypeStruct((kept // 2, lags), jnp.bfloat16),
            jax.ShapeDtypeStruct((kept // 2, lags), jnp.bfloat16),
        ],
        [
            pltpu.VMEM((3, count, rows, size), jnp.bfloat16),
            pltpu.VMEM(table.shape, jnp.bfloat16),
            pltpu.VMEM((3, count, rows, width), jnp.float32),
            pltpu.VMEM((count, filters, width), jnp.float32),
            pltpu.VMEM((2 * count, kept, width), jnp.float32),
            pltpu.VMEM((2 * count, kept, width), jnp.bfloat16),
            pltpu.VMEM((2, count, kept, size), jnp.float32),
            pltpu.VMEM((kept, lags), jnp.bfloat16),
            pltpu.VMEM((kept, lags), jnp.float32),
            pltpu.VMEM((kept, lags), jnp.bfloat16),
            pltpu.SemaphoreType.DMA((5,)),
            pltpu.SemaphoreType.DMA((3, count, merge)),
        ],
    )


def body(pre_gate, values, post_gate, filters, cotangent):
    blocks = lax.axis_size("ctx")
    groups = lax.axis_size("dp")
    half_blocks = blocks // 2
    local_rows, tokens = pre_gate.shape
    local_filters = filters.shape[0]
    repeats = local_rows // (local_filters * blocks)
    rows = 2 * local_filters * repeats
    table = dft_table(2 * tokens)
    arrays = (pre_gate, values, post_gate, cotangent)
    sides = [list(range(half_blocks)), list(range(half_blocks, blocks))]

    def swap(array):
        return lax.ppermute(array, "ctx", [(i, i ^ half_blocks) for i in range(blocks)])

    def other_group(array):
        return lax.ppermute(array, "dp", [(0, 1), (1, 0)])

    near, even, odd, taps = gate(arrays, filters, repeats, half_blocks)
    here = pack_taps(taps, swap(taps), half_blocks)
    odd, here = lax.optimization_barrier((odd, here))
    near = lax.all_to_all(near.reshape(blocks, rows, tokens), "ctx", split_axis=0, concat_axis=0, tiled=True)
    shape = (half_blocks // 2, rows, tokens)
    own = exchange_own(even.reshape(shape), odd.reshape(shape), half_blocks)
    filt = transform_taps(here, other_group(here), half_blocks, groups, table)

    result = results(near, own, filt, half_blocks, table)
    result, near = lax.optimization_barrier((result, near))
    returned = lax.all_to_all(
        result, "ctx", split_axis=0, concat_axis=0, tiled=True, axis_index_groups=sides
    )
    give, mine, upper, lower = filter_terms(near, own, 2 * local_filters, half_blocks, table)
    to_first = [(blocks + i, i ^ half_blocks) for i in range(blocks)]
    halves = (swap(give), lax.ppermute(give, ("dp", "ctx"), to_first))
    theirs = jnp.concatenate([other_group(upper), other_group(lower)])
    outputs = finish(returned.reshape(half_blocks, 2, repeats, 2, local_filters, tokens), arrays)
    mine, mixed, pre_grad, value_grad, post_grad = lax.optimization_barrier((mine, *outputs))
    first = jnp.where(lax.axis_index("dp") == 0, 1.0, 0.0)
    filter_grad = mine + theirs.astype(jnp.float32) + first * (halves[0].astype(jnp.float32) + halves[1].astype(jnp.float32))
    return (mixed, pre_grad, value_grad, post_grad, filter_grad)


def matmul(left, right):
    return jnp.dot(left, right, precision=lax.Precision.HIGHEST, preferred_element_type=jnp.float32)


def contract(form, left, right):
    return jnp.einsum(
        form, left, right, precision=lax.Precision.HIGHEST, preferred_element_type=jnp.float32
    )


def phases(height, width, modulus):
    product = lax.broadcasted_iota(jnp.int32, (height, width), 0) * lax.broadcasted_iota(
        jnp.int32, (height, width), 1
    )
    return (product % modulus).astype(jnp.float32) * (2.0 * math.pi / modulus)


def build_tables(blocks, tokens):
    factor = 1
    for candidate in range(1, tokens + 1):
        if tokens % candidate == 0 and candidate * candidate <= tokens:
            factor = candidate
    second = tokens // factor
    rows = blocks + 1
    total = 2 * blocks * tokens
    first_angle = phases(rows, blocks, 2 * blocks)
    twist_angle = phases(rows, tokens, total)
    inner_angle = phases(factor, factor, factor)
    middle_angle = phases(factor, second, tokens)
    outer_angle = phases(second, second, second)
    back_angle = phases(blocks, rows, 2 * blocks)
    column = lax.broadcasted_iota(jnp.int32, (blocks, rows), 1)
    weight = jnp.where((column == 0) | (column == blocks), 1.0, 2.0).astype(jnp.float32) / total
    return {
        "first_cos": jnp.cos(first_angle),
        "first_nsin": -jnp.sin(first_angle),
        "twist_cos": jnp.cos(twist_angle),
        "twist_sin": jnp.sin(twist_angle),
        "inner_cos": jnp.cos(inner_angle),
        "inner_sin": jnp.sin(inner_angle),
        "middle_cos": jnp.cos(middle_angle),
        "middle_sin": jnp.sin(middle_angle),
        "outer_cos": jnp.cos(outer_angle),
        "outer_sin": jnp.sin(outer_angle),
        "back_cos": weight * jnp.cos(back_angle),
        "back_sin": weight * jnp.sin(back_angle),
    }


def expand(table, ndim):
    return table.reshape((table.shape[0],) + (1,) * (ndim - 2) + (table.shape[1],))


def block_table(cos_part, sin_part):
    return jnp.stack([jnp.stack([cos_part, sin_part]), jnp.stack([-sin_part, cos_part])])


def wave(real_part, imag_part, tables, sign):
    shape = real_part.shape
    factor = tables["inner_cos"].shape[0]
    second = tables["outer_cos"].shape[0]
    stacked = jnp.stack(
        [real_part.reshape(-1, factor, second), imag_part.reshape(-1, factor, second)]
    )
    inner_table = block_table(tables["inner_cos"], sign * tables["inner_sin"])
    middle = contract("prab,pqac->qrcb", stacked, inner_table)
    middle_cos = tables["middle_cos"]
    middle_sin = sign * tables["middle_sin"]
    real_turn = middle[0] * middle_cos - middle[1] * middle_sin
    imag_turn = middle[0] * middle_sin + middle[1] * middle_cos
    turned = jnp.stack([real_turn, imag_turn])
    outer_table = block_table(tables["outer_cos"], sign * tables["outer_sin"])
    result = contract("prcb,pqbd->qrdc", turned, outer_table)
    return (result[0].reshape(shape), result[1].reshape(shape))


def finish_forward(real_first, imag_first, tables):
    ndim = real_first.ndim
    twist_cos = expand(tables["twist_cos"], ndim)
    twist_sin = expand(tables["twist_sin"], ndim)
    real_twist = real_first * twist_cos + imag_first * twist_sin
    imag_twist = imag_first * twist_cos - real_first * twist_sin
    return wave(real_twist, imag_twist, tables, -1.0)


def spectrum(signal, tables):
    flat = signal.reshape(signal.shape[0], -1)
    shape = (tables["first_cos"].shape[0],) + signal.shape[1:]
    real_first = matmul(tables["first_cos"], flat).reshape(shape)
    imag_first = matmul(tables["first_nsin"], flat).reshape(shape)
    return finish_forward(real_first, imag_first, tables)


def inverse_prepare(real_spec, imag_spec, tables):
    ndim = real_spec.ndim
    real_wave, imag_wave = wave(real_spec, imag_spec, tables, 1.0)
    twist_cos = expand(tables["twist_cos"], ndim)
    twist_sin = expand(tables["twist_sin"], ndim)
    real_twist = real_wave * twist_cos - imag_wave * twist_sin
    imag_twist = real_wave * twist_sin + imag_wave * twist_cos
    rows = real_spec.shape[0]
    return (real_twist.reshape(rows, -1), imag_twist.reshape(rows, -1))


def inverse_full(real_spec, imag_spec, tables):
    real_flat, imag_flat = inverse_prepare(real_spec, imag_spec, tables)
    signal = matmul(tables["back_cos"], real_flat) - matmul(tables["back_sin"], imag_flat)
    return signal.reshape((tables["back_cos"].shape[0],) + real_spec.shape[1:])


def plain_body(pre_gate, values, post_gate, filters, cotangent):
    blocks = lax.axis_size("ctx")
    groups = lax.axis_size("dp")
    local_rows = pre_gate.shape[0]
    tokens = pre_gate.shape[1]
    local_filters = filters.shape[0]
    repeats = local_rows // (local_filters * blocks)
    share = blocks // groups
    tables = build_tables(blocks, tokens)
    gated = (pre_gate.astype(jnp.float32) * values.astype(jnp.float32)).astype(jnp.bfloat16)
    conv_grad = (cotangent.astype(jnp.float32) * post_gate.astype(jnp.float32)).astype(jnp.bfloat16)
    gated_blocks = gated.reshape(repeats, blocks, local_filters, tokens)
    grad_blocks = conv_grad.reshape(repeats, blocks, local_filters, tokens)
    tap_local = jnp.transpose(filters.reshape(local_filters, share, tokens), (1, 0, 2))
    piece = lax.all_gather(tap_local, "dp", axis=0, tiled=True)
    count = piece.shape[0]
    flat = piece.reshape(count, -1)
    cos_cols = tables["first_cos"]
    sin_cols = tables["first_nsin"]
    real_first = matmul(cos_cols, flat)
    imag_first = matmul(sin_cols, flat)
    spec_shape = (blocks + 1, 1, local_filters, tokens)
    filt_real, filt_imag = finish_forward(
        real_first.reshape(spec_shape), imag_first.reshape(spec_shape), tables
    )

    def single_spectrum(received):
        signal = received.reshape(blocks, -1, received.shape[2], received.shape[3])
        return spectrum(signal.astype(jnp.float32), tables)

    gated_real, gated_imag = single_spectrum(
        lax.all_to_all(gated_blocks, "ctx", split_axis=1, concat_axis=0, tiled=True)
    )
    prod_real = gated_real * filt_real - gated_imag * filt_imag
    prod_imag = gated_real * filt_imag + gated_imag * filt_real
    result = inverse_full(prod_real, prod_imag, tables).astype(jnp.bfloat16)
    conv_chan = result.reshape(blocks * repeats, 1, local_filters, tokens)
    conv_seq = lax.all_to_all(conv_chan, "ctx", split_axis=0, concat_axis=1, tiled=True)
    grad_real, grad_imag = single_spectrum(
        lax.all_to_all(grad_blocks, "ctx", split_axis=1, concat_axis=0, tiled=True)
    )
    prod_real = filt_real * grad_real + filt_imag * grad_imag
    prod_imag = filt_real * grad_imag - filt_imag * grad_real
    result = inverse_full(prod_real, prod_imag, tables).astype(jnp.bfloat16)
    gated_chan_grad = result.reshape(blocks * repeats, 1, local_filters, tokens)
    gated_seq_grad = lax.all_to_all(gated_chan_grad, "ctx", split_axis=0, concat_axis=1, tiled=True)
    cross_real = jnp.sum(gated_real * grad_real + gated_imag * grad_imag, axis=1)
    cross_imag = jnp.sum(gated_real * grad_imag - gated_imag * grad_real, axis=1)
    wave_real, wave_imag = inverse_prepare(cross_real, cross_imag, tables)
    cos_rows = tables["back_cos"]
    sin_rows = tables["back_sin"]
    term = matmul(cos_rows, wave_real) - matmul(sin_rows, wave_imag)
    summed = lax.psum_scatter(
        term.reshape(lax.axis_size("dp") * share, local_filters, tokens).astype(jnp.bfloat16),
        "dp",
        scatter_dimension=0,
        tiled=True,
    ).astype(jnp.float32)
    filter_grad = jnp.transpose(summed, (1, 0, 2)).reshape(local_filters, share * tokens)
    conv_full = conv_seq.reshape(pre_gate.shape).astype(jnp.float32)
    gated_grad = gated_seq_grad.reshape(pre_gate.shape).astype(jnp.float32)
    mixed = (post_gate.astype(jnp.float32) * conv_full).astype(jnp.bfloat16)
    post_grad = (cotangent.astype(jnp.float32) * conv_full).astype(jnp.bfloat16)
    pre_grad = (gated_grad * values.astype(jnp.float32)).astype(jnp.bfloat16)
    value_grad = (gated_grad * pre_gate.astype(jnp.float32)).astype(jnp.bfloat16)
    return (mixed, pre_grad, value_grad, post_grad, filter_grad)


def solution(mesh):
    placed = (P("dp", "ctx"), P("dp", "ctx"), P("dp", "ctx"), P("ctx", "dp"), P("dp", "ctx"))
    groups, blocks = mesh.shape["dp"], mesh.shape["ctx"]

    def program(pre_gate, values, post_gate, filters, cotangent):
        kernels = groups == 2 and blocks >= 8 and blocks & (blocks - 1) == 0 and filters.shape[0] % 16 == 0
        return (body if kernels else plain_body)(pre_gate, values, post_gate, filters, cotangent)

    return jax.shard_map(
        program,
        mesh=mesh,
        in_specs=placed,
        out_specs=(P("dp", "ctx"), P("dp", "ctx"), P("dp", "ctx"), P("dp", "ctx"), P("ctx", "dp")),
        check_vma=False,
    )
```

```python
import math

import jax
import jax.numpy as jnp
import numpy as np
from jax import lax
from jax.experimental import pallas as pl
from jax.experimental.pallas import tpu as pltpu
from jax.sharding import PartitionSpec as P


LANES = 128
SUBLANES = 8
VMEM_BYTES = 60 * 1024 * 1024
HEAVY = 1 << 37


def dft_table(size):
    angle = np.arange(size)[:, None] * (2.0 * np.arange(size)[None, :] + 1.0) * (math.pi / (2 * size))
    strips = size // LANES
    cos, sin = (part.reshape(size, strips, 1, LANES) for part in (np.cos(angle), np.sin(angle)))
    return jnp.asarray(np.concatenate([cos, -sin], axis=2).reshape(size, 2 * size), jnp.bfloat16)


def dot(left, right):
    return jnp.dot(left, right, preferred_element_type=jnp.float32)


def back(spectrum, table):
    result = lax.dot_general(spectrum, table, (((1,), (1,)), ((), ())), preferred_element_type=jnp.float32)
    return result * (2.0 / table.shape[1])


def alternating():
    odd = lax.broadcasted_iota(jnp.int32, (SUBLANES, LANES), 1) % 2
    return 1.0 - 2.0 * odd.astype(jnp.float32)


def place(half_blocks):
    index = lax.axis_index("ctx")
    return index // half_blocks, lax.rem(index, half_blocks)


def real_of(strip):
    return pl.ds(2 * strip * LANES, LANES)


def imag_of(strip):
    return pl.ds((2 * strip + 1) * LANES, LANES)


def begin(copies):
    for copy in copies:
        copy.start()
    return copies


def end(copies):
    for copy in copies:
        copy.wait()


def call(kernel, name, operands, outputs, scratch, weight=1, vmem=VMEM_BYTES, space=pltpu.HBM):
    hbm = pl.BlockSpec(memory_space=pltpu.HBM)
    return pl.pallas_call(
        kernel,
        in_specs=[pl.BlockSpec(memory_space=space)] * len(operands),
        out_specs=[hbm] * len(outputs),
        out_shape=outputs,
        scratch_shapes=scratch,
        compiler_params=pltpu.CompilerParams(vmem_limit_bytes=vmem),
        cost_estimate=pl.CostEstimate(flops=weight, bytes_accessed=weight, transcendentals=0),
        name=name,
    )(*operands)


def gate(arrays, filters, repeats, half_blocks):
    rows_all, tokens = arrays[0].shape
    rows = rows_all // repeats
    share = rows // (2 * half_blocks)
    piece = (repeats, 2, share, tokens)

    def kernel(pre_ref, value_ref, post_ref, cot_ref, filt_ref, out_ref, even_ref, odd_ref, taps_ref, in_ref, result_ref, filt_in, taps_out, in_sems, out_sems, own_sems, taps_sems):
        half, me = place(half_blocks)
        sources = (pre_ref, value_ref, cot_ref, post_ref)

        def fetch(r):
            at = pl.ds(r * rows, rows)
            return [
                pltpu.make_async_copy(ref.at[at], in_ref.at[which, r], in_sems.at[which, r])
                for which, ref in enumerate(sources)
            ]

        for r in range(repeats):
            begin(fetch(r))
        loaded = begin([pltpu.make_async_copy(filt_ref, filt_in, taps_sems.at[0])])
        sent = []
        for r in range(repeats):
            end(fetch(r))
            for which in range(2):
                product = in_ref[2 * which, r].astype(jnp.float32) * in_ref[2 * which + 1, r].astype(jnp.float32)
                product = product.astype(jnp.bfloat16).reshape(2, half_blocks, share, tokens)
                at = half if which == 0 else 1 - half
                for side in range(2):
                    result_ref[at, :, r, side] = product[side]
            for to in range(2):
                copy = pltpu.make_async_copy(result_ref.at[0, :, r], out_ref.at[to, :, r], out_sems.at[to, r])
                sent += begin([copy])
        for at in range(half_blocks // 2):
            for odd, target in enumerate((even_ref, odd_ref)):
                source = result_ref.at[1, jnp.bitwise_xor(me, 2 * at + odd)]
                sent += begin([pltpu.make_async_copy(source, target.at[at], own_sems.at[odd, at])])
        end(loaded)
        taps_out[...] = filt_in[...].astype(jnp.bfloat16)
        sent += begin([pltpu.make_async_copy(taps_out, taps_ref, taps_sems.at[1])])
        end(sent)

    own_shape = jax.ShapeDtypeStruct((half_blocks // 2, *piece), jnp.bfloat16)
    return call(
        kernel,
        "gate",
        (*arrays, filters),
        [
            jax.ShapeDtypeStruct((2, half_blocks, *piece), jnp.bfloat16),
            own_shape,
            own_shape,
            jax.ShapeDtypeStruct(filters.shape, jnp.bfloat16),
        ],
        [
            pltpu.VMEM((4, repeats, rows, tokens), jnp.bfloat16),
            pltpu.VMEM((2, half_blocks, *piece), jnp.bfloat16),
            pltpu.VMEM(filters.shape, filters.dtype),
            pltpu.VMEM(filters.shape, jnp.bfloat16),
            pltpu.SemaphoreType.DMA((4, repeats)),
            pltpu.SemaphoreType.DMA((2, repeats)),
            pltpu.SemaphoreType.DMA((2, half_blocks // 2)),
            pltpu.SemaphoreType.DMA((2,)),
        ],
    )


def exchange_own(even, odd, half_blocks):
    def swap(array, slot):
        return lax.ppermute(array, "ctx", [(i, i ^ slot) for i in range(2 * half_blocks)])

    odd = swap(odd, 1)
    groups = [([0], even[:1]), ([1], odd[:1])]
    for at in range(1, half_blocks // 2):
        pair = jnp.concatenate([even[at : at + 1], odd[at : at + 1]])
        groups.append(([2 * at, 2 * at + 1], swap(pair, 2 * at)))
    return groups


def finish(returned, arrays):
    half_blocks, _, repeats, sides, share, tokens = returned.shape
    count, rows = repeats * sides, half_blocks * share

    def kernel(recv_ref, pre_ref, value_ref, post_ref, cot_ref, *refs):
        out_refs, (held_ref, sems) = refs[:4], refs[4:]
        half, _ = place(half_blocks)
        sent = []
        for part in range(count):
            r, side = part // sides, part % sides
            at = pl.ds(part * rows, rows)
            conv = recv_ref[:, half, r, side].reshape(rows, tokens).astype(jnp.float32)
            grad = recv_ref[:, 1 - half, r, side].reshape(rows, tokens).astype(jnp.float32)
            for which, (factor_ref, result) in enumerate(
                ((post_ref, conv), (value_ref, grad), (pre_ref, grad), (cot_ref, conv))
            ):
                held_ref[which, part] = (factor_ref[at].astype(jnp.float32) * result).astype(jnp.bfloat16)
                sent += begin(
                    [pltpu.make_async_copy(held_ref.at[which, part], out_refs[which].at[at], sems.at[which, part])]
                )
        end(sent)

    shapes = [jax.ShapeDtypeStruct(arrays[0].shape, jnp.bfloat16)] * 4
    return pl.pallas_call(
        kernel,
        in_specs=[pl.BlockSpec(memory_space=pltpu.VMEM)] * 5,
        out_specs=[pl.BlockSpec(memory_space=pltpu.HBM)] * 4,
        out_shape=shapes,
        scratch_shapes=[
            pltpu.VMEM((4, count, rows, tokens), jnp.bfloat16),
            pltpu.SemaphoreType.DMA((4, count)),
        ],
        compiler_params=pltpu.CompilerParams(vmem_limit_bytes=VMEM_BYTES // 6),
        name="finish",
    )(returned, *arrays)


def pack_taps(taps, pair, half_blocks):
    share, lags = taps.shape

    def kernel(taps_ref, pair_ref, out_ref, held_ref, sems):
        half, _ = place(half_blocks)
        end(
            begin(
                [
                    pltpu.make_async_copy(taps_ref, held_ref.at[half], sems.at[0]),
                    pltpu.make_async_copy(pair_ref, held_ref.at[1 - half], sems.at[1]),
                ]
            )
        )
        end(begin([pltpu.make_async_copy(held_ref, out_ref, sems.at[2])]))

    return call(
        kernel,
        "pack_taps",
        (taps, pair),
        [jax.ShapeDtypeStruct((2, share, lags), jnp.bfloat16)],
        [pltpu.VMEM((2, share, lags), jnp.bfloat16), pltpu.SemaphoreType.DMA((3,))],
        weight=HEAVY,
        vmem=VMEM_BYTES // 12,
    )[0]


def transform_taps(here, there, half_blocks, groups, table):
    sides, share, lags = here.shape
    size = table.shape[0]
    count = groups * lags // size
    rows, width = sides * share, 2 * size

    def kernel(here_ref, there_ref, table_hbm, out_hbm, piece_ref, table_ref, stage_ref, out_ref, sems):
        sources = (here_ref, there_ref)
        loads = begin([pltpu.make_async_copy(ref, piece_ref.at[at], sems.at[at]) for at, ref in enumerate(sources)])
        tabled = begin([pltpu.make_async_copy(table_hbm, table_ref, sems.at[2])])
        half, _ = place(half_blocks)
        group = lax.axis_index("dp")
        end(loads)
        for at in range(2):
            first = (group if at == 0 else 1 - group) * (lags // size)
            for side in range(sides):
                for k in range(lags // size):
                    piece = piece_ref[at, side, :, k * size : (k + 1) * size]
                    stage_ref[first + k, side * share : (side + 1) * share] = piece
        end(tabled)
        spectrum = dot(stage_ref[...].reshape(count * rows, size), table_ref[...]).reshape(count, rows, width)
        turn = jnp.where(half == 0, 1.0, -1.0).astype(jnp.float32)
        sign = alternating()[:1]
        sent = []
        for k in range(count):
            for strip in range(size // LANES):
                re = slice(2 * strip * LANES, (2 * strip + 1) * LANES)
                im = slice((2 * strip + 1) * LANES, (2 * strip + 2) * LANES)
                real, imag = spectrum[k, :, re], spectrum[k, :, im]
                if k > 0:
                    real, imag = real - sign * spectrum[k - 1, :, im], imag + sign * spectrum[k - 1, :, re]
                out_ref[k, :, re] = real.astype(jnp.bfloat16)
                out_ref[k, :, im] = (turn * imag).astype(jnp.bfloat16)
            sent += begin([pltpu.make_async_copy(out_ref.at[k], out_hbm.at[k], sems.at[3 + k])])
        end(sent)

    return call(
        kernel,
        "taps",
        (here, there, table),
        [jax.ShapeDtypeStruct((count, rows, width), jnp.bfloat16)],
        [
            pltpu.VMEM((2, sides, share, lags), jnp.bfloat16),
            pltpu.VMEM((size, width), jnp.bfloat16),
            pltpu.VMEM((count, rows, size), jnp.bfloat16),
            pltpu.VMEM((count, rows, width), jnp.bfloat16),
            pltpu.SemaphoreType.DMA((3 + count,)),
        ],
        vmem=VMEM_BYTES // 6,
    )[0]


def add(total, term):
    return term if total is None else (total[0] + term[0], total[1] + term[1])


def times(a, b):
    return a[0] * b[0] - a[1] * b[1], a[0] * b[1] + a[1] * b[0]


def conj_times(a, b):
    return a[0] * b[0] + a[1] * b[1], a[0] * b[1] - a[1] * b[0]


def transform(stage_ref, table_ref, spec_ref):
    width = spec_ref.shape[-1]
    staged = stage_ref[...].reshape(-1, stage_ref.shape[-1])
    for strip in range(width // (2 * LANES)):
        columns = slice(2 * strip * LANES, 2 * (strip + 1) * LANES)
        spec_ref[..., columns] = dot(staged, table_ref[:, columns]).reshape(spec_ref.shape[:-1] + (2 * LANES,))


def stage_copies(source, base, stage_ref, sems, outer, half_blocks):
    count, _, size = stage_ref.shape
    tokens = source.shape[2]
    merge = size // tokens
    half, _ = place(half_blocks)
    copies = []
    for k in range(count):
        block = order(k, count, half, outer)
        for q in range(merge):
            target = stage_ref.at[k, :, pl.ds(q * tokens, tokens)]
            copies.append(pltpu.make_async_copy(source.at[base + block * merge + q], target, sems.at[k, q]))
    return copies


def stage_all(near_hbm, own_refs, slots, stage_ref, sems, half_blocks):
    _, count, _, size = stage_ref.shape
    tokens = near_hbm.shape[2]
    merge = size // tokens
    half, me = place(half_blocks)
    near = stage_copies(near_hbm, half * half_blocks, stage_ref.at[0], sems.at[0], True, half_blocks)
    far = stage_copies(near_hbm, (1 - half) * half_blocks, stage_ref.at[1], sems.at[1], False, half_blocks)
    own = []
    for group, ref in zip(slots, own_refs):
        for at, slot in enumerate(group):
            position = jnp.bitwise_xor(me, slot)
            k = order(position // merge, count, half, False)
            start = pl.multiple_of(lax.rem(position, merge) * tokens, tokens)
            target = stage_ref.at[2, k, :, pl.ds(start, tokens)]
            own.append(pltpu.make_async_copy(ref.at[at], target, sems.at[2, slot // merge, slot % merge]))
    return begin(near) + begin(far), begin(own)


def order(k, count, half, outer):
    return jnp.where(half == (0 if outer else 1), k, count - 1 - k)


def tile_loop(rows, body):
    @pl.loop(0, rows // SUBLANES)
    def _(tile):
        body(pl.multiple_of(tile * SUBLANES, SUBLANES))


def parts(ref, k, row, strip):
    return ref[k, row, real_of(strip)], ref[k, row, imag_of(strip)]


def keep(ref, k, row, strip, value):
    ref[k, row, real_of(strip)], ref[k, row, imag_of(strip)] = value


def give_back(prod_ref, table_ref, held_ref, out_ref, sems, outer, half_blocks):
    count, rows, width = prod_ref.shape
    merge, tokens = held_ref.shape[1], held_ref.shape[3]
    half, _ = place(half_blocks)
    sent = []
    spectrum = prod_ref[...].astype(jnp.bfloat16).reshape(count * rows, width)
    for q in range(merge):
        result = back(spectrum, table_ref[q * tokens : (q + 1) * tokens])
        held_ref[:, q] = result.astype(jnp.bfloat16).reshape(count, rows, tokens)
        for k in range(count):
            block = order(k, count, half, outer)
            sent += begin(
                [pltpu.make_async_copy(held_ref.at[k, q], out_ref.at[block * merge + q], sems.at[k, q])]
            )
    end(sent)


def results(near, own, filt, half_blocks, table):
    slots = [group for group, _ in own]
    _, rows, tokens = near.shape
    size, width = table.shape
    merge = size // tokens
    count = half_blocks // merge
    filters = filt.shape[1]

    def kernel(near_ref, *refs):
        own_refs, (filt_in, table_ref, out_hbm) = refs[: len(own)], refs[len(own) : len(own) + 3]
        stage_ref, filt_ref, spec_ref, prod_ref, held_ref, out_sems = refs[len(own) + 3 :]
        half, me = place(half_blocks)
        for k in range(count):
            for q in range(merge):
                lanes = pl.ds(q * tokens, tokens)
                outer, inner = order(k, count, half, True), order(k, count, half, False)
                stage_ref[0, k, :, lanes] = near_ref[half * half_blocks + outer * merge + q]
                stage_ref[1, k, :, lanes] = near_ref[(1 - half) * half_blocks + inner * merge + q]
        for group, ref in zip(slots, own_refs):
            for at, slot in enumerate(group):
                position = jnp.bitwise_xor(me, slot)
                k = order(position // merge, count, half, False)
                start = pl.multiple_of(lax.rem(position, merge) * tokens, tokens)
                stage_ref[2, k, :, pl.ds(start, tokens)] = ref[at]
        filt_ref[...] = filt_in[...].astype(jnp.float32)
        transform(stage_ref, table_ref, spec_ref)

        def tile(first):
            row = pl.ds(first, SUBLANES)
            tap_row = pl.ds(pl.multiple_of(lax.rem(first, filters), SUBLANES), SUBLANES)
            for strip in range(size // LANES):
                taps = [parts(filt_ref, k, tap_row, strip) for k in range(2 * count)]
                near, far, own = ([parts(spec_ref.at[which], k, row, strip) for k in range(count)] for which in range(3))
                for out in range(count):
                    total = None
                    for k in range(out + 1):
                        total = add(total, times(taps[out - k], near[k]))
                    keep(prod_ref.at[0], out, row, strip, total)
                for out in range(count):
                    total = None
                    for k in range(out + 1):
                        total = add(total, conj_times(taps[out - k], own[k]))
                    for k in range(count):
                        total = add(total, conj_times(taps[count + out - k], far[k]))
                    keep(prod_ref.at[1], out, row, strip, total)

        tile_loop(rows, tile)
        spectrum = prod_ref[...].astype(jnp.bfloat16).reshape(2 * count * rows, width)
        sent = []
        for q in range(merge):
            result = back(spectrum, table_ref[q * tokens : (q + 1) * tokens]).astype(jnp.bfloat16)
            held_ref[:, :, q] = result.reshape(2, count, rows, tokens)
            for which in range(2):
                for k in range(count):
                    position = order(k, count, half, which == 0) * merge + q
                    copy = pltpu.make_async_copy(
                        held_ref.at[which, k, q], out_hbm.at[position, which], out_sems.at[which, k, q]
                    )
                    sent += begin([copy])
        end(sent)

    return call(
        kernel,
        "results",
        (near, *[array for _, array in own], filt, table),
        [jax.ShapeDtypeStruct((half_blocks, 2, rows, tokens), jnp.bfloat16)],
        [
            pltpu.VMEM((3, count, rows, size), jnp.bfloat16),
            pltpu.VMEM((2 * count, filters, width), jnp.float32),
            pltpu.VMEM((3, count, rows, width), jnp.float32),
            pltpu.VMEM((2, count, rows, width), jnp.float32),
            pltpu.VMEM((2, count, merge, rows, tokens), jnp.bfloat16),
            pltpu.SemaphoreType.DMA((2, count, merge)),
        ],
        vmem=VMEM_BYTES // 2,
        weight=HEAVY,
        space=pltpu.VMEM,
    )[0]


def lag_products(near_ref, other_ref, row_at, strip, repeats, filters, totals):
    count = near_ref.shape[0]
    sums = [None] * len(totals)
    for repeat in range(repeats):
        row = pl.ds(pl.multiple_of(repeat * filters + row_at, SUBLANES), SUBLANES)
        near = [parts(near_ref, k, row, strip) for k in range(count)]
        other = [parts(other_ref, k, row, strip) for k in range(count)]
        for at, total in enumerate(totals):
            for a in range(count):
                if 0 <= total - a < count:
                    sums[at] = add(sums[at], conj_times(near[a], other[total - a]))
    return sums


def join_lags(ref, row, joint_ref, base):
    lags, size = ref.shape[0], ref.shape[2] // 2
    sign = alternating()[:1]
    for k in range(lags):
        for strip in range(size // LANES):
            real, imag = parts(ref, k, row, strip)
            if k + 1 < lags:
                next_real, next_imag = parts(ref, k + 1, row, strip)
                real, imag = real + sign * next_imag, imag - sign * next_real
            keep(joint_ref, base + k, slice(None), strip, (real.astype(jnp.bfloat16), imag.astype(jnp.bfloat16)))


def filter_terms(near, own, filters, half_blocks, table):
    slots = [group for group, _ in own]
    _, rows, tokens = near.shape
    size, width = table.shape
    merge = size // tokens
    count = half_blocks // merge
    kept, lags = filters // 2, count * size
    repeats = rows // filters

    def kernel(near_hbm, *refs):
        own_hbm, refs = refs[: len(own)], refs[len(own) :]
        table_hbm, give_hbm, mine_hbm, upper_hbm, lower_hbm, stage_ref, table_ref, spec_ref, local_ref, cross_ref, joint_ref = refs[:11]
        held_ref, give_ref, mine_ref, theirs_ref, sems, stage_sems = refs[11:]
        tabled = begin([pltpu.make_async_copy(table_hbm, table_ref, sems.at[0])])
        staged, later = stage_all(near_hbm, own_hbm, slots, stage_ref, stage_sems, half_blocks)
        half, _ = place(half_blocks)
        group = lax.axis_index("dp")
        turn = jnp.where(half == 0, 1.0, -1.0).astype(jnp.float32)
        end(tabled)
        end(staged)
        end(later)
        transform(stage_ref, table_ref, spec_ref)
        near_ref, far_ref, own_ref = (spec_ref.at[which] for which in range(3))

        def local_tile(first):
            for strip in range(size // LANES):
                sums = lag_products(near_ref, own_ref, first, strip, repeats, filters, [count - 1 - k for k in range(count)])
                for k, (real, imag) in enumerate(sums):
                    keep(local_ref, k, pl.ds(first, SUBLANES), strip, (real, turn * imag))

        tile_loop(filters, local_tile)
        mine = pl.multiple_of(half * kept, SUBLANES)
        other = pl.multiple_of((1 - half) * kept, SUBLANES)
        join_lags(local_ref, pl.ds(other, kept), joint_ref, 0)
        result = back(joint_ref[:count].reshape(count * kept, width), table_ref[...]).reshape(count, kept, size)
        for k in range(count):
            give_ref[:, k * size : (k + 1) * size] = result[k].astype(jnp.bfloat16)
        sent = begin([pltpu.make_async_copy(give_ref, give_hbm, sems.at[1])])

        def cross_tile(first):
            row = pl.ds(first, SUBLANES)
            at = pl.ds(pl.multiple_of(mine + first, SUBLANES), SUBLANES)
            for strip in range(size // LANES):
                totals = [2 * count - 1 - k for k in range(1, 2 * count)]
                sums = lag_products(near_ref, far_ref, mine + first, strip, repeats, filters, totals)
                keep(cross_ref, 0, row, strip, parts(local_ref, 0, at, strip))
                for k, (real, imag) in enumerate(sums, 1):
                    value = (real, turn * imag)
                    keep(cross_ref, k, row, strip, add(value, parts(local_ref, k, at, strip)) if k < count else value)

        tile_loop(kept, cross_tile)
        join_lags(cross_ref, slice(None), joint_ref, 0)
        result = back(joint_ref[...].reshape(2 * count * kept, width), table_ref[...])
        held_ref[...] = result.reshape(2, count, kept, size)
        for k in range(count):
            columns = slice(k * size, (k + 1) * size)
            mine_ref[:, columns] = held_ref[group, k]
            theirs_ref[:, columns] = held_ref[1 - group, k].astype(jnp.bfloat16)
        sent += begin(
            [
                pltpu.make_async_copy(theirs_ref.at[pl.ds(0, kept // 2)], upper_hbm, sems.at[2]),
                pltpu.make_async_copy(theirs_ref.at[pl.ds(kept // 2, kept // 2)], lower_hbm, sems.at[3]),
                pltpu.make_async_copy(mine_ref, mine_hbm, sems.at[4]),
            ]
        )
        end(sent)

    return call(
        kernel,
        "filter_terms",
        (near, *[array for _, array in own], table),
        [
            jax.ShapeDtypeStruct((kept, lags), jnp.bfloat16),
            jax.ShapeDtypeStruct((kept, lags), jnp.float32),
            jax.ShapeDtypeStruct((kept // 2, lags), jnp.bfloat16),
            jax.ShapeDtypeStruct((kept // 2, lags), jnp.bfloat16),
        ],
        [
            pltpu.VMEM((3, count, rows, size), jnp.bfloat16),
            pltpu.VMEM(table.shape, jnp.bfloat16),
            pltpu.VMEM((3, count, rows, width), jnp.float32),
            pltpu.VMEM((count, filters, width), jnp.float32),
            pltpu.VMEM((2 * count, kept, width), jnp.float32),
            pltpu.VMEM((2 * count, kept, width), jnp.bfloat16),
            pltpu.VMEM((2, count, kept, size), jnp.float32),
            pltpu.VMEM((kept, lags), jnp.bfloat16),
            pltpu.VMEM((kept, lags), jnp.float32),
            pltpu.VMEM((kept, lags), jnp.bfloat16),
            pltpu.SemaphoreType.DMA((5,)),
            pltpu.SemaphoreType.DMA((3, count, merge)),
        ],
    )


def body(pre_gate, values, post_gate, filters, cotangent):
    blocks = lax.axis_size("ctx")
    groups = lax.axis_size("dp")
    half_blocks = blocks // 2
    local_rows, tokens = pre_gate.shape
    local_filters = filters.shape[0]
    repeats = local_rows // (local_filters * blocks)
    rows = 2 * local_filters * repeats
    table = dft_table(2 * tokens)
    arrays = (pre_gate, values, post_gate, cotangent)
    sides = [list(range(half_blocks)), list(range(half_blocks, blocks))]

    def swap(array):
        return lax.ppermute(array, "ctx", [(i, i ^ half_blocks) for i in range(blocks)])

    def other_group(array):
        return lax.ppermute(array, "dp", [(0, 1), (1, 0)])

    near, even, odd, taps = gate(arrays, filters, repeats, half_blocks)
    here = pack_taps(taps, swap(taps), half_blocks)
    odd, here = lax.optimization_barrier((odd, here))
    near = lax.all_to_all(near.reshape(blocks, rows, tokens), "ctx", split_axis=0, concat_axis=0, tiled=True)
    shape = (half_blocks // 2, rows, tokens)
    own = exchange_own(even.reshape(shape), odd.reshape(shape), half_blocks)
    filt = transform_taps(here, other_group(here), half_blocks, groups, table)

    result = results(near, own, filt, half_blocks, table)
    result, near = lax.optimization_barrier((result, near))
    returned = lax.all_to_all(
        result, "ctx", split_axis=0, concat_axis=0, tiled=True, axis_index_groups=sides
    )
    give, mine, upper, lower = filter_terms(near, own, 2 * local_filters, half_blocks, table)
    to_first = [(blocks + i, i ^ half_blocks) for i in range(blocks)]
    halves = (swap(give), lax.ppermute(give, ("dp", "ctx"), to_first))
    theirs = jnp.concatenate([other_group(upper), other_group(lower)])
    outputs = finish(returned.reshape(half_blocks, 2, repeats, 2, local_filters, tokens), arrays)
    mine, mixed, pre_grad, value_grad, post_grad = lax.optimization_barrier((mine, *outputs))
    first = jnp.where(lax.axis_index("dp") == 0, 1.0, 0.0)
    filter_grad = mine + theirs.astype(jnp.float32) + first * (halves[0].astype(jnp.float32) + halves[1].astype(jnp.float32))
    return (mixed, pre_grad, value_grad, post_grad, filter_grad)


def matmul(left, right):
    return jnp.dot(left, right, precision=lax.Precision.HIGHEST, preferred_element_type=jnp.float32)


def contract(form, left, right):
    return jnp.einsum(
        form, left, right, precision=lax.Precision.HIGHEST, preferred_element_type=jnp.float32
    )


def phases(height, width, modulus):
    product = lax.broadcasted_iota(jnp.int32, (height, width), 0) * lax.broadcasted_iota(
        jnp.int32, (height, width), 1
    )
    return (product % modulus).astype(jnp.float32) * (2.0 * math.pi / modulus)


def build_tables(blocks, tokens):
    factor = 1
    for candidate in range(1, tokens + 1):
        if tokens % candidate == 0 and candidate * candidate <= tokens:
            factor = candidate
    second = tokens // factor
    rows = blocks + 1
    total = 2 * blocks * tokens
    first_angle = phases(rows, blocks, 2 * blocks)
    twist_angle = phases(rows, tokens, total)
    inner_angle = phases(factor, factor, factor)
    middle_angle = phases(factor, second, tokens)
    outer_angle = phases(second, second, second)
    back_angle = phases(blocks, rows, 2 * blocks)
    column = lax.broadcasted_iota(jnp.int32, (blocks, rows), 1)
    weight = jnp.where((column == 0) | (column == blocks), 1.0, 2.0).astype(jnp.float32) / total
    return {
        "first_cos": jnp.cos(first_angle),
        "first_nsin": -jnp.sin(first_angle),
        "twist_cos": jnp.cos(twist_angle),
        "twist_sin": jnp.sin(twist_angle),
        "inner_cos": jnp.cos(inner_angle),
        "inner_sin": jnp.sin(inner_angle),
        "middle_cos": jnp.cos(middle_angle),
        "middle_sin": jnp.sin(middle_angle),
        "outer_cos": jnp.cos(outer_angle),
        "outer_sin": jnp.sin(outer_angle),
        "back_cos": weight * jnp.cos(back_angle),
        "back_sin": weight * jnp.sin(back_angle),
    }


def expand(table, ndim):
    return table.reshape((table.shape[0],) + (1,) * (ndim - 2) + (table.shape[1],))


def block_table(cos_part, sin_part):
    return jnp.stack([jnp.stack([cos_part, sin_part]), jnp.stack([-sin_part, cos_part])])


def wave(real_part, imag_part, tables, sign):
    shape = real_part.shape
    factor = tables["inner_cos"].shape[0]
    second = tables["outer_cos"].shape[0]
    stacked = jnp.stack(
        [real_part.reshape(-1, factor, second), imag_part.reshape(-1, factor, second)]
    )
    inner_table = block_table(tables["inner_cos"], sign * tables["inner_sin"])
    middle = contract("prab,pqac->qrcb", stacked, inner_table)
    middle_cos = tables["middle_cos"]
    middle_sin = sign * tables["middle_sin"]
    real_turn = middle[0] * middle_cos - middle[1] * middle_sin
    imag_turn = middle[0] * middle_sin + middle[1] * middle_cos
    turned = jnp.stack([real_turn, imag_turn])
    outer_table = block_table(tables["outer_cos"], sign * tables["outer_sin"])
    result = contract("prcb,pqbd->qrdc", turned, outer_table)
    return (result[0].reshape(shape), result[1].reshape(shape))


def finish_forward(real_first, imag_first, tables):
    ndim = real_first.ndim
    twist_cos = expand(tables["twist_cos"], ndim)
    twist_sin = expand(tables["twist_sin"], ndim)
    real_twist = real_first * twist_cos + imag_first * twist_sin
    imag_twist = imag_first * twist_cos - real_first * twist_sin
    return wave(real_twist, imag_twist, tables, -1.0)


def spectrum(signal, tables):
    flat = signal.reshape(signal.shape[0], -1)
    shape = (tables["first_cos"].shape[0],) + signal.shape[1:]
    real_first = matmul(tables["first_cos"], flat).reshape(shape)
    imag_first = matmul(tables["first_nsin"], flat).reshape(shape)
    return finish_forward(real_first, imag_first, tables)


def inverse_prepare(real_spec, imag_spec, tables):
    ndim = real_spec.ndim
    real_wave, imag_wave = wave(real_spec, imag_spec, tables, 1.0)
    twist_cos = expand(tables["twist_cos"], ndim)
    twist_sin = expand(tables["twist_sin"], ndim)
    real_twist = real_wave * twist_cos - imag_wave * twist_sin
    imag_twist = real_wave * twist_sin + imag_wave * twist_cos
    rows = real_spec.shape[0]
    return (real_twist.reshape(rows, -1), imag_twist.reshape(rows, -1))


def inverse_full(real_spec, imag_spec, tables):
    real_flat, imag_flat = inverse_prepare(real_spec, imag_spec, tables)
    signal = matmul(tables["back_cos"], real_flat) - matmul(tables["back_sin"], imag_flat)
    return signal.reshape((tables["back_cos"].shape[0],) + real_spec.shape[1:])


def plain_body(pre_gate, values, post_gate, filters, cotangent):
    blocks = lax.axis_size("ctx")
    groups = lax.axis_size("dp")
    local_rows = pre_gate.shape[0]
    tokens = pre_gate.shape[1]
    local_filters = filters.shape[0]
    repeats = local_rows // (local_filters * blocks)
    share = blocks // groups
    tables = build_tables(blocks, tokens)
    gated = (pre_gate.astype(jnp.float32) * values.astype(jnp.float32)).astype(jnp.bfloat16)
    conv_grad = (cotangent.astype(jnp.float32) * post_gate.astype(jnp.float32)).astype(jnp.bfloat16)
    gated_blocks = gated.reshape(repeats, blocks, local_filters, tokens)
    grad_blocks = conv_grad.reshape(repeats, blocks, local_filters, tokens)
    tap_local = jnp.transpose(filters.reshape(local_filters, share, tokens), (1, 0, 2))
    piece = lax.all_gather(tap_local, "dp", axis=0, tiled=True)
    count = piece.shape[0]
    flat = piece.reshape(count, -1)
    cos_cols = tables["first_cos"]
    sin_cols = tables["first_nsin"]
    real_first = matmul(cos_cols, flat)
    imag_first = matmul(sin_cols, flat)
    spec_shape = (blocks + 1, 1, local_filters, tokens)
    filt_real, filt_imag = finish_forward(
        real_first.reshape(spec_shape), imag_first.reshape(spec_shape), tables
    )

    def single_spectrum(received):
        signal = received.reshape(blocks, -1, received.shape[2], received.shape[3])
        return spectrum(signal.astype(jnp.float32), tables)

    gated_real, gated_imag = single_spectrum(
        lax.all_to_all(gated_blocks, "ctx", split_axis=1, concat_axis=0, tiled=True)
    )
    prod_real = gated_real * filt_real - gated_imag * filt_imag
    prod_imag = gated_real * filt_imag + gated_imag * filt_real
    result = inverse_full(prod_real, prod_imag, tables).astype(jnp.bfloat16)
    conv_chan = result.reshape(blocks * repeats, 1, local_filters, tokens)
    conv_seq = lax.all_to_all(conv_chan, "ctx", split_axis=0, concat_axis=1, tiled=True)
    grad_real, grad_imag = single_spectrum(
        lax.all_to_all(grad_blocks, "ctx", split_axis=1, concat_axis=0, tiled=True)
    )
    prod_real = filt_real * grad_real + filt_imag * grad_imag
    prod_imag = filt_real * grad_imag - filt_imag * grad_real
    result = inverse_full(prod_real, prod_imag, tables).astype(jnp.bfloat16)
    gated_chan_grad = result.reshape(blocks * repeats, 1, local_filters, tokens)
    gated_seq_grad = lax.all_to_all(gated_chan_grad, "ctx", split_axis=0, concat_axis=1, tiled=True)
    cross_real = jnp.sum(gated_real * grad_real + gated_imag * grad_imag, axis=1)
    cross_imag = jnp.sum(gated_real * grad_imag - gated_imag * grad_real, axis=1)
    wave_real, wave_imag = inverse_prepare(cross_real, cross_imag, tables)
    cos_rows = tables["back_cos"]
    sin_rows = tables["back_sin"]
    term = matmul(cos_rows, wave_real) - matmul(sin_rows, wave_imag)
    summed = lax.psum_scatter(
        term.reshape(lax.axis_size("dp") * share, local_filters, tokens).astype(jnp.bfloat16),
        "dp",
        scatter_dimension=0,
        tiled=True,
    ).astype(jnp.float32)
    filter_grad = jnp.transpose(summed, (1, 0, 2)).reshape(local_filters, share * tokens)
    conv_full = conv_seq.reshape(pre_gate.shape).astype(jnp.float32)
    gated_grad = gated_seq_grad.reshape(pre_gate.shape).astype(jnp.float32)
    mixed = (post_gate.astype(jnp.float32) * conv_full).astype(jnp.bfloat16)
    post_grad = (cotangent.astype(jnp.float32) * conv_full).astype(jnp.bfloat16)
    pre_grad = (gated_grad * values.astype(jnp.float32)).astype(jnp.bfloat16)
    value_grad = (gated_grad * pre_gate.astype(jnp.float32)).astype(jnp.bfloat16)
    return (mixed, pre_grad, value_grad, post_grad, filter_grad)


def solution(mesh):
    placed = (P("dp", "ctx"), P("dp", "ctx"), P("dp", "ctx"), P("ctx", "dp"), P("dp", "ctx"))
    groups, blocks = mesh.shape["dp"], mesh.shape["ctx"]

    def program(pre_gate, values, post_gate, filters, cotangent):
        kernels = groups == 2 and blocks >= 8 and blocks & (blocks - 1) == 0 and filters.shape[0] % 16 == 0
        return (body if kernels else plain_body)(pre_gate, values, post_gate, filters, cotangent)

    return jax.shard_map(
        program,
        mesh=mesh,
        in_specs=placed,
        out_specs=(P("dp", "ctx"), P("dp", "ctx"), P("dp", "ctx"), P("dp", "ctx"), P("ctx", "dp")),
        check_vma=False,
    )
```

```python
import math

import jax
import jax.numpy as jnp
import numpy as np
from jax import lax
from jax.experimental import pallas as pl
from jax.experimental.pallas import tpu as pltpu
from jax.sharding import PartitionSpec as P


LANES = 128
SUBLANES = 8
VMEM_BYTES = 60 * 1024 * 1024
HEAVY = 1 << 37


def dft_table(size):
    angle = np.arange(size)[:, None] * (2.0 * np.arange(size)[None, :] + 1.0) * (math.pi / (2 * size))
    strips = size // LANES
    cos, sin = (part.reshape(size, strips, 1, LANES) for part in (np.cos(angle), np.sin(angle)))
    return jnp.asarray(np.concatenate([cos, -sin], axis=2).reshape(size, 2 * size), jnp.bfloat16)


def dot(left, right):
    return jnp.dot(left, right, preferred_element_type=jnp.float32)


def back(spectrum, table):
    result = lax.dot_general(spectrum, table, (((1,), (1,)), ((), ())), preferred_element_type=jnp.float32)
    return result * (2.0 / table.shape[1])


def alternating():
    odd = lax.broadcasted_iota(jnp.int32, (SUBLANES, LANES), 1) % 2
    return 1.0 - 2.0 * odd.astype(jnp.float32)


def place(half_blocks):
    index = lax.axis_index("ctx")
    return index // half_blocks, lax.rem(index, half_blocks)


def real_of(strip):
    return pl.ds(2 * strip * LANES, LANES)


def imag_of(strip):
    return pl.ds((2 * strip + 1) * LANES, LANES)


def begin(copies):
    for copy in copies:
        copy.start()
    return copies


def end(copies):
    for copy in copies:
        copy.wait()


def call(kernel, name, operands, outputs, scratch, weight=1, vmem=VMEM_BYTES, space=pltpu.HBM):
    hbm = pl.BlockSpec(memory_space=pltpu.HBM)
    return pl.pallas_call(
        kernel,
        in_specs=[pl.BlockSpec(memory_space=space)] * len(operands),
        out_specs=[hbm] * len(outputs),
        out_shape=outputs,
        scratch_shapes=scratch,
        compiler_params=pltpu.CompilerParams(vmem_limit_bytes=vmem),
        cost_estimate=pl.CostEstimate(flops=weight, bytes_accessed=weight, transcendentals=0),
        name=name,
    )(*operands)


def gate(arrays, filters, repeats, half_blocks):
    rows_all, tokens = arrays[0].shape
    rows = rows_all // repeats
    share = rows // (2 * half_blocks)
    piece = (repeats, 2, share, tokens)

    def kernel(pre_ref, value_ref, post_ref, cot_ref, filt_ref, out_ref, even_ref, odd_ref, taps_ref, in_ref, result_ref, filt_in, taps_out, in_sems, out_sems, own_sems, taps_sems):
        half, me = place(half_blocks)
        sources = (pre_ref, value_ref, cot_ref, post_ref)

        def fetch(r):
            at = pl.ds(r * rows, rows)
            return [
                pltpu.make_async_copy(ref.at[at], in_ref.at[which, r], in_sems.at[which, r])
                for which, ref in enumerate(sources)
            ]

        for r in range(repeats):
            begin(fetch(r))
        loaded = begin([pltpu.make_async_copy(filt_ref, filt_in, taps_sems.at[0])])
        sent = []
        for r in range(repeats):
            end(fetch(r))
            for which in range(2):
                product = in_ref[2 * which, r].astype(jnp.float32) * in_ref[2 * which + 1, r].astype(jnp.float32)
                product = product.astype(jnp.bfloat16).reshape(2, half_blocks, share, tokens)
                at = half if which == 0 else 1 - half
                for side in range(2):
                    result_ref[at, :, r, side] = product[side]
            for to in range(2):
                copy = pltpu.make_async_copy(result_ref.at[0, :, r], out_ref.at[to, :, r], out_sems.at[to, r])
                sent += begin([copy])
        for at in range(half_blocks // 2):
            for odd, target in enumerate((even_ref, odd_ref)):
                source = result_ref.at[1, jnp.bitwise_xor(me, 2 * at + odd)]
                sent += begin([pltpu.make_async_copy(source, target.at[at], own_sems.at[odd, at])])
        end(loaded)
        taps_out[...] = filt_in[...].astype(jnp.bfloat16)
        sent += begin([pltpu.make_async_copy(taps_out, taps_ref, taps_sems.at[1])])
        end(sent)

    own_shape = jax.ShapeDtypeStruct((half_blocks // 2, *piece), jnp.bfloat16)
    return call(
        kernel,
        "gate",
        (*arrays, filters),
        [
            jax.ShapeDtypeStruct((2, half_blocks, *piece), jnp.bfloat16),
            own_shape,
            own_shape,
            jax.ShapeDtypeStruct(filters.shape, jnp.bfloat16),
        ],
        [
            pltpu.VMEM((4, repeats, rows, tokens), jnp.bfloat16),
            pltpu.VMEM((2, half_blocks, *piece), jnp.bfloat16),
            pltpu.VMEM(filters.shape, filters.dtype),
            pltpu.VMEM(filters.shape, jnp.bfloat16),
            pltpu.SemaphoreType.DMA((4, repeats)),
            pltpu.SemaphoreType.DMA((2, repeats)),
            pltpu.SemaphoreType.DMA((2, half_blocks // 2)),
            pltpu.SemaphoreType.DMA((2,)),
        ],
    )


def exchange_own(even, odd, half_blocks):
    def swap(array, slot):
        return lax.ppermute(array, "ctx", [(i, i ^ slot) for i in range(2 * half_blocks)])

    odd = swap(odd, 1)
    groups = [([0], even[:1]), ([1], odd[:1])]
    for at in range(1, half_blocks // 2):
        pair = jnp.concatenate([even[at : at + 1], odd[at : at + 1]])
        groups.append(([2 * at, 2 * at + 1], swap(pair, 2 * at)))
    return groups


def finish(returned, arrays):
    half_blocks, _, repeats, sides, share, tokens = returned.shape
    count, rows = repeats * sides, half_blocks * share

    def kernel(recv_ref, pre_ref, value_ref, post_ref, cot_ref, *refs):
        out_refs, (held_ref, sems) = refs[:4], refs[4:]
        half, _ = place(half_blocks)
        sent = []
        for part in range(count):
            r, side = part // sides, part % sides
            at = pl.ds(part * rows, rows)
            conv = recv_ref[:, half, r, side].reshape(rows, tokens).astype(jnp.float32)
            grad = recv_ref[:, 1 - half, r, side].reshape(rows, tokens).astype(jnp.float32)
            for which, (factor_ref, result) in enumerate(
                ((post_ref, conv), (value_ref, grad), (pre_ref, grad), (cot_ref, conv))
            ):
                held_ref[which, part] = (factor_ref[at].astype(jnp.float32) * result).astype(jnp.bfloat16)
                sent += begin(
                    [pltpu.make_async_copy(held_ref.at[which, part], out_refs[which].at[at], sems.at[which, part])]
                )
        end(sent)

    shapes = [jax.ShapeDtypeStruct(arrays[0].shape, jnp.bfloat16)] * 4
    return pl.pallas_call(
        kernel,
        in_specs=[pl.BlockSpec(memory_space=pltpu.VMEM)] * 5,
        out_specs=[pl.BlockSpec(memory_space=pltpu.HBM)] * 4,
        out_shape=shapes,
        scratch_shapes=[
            pltpu.VMEM((4, count, rows, tokens), jnp.bfloat16),
            pltpu.SemaphoreType.DMA((4, count)),
        ],
        compiler_params=pltpu.CompilerParams(vmem_limit_bytes=VMEM_BYTES // 6),
        name="finish",
    )(returned, *arrays)


def pack_taps(taps, pair, half_blocks):
    share, lags = taps.shape

    def kernel(taps_ref, pair_ref, out_ref, held_ref, sems):
        half, _ = place(half_blocks)
        end(
            begin(
                [
                    pltpu.make_async_copy(taps_ref, held_ref.at[half], sems.at[0]),
                    pltpu.make_async_copy(pair_ref, held_ref.at[1 - half], sems.at[1]),
                ]
            )
        )
        end(begin([pltpu.make_async_copy(held_ref, out_ref, sems.at[2])]))

    return call(
        kernel,
        "pack_taps",
        (taps, pair),
        [jax.ShapeDtypeStruct((2, share, lags), jnp.bfloat16)],
        [pltpu.VMEM((2, share, lags), jnp.bfloat16), pltpu.SemaphoreType.DMA((3,))],
        weight=HEAVY,
        vmem=VMEM_BYTES // 12,
    )[0]


def transform_taps(here, there, half_blocks, groups, table):
    sides, share, lags = here.shape
    size = table.shape[0]
    count = groups * lags // size
    rows, width = sides * share, 2 * size

    def kernel(here_ref, there_ref, table_hbm, out_hbm, piece_ref, table_ref, stage_ref, out_ref, sems):
        sources = (here_ref, there_ref)
        loads = begin([pltpu.make_async_copy(ref, piece_ref.at[at], sems.at[at]) for at, ref in enumerate(sources)])
        tabled = begin([pltpu.make_async_copy(table_hbm, table_ref, sems.at[2])])
        half, _ = place(half_blocks)
        group = lax.axis_index("dp")
        end(loads)
        for at in range(2):
            first = (group if at == 0 else 1 - group) * (lags // size)
            for side in range(sides):
                for k in range(lags // size):
                    piece = piece_ref[at, side, :, k * size : (k + 1) * size]
                    stage_ref[first + k, side * share : (side + 1) * share] = piece
        end(tabled)
        spectrum = dot(stage_ref[...].reshape(count * rows, size), table_ref[...]).reshape(count, rows, width)
        turn = jnp.where(half == 0, 1.0, -1.0).astype(jnp.float32)
        sign = alternating()[:1]
        sent = []
        for k in range(count):
            for strip in range(size // LANES):
                re = slice(2 * strip * LANES, (2 * strip + 1) * LANES)
                im = slice((2 * strip + 1) * LANES, (2 * strip + 2) * LANES)
                real, imag = spectrum[k, :, re], spectrum[k, :, im]
                if k > 0:
                    real, imag = real - sign * spectrum[k - 1, :, im], imag + sign * spectrum[k - 1, :, re]
                out_ref[k, :, re] = real.astype(jnp.bfloat16)
                out_ref[k, :, im] = (turn * imag).astype(jnp.bfloat16)
            sent += begin([pltpu.make_async_copy(out_ref.at[k], out_hbm.at[k], sems.at[3 + k])])
        end(sent)

    return call(
        kernel,
        "taps",
        (here, there, table),
        [jax.ShapeDtypeStruct((count, rows, width), jnp.bfloat16)],
        [
            pltpu.VMEM((2, sides, share, lags), jnp.bfloat16),
            pltpu.VMEM((size, width), jnp.bfloat16),
            pltpu.VMEM((count, rows, size), jnp.bfloat16),
            pltpu.VMEM((count, rows, width), jnp.bfloat16),
            pltpu.SemaphoreType.DMA((3 + count,)),
        ],
        vmem=VMEM_BYTES // 6,
    )[0]


def add(total, term):
    return term if total is None else (total[0] + term[0], total[1] + term[1])


def times(a, b):
    return a[0] * b[0] - a[1] * b[1], a[0] * b[1] + a[1] * b[0]


def conj_times(a, b):
    return a[0] * b[0] + a[1] * b[1], a[0] * b[1] - a[1] * b[0]


def transform(stage_ref, table_ref, spec_ref):
    width = spec_ref.shape[-1]
    staged = stage_ref[...].reshape(-1, stage_ref.shape[-1])
    for strip in range(width // (2 * LANES)):
        columns = slice(2 * strip * LANES, 2 * (strip + 1) * LANES)
        spec_ref[..., columns] = dot(staged, table_ref[:, columns]).reshape(spec_ref.shape[:-1] + (2 * LANES,))


def stage_copies(source, base, stage_ref, sems, outer, half_blocks):
    count, _, size = stage_ref.shape
    tokens = source.shape[2]
    merge = size // tokens
    half, _ = place(half_blocks)
    copies = []
    for k in range(count):
        block = order(k, count, half, outer)
        for q in range(merge):
            target = stage_ref.at[k, :, pl.ds(q * tokens, tokens)]
            copies.append(pltpu.make_async_copy(source.at[base + block * merge + q], target, sems.at[k, q]))
    return copies


def stage_all(near_hbm, own_refs, slots, stage_ref, sems, half_blocks):
    _, count, _, size = stage_ref.shape
    tokens = near_hbm.shape[2]
    merge = size // tokens
    half, me = place(half_blocks)
    near = stage_copies(near_hbm, half * half_blocks, stage_ref.at[0], sems.at[0], True, half_blocks)
    far = stage_copies(near_hbm, (1 - half) * half_blocks, stage_ref.at[1], sems.at[1], False, half_blocks)
    own = []
    for group, ref in zip(slots, own_refs):
        for at, slot in enumerate(group):
            position = jnp.bitwise_xor(me, slot)
            k = order(position // merge, count, half, False)
            start = pl.multiple_of(lax.rem(position, merge) * tokens, tokens)
            target = stage_ref.at[2, k, :, pl.ds(start, tokens)]
            own.append(pltpu.make_async_copy(ref.at[at], target, sems.at[2, slot // merge, slot % merge]))
    return begin(near) + begin(far), begin(own)


def order(k, count, half, outer):
    return jnp.where(half == (0 if outer else 1), k, count - 1 - k)


def tile_loop(rows, body):
    @pl.loop(0, rows // SUBLANES)
    def _(tile):
        body(pl.multiple_of(tile * SUBLANES, SUBLANES))


def parts(ref, k, row, strip):
    return ref[k, row, real_of(strip)], ref[k, row, imag_of(strip)]


def keep(ref, k, row, strip, value):
    ref[k, row, real_of(strip)], ref[k, row, imag_of(strip)] = value


def give_back(prod_ref, table_ref, held_ref, out_ref, sems, outer, half_blocks):
    count, rows, width = prod_ref.shape
    merge, tokens = held_ref.shape[1], held_ref.shape[3]
    half, _ = place(half_blocks)
    sent = []
    spectrum = prod_ref[...].astype(jnp.bfloat16).reshape(count * rows, width)
    for q in range(merge):
        result = back(spectrum, table_ref[q * tokens : (q + 1) * tokens])
        held_ref[:, q] = result.astype(jnp.bfloat16).reshape(count, rows, tokens)
        for k in range(count):
            block = order(k, count, half, outer)
            sent += begin(
                [pltpu.make_async_copy(held_ref.at[k, q], out_ref.at[block * merge + q], sems.at[k, q])]
            )
    end(sent)


def results(near, own, filt, half_blocks, table):
    slots = [group for group, _ in own]
    _, rows, tokens = near.shape
    size, width = table.shape
    merge = size // tokens
    count = half_blocks // merge
    filters = filt.shape[1]

    def kernel(near_ref, *refs):
        own_refs, (filt_in, table_ref, out_hbm) = refs[: len(own)], refs[len(own) : len(own) + 3]
        stage_ref, filt_ref, spec_ref, prod_ref, held_ref, out_sems = refs[len(own) + 3 :]
        half, me = place(half_blocks)
        for k in range(count):
            for q in range(merge):
                lanes = pl.ds(q * tokens, tokens)
                outer, inner = order(k, count, half, True), order(k, count, half, False)
                stage_ref[0, k, :, lanes] = near_ref[half * half_blocks + outer * merge + q]
                stage_ref[1, k, :, lanes] = near_ref[(1 - half) * half_blocks + inner * merge + q]
        for group, ref in zip(slots, own_refs):
            for at, slot in enumerate(group):
                position = jnp.bitwise_xor(me, slot)
                k = order(position // merge, count, half, False)
                start = pl.multiple_of(lax.rem(position, merge) * tokens, tokens)
                stage_ref[2, k, :, pl.ds(start, tokens)] = ref[at]
        filt_ref[...] = filt_in[...].astype(jnp.float32)
        transform(stage_ref, table_ref, spec_ref)

        def tile(first):
            row = pl.ds(first, SUBLANES)
            tap_row = pl.ds(pl.multiple_of(lax.rem(first, filters), SUBLANES), SUBLANES)
            for strip in range(size // LANES):
                taps = [parts(filt_ref, k, tap_row, strip) for k in range(2 * count)]
                near, far, own = ([parts(spec_ref.at[which], k, row, strip) for k in range(count)] for which in range(3))
                for out in range(count):
                    total = None
                    for k in range(out + 1):
                        total = add(total, times(taps[out - k], near[k]))
                    keep(prod_ref.at[0], out, row, strip, total)
                for out in range(count):
                    total = None
                    for k in range(out + 1):
                        total = add(total, conj_times(taps[out - k], own[k]))
                    for k in range(count):
                        total = add(total, conj_times(taps[count + out - k], far[k]))
                    keep(prod_ref.at[1], out, row, strip, total)

        tile_loop(rows, tile)
        spectrum = prod_ref[...].astype(jnp.bfloat16).reshape(2 * count * rows, width)
        sent = []
        for q in range(merge):
            result = back(spectrum, table_ref[q * tokens : (q + 1) * tokens]).astype(jnp.bfloat16)
            held_ref[:, :, q] = result.reshape(2, count, rows, tokens)
            for which in range(2):
                for k in range(count):
                    position = order(k, count, half, which == 0) * merge + q
                    copy = pltpu.make_async_copy(
                        held_ref.at[which, k, q], out_hbm.at[position, which], out_sems.at[which, k, q]
                    )
                    sent += begin([copy])
        end(sent)

    return call(
        kernel,
        "results",
        (near, *[array for _, array in own], filt, table),
        [jax.ShapeDtypeStruct((half_blocks, 2, rows, tokens), jnp.bfloat16)],
        [
            pltpu.VMEM((3, count, rows, size), jnp.bfloat16),
            pltpu.VMEM((2 * count, filters, width), jnp.float32),
            pltpu.VMEM((3, count, rows, width), jnp.float32),
            pltpu.VMEM((2, count, rows, width), jnp.float32),
            pltpu.VMEM((2, count, merge, rows, tokens), jnp.bfloat16),
            pltpu.SemaphoreType.DMA((2, count, merge)),
        ],
        vmem=VMEM_BYTES // 2,
        weight=HEAVY,
        space=pltpu.VMEM,
    )[0]


def lag_products(near_ref, other_ref, row_at, strip, repeats, filters, totals):
    count = near_ref.shape[0]
    sums = [None] * len(totals)
    for repeat in range(repeats):
        row = pl.ds(pl.multiple_of(repeat * filters + row_at, SUBLANES), SUBLANES)
        near = [parts(near_ref, k, row, strip) for k in range(count)]
        other = [parts(other_ref, k, row, strip) for k in range(count)]
        for at, total in enumerate(totals):
            for a in range(count):
                if 0 <= total - a < count:
                    sums[at] = add(sums[at], conj_times(near[a], other[total - a]))
    return sums


def join_lags(ref, row, joint_ref, base):
    lags, size = ref.shape[0], ref.shape[2] // 2
    sign = alternating()[:1]
    for k in range(lags):
        for strip in range(size // LANES):
            real, imag = parts(ref, k, row, strip)
            if k + 1 < lags:
                next_real, next_imag = parts(ref, k + 1, row, strip)
                real, imag = real + sign * next_imag, imag - sign * next_real
            keep(joint_ref, base + k, slice(None), strip, (real.astype(jnp.bfloat16), imag.astype(jnp.bfloat16)))


def filter_terms(near, own, filters, half_blocks, table):
    slots = [group for group, _ in own]
    _, rows, tokens = near.shape
    size, width = table.shape
    merge = size // tokens
    count = half_blocks // merge
    kept, lags = filters // 2, count * size
    repeats = rows // filters

    def kernel(near_hbm, *refs):
        own_hbm, refs = refs[: len(own)], refs[len(own) :]
        table_hbm, give_hbm, mine_hbm, theirs_hbm, stage_ref, table_ref, spec_ref, local_ref, cross_ref, joint_ref = refs[:10]
        held_ref, give_ref, mine_ref, theirs_ref, sems, stage_sems = refs[10:]
        tabled = begin([pltpu.make_async_copy(table_hbm, table_ref, sems.at[0])])
        staged, later = stage_all(near_hbm, own_hbm, slots, stage_ref, stage_sems, half_blocks)
        half, _ = place(half_blocks)
        group = lax.axis_index("dp")
        turn = jnp.where(half == 0, 1.0, -1.0).astype(jnp.float32)
        end(tabled)
        end(staged)
        end(later)
        transform(stage_ref, table_ref, spec_ref)
        near_ref, far_ref, own_ref = (spec_ref.at[which] for which in range(3))

        def local_tile(first):
            for strip in range(size // LANES):
                sums = lag_products(near_ref, own_ref, first, strip, repeats, filters, [count - 1 - k for k in range(count)])
                for k, (real, imag) in enumerate(sums):
                    keep(local_ref, k, pl.ds(first, SUBLANES), strip, (real, turn * imag))

        tile_loop(filters, local_tile)
        mine = pl.multiple_of(half * kept, SUBLANES)
        other = pl.multiple_of((1 - half) * kept, SUBLANES)
        join_lags(local_ref, pl.ds(other, kept), joint_ref, 0)
        result = back(joint_ref[:count].reshape(count * kept, width), table_ref[...]).reshape(count, kept, size)
        for k in range(count):
            give_ref[:, k * size : (k + 1) * size] = result[k].astype(jnp.bfloat16)
        sent = begin([pltpu.make_async_copy(give_ref, give_hbm, sems.at[1])])

        def cross_tile(first):
            row = pl.ds(first, SUBLANES)
            at = pl.ds(pl.multiple_of(mine + first, SUBLANES), SUBLANES)
            for strip in range(size // LANES):
                totals = [2 * count - 1 - k for k in range(1, 2 * count)]
                sums = lag_products(near_ref, far_ref, mine + first, strip, repeats, filters, totals)
                keep(cross_ref, 0, row, strip, parts(local_ref, 0, at, strip))
                for k, (real, imag) in enumerate(sums, 1):
                    value = (real, turn * imag)
                    keep(cross_ref, k, row, strip, add(value, parts(local_ref, k, at, strip)) if k < count else value)

        tile_loop(kept, cross_tile)
        join_lags(cross_ref, slice(None), joint_ref, 0)
        result = back(joint_ref[...].reshape(2 * count * kept, width), table_ref[...])
        held_ref[...] = result.reshape(2, count, kept, size)
        for k in range(count):
            columns = slice(k * size, (k + 1) * size)
            mine_ref[:, columns] = held_ref[group, k]
            theirs_ref[:, columns] = held_ref[1 - group, k].astype(jnp.bfloat16)
        sent += begin(
            [
                pltpu.make_async_copy(theirs_ref, theirs_hbm, sems.at[2]),
                pltpu.make_async_copy(mine_ref, mine_hbm, sems.at[3]),
            ]
        )
        end(sent)

    return call(
        kernel,
        "filter_terms",
        (near, *[array for _, array in own], table),
        [
            jax.ShapeDtypeStruct((kept, lags), jnp.bfloat16),
            jax.ShapeDtypeStruct((kept, lags), jnp.float32),
            jax.ShapeDtypeStruct((kept, lags), jnp.bfloat16),
        ],
        [
            pltpu.VMEM((3, count, rows, size), jnp.bfloat16),
            pltpu.VMEM(table.shape, jnp.bfloat16),
            pltpu.VMEM((3, count, rows, width), jnp.float32),
            pltpu.VMEM((count, filters, width), jnp.float32),
            pltpu.VMEM((2 * count, kept, width), jnp.float32),
            pltpu.VMEM((2 * count, kept, width), jnp.bfloat16),
            pltpu.VMEM((2, count, kept, size), jnp.float32),
            pltpu.VMEM((kept, lags), jnp.bfloat16),
            pltpu.VMEM((kept, lags), jnp.float32),
            pltpu.VMEM((kept, lags), jnp.bfloat16),
            pltpu.SemaphoreType.DMA((4,)),
            pltpu.SemaphoreType.DMA((3, count, merge)),
        ],
    )


def body(pre_gate, values, post_gate, filters, cotangent):
    blocks = lax.axis_size("ctx")
    groups = lax.axis_size("dp")
    half_blocks = blocks // 2
    local_rows, tokens = pre_gate.shape
    local_filters = filters.shape[0]
    repeats = local_rows // (local_filters * blocks)
    rows = 2 * local_filters * repeats
    table = dft_table(2 * tokens)
    arrays = (pre_gate, values, post_gate, cotangent)
    sides = [list(range(half_blocks)), list(range(half_blocks, blocks))]

    def swap(array):
        return lax.ppermute(array, "ctx", [(i, i ^ half_blocks) for i in range(blocks)])

    def other_group(array):
        return lax.ppermute(array, "dp", [(0, 1), (1, 0)])

    near, even, odd, taps = gate(arrays, filters, repeats, half_blocks)
    here = pack_taps(taps, swap(taps), half_blocks)
    odd, here = lax.optimization_barrier((odd, here))
    near = lax.all_to_all(near.reshape(blocks, rows, tokens), "ctx", split_axis=0, concat_axis=0, tiled=True)
    shape = (half_blocks // 2, rows, tokens)
    own = exchange_own(even.reshape(shape), odd.reshape(shape), half_blocks)
    filt = transform_taps(here, other_group(here), half_blocks, groups, table)

    result = results(near, own, filt, half_blocks, table)
    result, near = lax.optimization_barrier((result, near))
    returned = lax.all_to_all(
        result, "ctx", split_axis=0, concat_axis=0, tiled=True, axis_index_groups=sides
    )
    give, mine, theirs = filter_terms(near, own, 2 * local_filters, half_blocks, table)
    halves = tuple(
        lax.ppermute(give, ("dp", "ctx"), [(g * blocks + i, i ^ half_blocks) for i in range(blocks)]) for g in range(groups)
    )
    theirs = other_group(theirs)
    outputs = finish(returned.reshape(half_blocks, 2, repeats, 2, local_filters, tokens), arrays)
    mine, mixed, pre_grad, value_grad, post_grad = lax.optimization_barrier((mine, *outputs))
    filter_grad = mine + theirs.astype(jnp.float32) + (halves[0].astype(jnp.float32) + halves[1].astype(jnp.float32))
    return (mixed, pre_grad, value_grad, post_grad, filter_grad)


def matmul(left, right):
    return jnp.dot(left, right, precision=lax.Precision.HIGHEST, preferred_element_type=jnp.float32)


def contract(form, left, right):
    return jnp.einsum(
        form, left, right, precision=lax.Precision.HIGHEST, preferred_element_type=jnp.float32
    )


def phases(height, width, modulus):
    product = lax.broadcasted_iota(jnp.int32, (height, width), 0) * lax.broadcasted_iota(
        jnp.int32, (height, width), 1
    )
    return (product % modulus).astype(jnp.float32) * (2.0 * math.pi / modulus)


def build_tables(blocks, tokens):
    factor = 1
    for candidate in range(1, tokens + 1):
        if tokens % candidate == 0 and candidate * candidate <= tokens:
            factor = candidate
    second = tokens // factor
    rows = blocks + 1
    total = 2 * blocks * tokens
    first_angle = phases(rows, blocks, 2 * blocks)
    twist_angle = phases(rows, tokens, total)
    inner_angle = phases(factor, factor, factor)
    middle_angle = phases(factor, second, tokens)
    outer_angle = phases(second, second, second)
    back_angle = phases(blocks, rows, 2 * blocks)
    column = lax.broadcasted_iota(jnp.int32, (blocks, rows), 1)
    weight = jnp.where((column == 0) | (column == blocks), 1.0, 2.0).astype(jnp.float32) / total
    return {
        "first_cos": jnp.cos(first_angle),
        "first_nsin": -jnp.sin(first_angle),
        "twist_cos": jnp.cos(twist_angle),
        "twist_sin": jnp.sin(twist_angle),
        "inner_cos": jnp.cos(inner_angle),
        "inner_sin": jnp.sin(inner_angle),
        "middle_cos": jnp.cos(middle_angle),
        "middle_sin": jnp.sin(middle_angle),
        "outer_cos": jnp.cos(outer_angle),
        "outer_sin": jnp.sin(outer_angle),
        "back_cos": weight * jnp.cos(back_angle),
        "back_sin": weight * jnp.sin(back_angle),
    }


def expand(table, ndim):
    return table.reshape((table.shape[0],) + (1,) * (ndim - 2) + (table.shape[1],))


def block_table(cos_part, sin_part):
    return jnp.stack([jnp.stack([cos_part, sin_part]), jnp.stack([-sin_part, cos_part])])


def wave(real_part, imag_part, tables, sign):
    shape = real_part.shape
    factor = tables["inner_cos"].shape[0]
    second = tables["outer_cos"].shape[0]
    stacked = jnp.stack(
        [real_part.reshape(-1, factor, second), imag_part.reshape(-1, factor, second)]
    )
    inner_table = block_table(tables["inner_cos"], sign * tables["inner_sin"])
    middle = contract("prab,pqac->qrcb", stacked, inner_table)
    middle_cos = tables["middle_cos"]
    middle_sin = sign * tables["middle_sin"]
    real_turn = middle[0] * middle_cos - middle[1] * middle_sin
    imag_turn = middle[0] * middle_sin + middle[1] * middle_cos
    turned = jnp.stack([real_turn, imag_turn])
    outer_table = block_table(tables["outer_cos"], sign * tables["outer_sin"])
    result = contract("prcb,pqbd->qrdc", turned, outer_table)
    return (result[0].reshape(shape), result[1].reshape(shape))


def finish_forward(real_first, imag_first, tables):
    ndim = real_first.ndim
    twist_cos = expand(tables["twist_cos"], ndim)
    twist_sin = expand(tables["twist_sin"], ndim)
    real_twist = real_first * twist_cos + imag_first * twist_sin
    imag_twist = imag_first * twist_cos - real_first * twist_sin
    return wave(real_twist, imag_twist, tables, -1.0)


def spectrum(signal, tables):
    flat = signal.reshape(signal.shape[0], -1)
    shape = (tables["first_cos"].shape[0],) + signal.shape[1:]
    real_first = matmul(tables["first_cos"], flat).reshape(shape)
    imag_first = matmul(tables["first_nsin"], flat).reshape(shape)
    return finish_forward(real_first, imag_first, tables)


def inverse_prepare(real_spec, imag_spec, tables):
    ndim = real_spec.ndim
    real_wave, imag_wave = wave(real_spec, imag_spec, tables, 1.0)
    twist_cos = expand(tables["twist_cos"], ndim)
    twist_sin = expand(tables["twist_sin"], ndim)
    real_twist = real_wave * twist_cos - imag_wave * twist_sin
    imag_twist = real_wave * twist_sin + imag_wave * twist_cos
    rows = real_spec.shape[0]
    return (real_twist.reshape(rows, -1), imag_twist.reshape(rows, -1))


def inverse_full(real_spec, imag_spec, tables):
    real_flat, imag_flat = inverse_prepare(real_spec, imag_spec, tables)
    signal = matmul(tables["back_cos"], real_flat) - matmul(tables["back_sin"], imag_flat)
    return signal.reshape((tables["back_cos"].shape[0],) + real_spec.shape[1:])


def plain_body(pre_gate, values, post_gate, filters, cotangent):
    blocks = lax.axis_size("ctx")
    groups = lax.axis_size("dp")
    local_rows = pre_gate.shape[0]
    tokens = pre_gate.shape[1]
    local_filters = filters.shape[0]
    repeats = local_rows // (local_filters * blocks)
    share = blocks // groups
    tables = build_tables(blocks, tokens)
    gated = (pre_gate.astype(jnp.float32) * values.astype(jnp.float32)).astype(jnp.bfloat16)
    conv_grad = (cotangent.astype(jnp.float32) * post_gate.astype(jnp.float32)).astype(jnp.bfloat16)
    gated_blocks = gated.reshape(repeats, blocks, local_filters, tokens)
    grad_blocks = conv_grad.reshape(repeats, blocks, local_filters, tokens)
    tap_local = jnp.transpose(filters.reshape(local_filters, share, tokens), (1, 0, 2))
    piece = lax.all_gather(tap_local, "dp", axis=0, tiled=True)
    count = piece.shape[0]
    flat = piece.reshape(count, -1)
    cos_cols = tables["first_cos"]
    sin_cols = tables["first_nsin"]
    real_first = matmul(cos_cols, flat)
    imag_first = matmul(sin_cols, flat)
    spec_shape = (blocks + 1, 1, local_filters, tokens)
    filt_real, filt_imag = finish_forward(
        real_first.reshape(spec_shape), imag_first.reshape(spec_shape), tables
    )

    def single_spectrum(received):
        signal = received.reshape(blocks, -1, received.shape[2], received.shape[3])
        return spectrum(signal.astype(jnp.float32), tables)

    gated_real, gated_imag = single_spectrum(
        lax.all_to_all(gated_blocks, "ctx", split_axis=1, concat_axis=0, tiled=True)
    )
    prod_real = gated_real * filt_real - gated_imag * filt_imag
    prod_imag = gated_real * filt_imag + gated_imag * filt_real
    result = inverse_full(prod_real, prod_imag, tables).astype(jnp.bfloat16)
    conv_chan = result.reshape(blocks * repeats, 1, local_filters, tokens)
    conv_seq = lax.all_to_all(conv_chan, "ctx", split_axis=0, concat_axis=1, tiled=True)
    grad_real, grad_imag = single_spectrum(
        lax.all_to_all(grad_blocks, "ctx", split_axis=1, concat_axis=0, tiled=True)
    )
    prod_real = filt_real * grad_real + filt_imag * grad_imag
    prod_imag = filt_real * grad_imag - filt_imag * grad_real
    result = inverse_full(prod_real, prod_imag, tables).astype(jnp.bfloat16)
    gated_chan_grad = result.reshape(blocks * repeats, 1, local_filters, tokens)
    gated_seq_grad = lax.all_to_all(gated_chan_grad, "ctx", split_axis=0, concat_axis=1, tiled=True)
    cross_real = jnp.sum(gated_real * grad_real + gated_imag * grad_imag, axis=1)
    cross_imag = jnp.sum(gated_real * grad_imag - gated_imag * grad_real, axis=1)
    wave_real, wave_imag = inverse_prepare(cross_real, cross_imag, tables)
    cos_rows = tables["back_cos"]
    sin_rows = tables["back_sin"]
    term = matmul(cos_rows, wave_real) - matmul(sin_rows, wave_imag)
    summed = lax.psum_scatter(
        term.reshape(lax.axis_size("dp") * share, local_filters, tokens).astype(jnp.bfloat16),
        "dp",
        scatter_dimension=0,
        tiled=True,
    ).astype(jnp.float32)
    filter_grad = jnp.transpose(summed, (1, 0, 2)).reshape(local_filters, share * tokens)
    conv_full = conv_seq.reshape(pre_gate.shape).astype(jnp.float32)
    gated_grad = gated_seq_grad.reshape(pre_gate.shape).astype(jnp.float32)
    mixed = (post_gate.astype(jnp.float32) * conv_full).astype(jnp.bfloat16)
    post_grad = (cotangent.astype(jnp.float32) * conv_full).astype(jnp.bfloat16)
    pre_grad = (gated_grad * values.astype(jnp.float32)).astype(jnp.bfloat16)
    value_grad = (gated_grad * pre_gate.astype(jnp.float32)).astype(jnp.bfloat16)
    return (mixed, pre_grad, value_grad, post_grad, filter_grad)


def solution(mesh):
    placed = (P("dp", "ctx"), P("dp", "ctx"), P("dp", "ctx"), P("ctx", "dp"), P("dp", "ctx"))
    groups, blocks = mesh.shape["dp"], mesh.shape["ctx"]

    def program(pre_gate, values, post_gate, filters, cotangent):
        kernels = groups == 2 and blocks >= 8 and blocks & (blocks - 1) == 0 and filters.shape[0] % 16 == 0
        return (body if kernels else plain_body)(pre_gate, values, post_gate, filters, cotangent)

    return jax.shard_map(
        program,
        mesh=mesh,
        in_specs=placed,
        out_specs=(P("dp", "ctx"), P("dp", "ctx"), P("dp", "ctx"), P("dp", "ctx"), P("ctx", "dp")),
        check_vma=False,
    )
```

```python
import math

import jax
import jax.numpy as jnp
import numpy as np
from jax import lax
from jax.experimental import pallas as pl
from jax.experimental.pallas import tpu as pltpu
from jax.sharding import PartitionSpec as P


LANES = 128
SUBLANES = 8
VMEM_BYTES = 60 * 1024 * 1024
HEAVY = 1 << 37


def dft_table(size):
    angle = np.arange(size)[:, None] * (2.0 * np.arange(size)[None, :] + 1.0) * (math.pi / (2 * size))
    strips = size // LANES
    cos, sin = (part.reshape(size, strips, 1, LANES) for part in (np.cos(angle), np.sin(angle)))
    return jnp.asarray(np.concatenate([cos, -sin], axis=2).reshape(size, 2 * size), jnp.bfloat16)


def dot(left, right):
    return jnp.dot(left, right, preferred_element_type=jnp.float32)


def back(spectrum, table):
    result = lax.dot_general(spectrum, table, (((1,), (1,)), ((), ())), preferred_element_type=jnp.float32)
    return result * (2.0 / table.shape[1])


def alternating():
    odd = lax.broadcasted_iota(jnp.int32, (SUBLANES, LANES), 1) % 2
    return 1.0 - 2.0 * odd.astype(jnp.float32)


def place(half_blocks):
    index = lax.axis_index("ctx")
    return index // half_blocks, lax.rem(index, half_blocks)


def real_of(strip):
    return pl.ds(2 * strip * LANES, LANES)


def imag_of(strip):
    return pl.ds((2 * strip + 1) * LANES, LANES)


def begin(copies):
    for copy in copies:
        copy.start()
    return copies


def end(copies):
    for copy in copies:
        copy.wait()


def call(kernel, name, operands, outputs, scratch, weight=1, vmem=VMEM_BYTES, space=pltpu.HBM):
    hbm = pl.BlockSpec(memory_space=pltpu.HBM)
    return pl.pallas_call(
        kernel,
        in_specs=[pl.BlockSpec(memory_space=space)] * len(operands),
        out_specs=[hbm] * len(outputs),
        out_shape=outputs,
        scratch_shapes=scratch,
        compiler_params=pltpu.CompilerParams(vmem_limit_bytes=vmem),
        cost_estimate=pl.CostEstimate(flops=weight, bytes_accessed=weight, transcendentals=0),
        name=name,
    )(*operands)


def gate(near, arrays, filters, repeats, half_blocks):
    rows_all, tokens = arrays[0].shape
    rows = rows_all // repeats
    share = rows // (2 * half_blocks)
    piece = (repeats, 2, share, tokens)

    def kernel(pre_ref, value_ref, post_ref, cot_ref, *refs):
        if near:
            filt_ref, out_ref, taps_ref, left_ref, right_ref, result_ref, in_sems, out_sems, filt_in, taps_out, taps_sems = refs
            loaded = begin([pltpu.make_async_copy(filt_ref, filt_in, taps_sems.at[0])])
        else:
            even_ref, odd_ref, left_ref, right_ref, result_ref, in_sems, out_sems = refs
        half, me = place(half_blocks)
        use_gated = half == 0 if near else half != 0

        def fetch(r, left, right):
            at = pl.ds(r * rows, rows)
            return (
                pltpu.make_async_copy(left.at[at], left_ref.at[r], in_sems.at[0, r]),
                pltpu.make_async_copy(right.at[at], right_ref.at[r], in_sems.at[1, r]),
            )

        @pl.when(use_gated)
        def _():
            for r in range(repeats):
                begin(fetch(r, pre_ref, value_ref))

        @pl.when(jnp.logical_not(use_gated))
        def _():
            for r in range(repeats):
                begin(fetch(r, cot_ref, post_ref))

        sent = []
        for r in range(repeats):
            end(fetch(r, pre_ref, value_ref))
            product = left_ref[r].astype(jnp.float32) * right_ref[r].astype(jnp.float32)
            product = product.astype(jnp.bfloat16).reshape(2, half_blocks, share, tokens)
            for side in range(2):
                result_ref[:, r, side] = product[side]
            for to in range(2 if near else 0):
                sent += begin([pltpu.make_async_copy(result_ref.at[:, r], out_ref.at[to, :, r], out_sems.at[to, r])])
        if near:
            end(loaded)
            taps_out[...] = filt_in[...].astype(jnp.bfloat16)
            sent += begin([pltpu.make_async_copy(taps_out, taps_ref, taps_sems.at[1])])
        else:
            for at in range(half_blocks // 2):
                for odd, target in enumerate((even_ref, odd_ref)):
                    source = result_ref.at[jnp.bitwise_xor(me, 2 * at + odd)]
                    sent += begin([pltpu.make_async_copy(source, target.at[at], out_sems.at[odd, at])])
        end(sent)

    own_shape = jax.ShapeDtypeStruct((half_blocks // 2, *piece), jnp.bfloat16)
    near_shape = jax.ShapeDtypeStruct((2, half_blocks, *piece), jnp.bfloat16)
    scratch = [
        pltpu.VMEM((repeats, rows, tokens), jnp.bfloat16),
        pltpu.VMEM((repeats, rows, tokens), jnp.bfloat16),
        pltpu.VMEM((half_blocks, *piece), jnp.bfloat16),
        pltpu.SemaphoreType.DMA((2, repeats)),
        pltpu.SemaphoreType.DMA((2, repeats if near else half_blocks // 2)),
    ]
    if near:
        scratch += [
            pltpu.VMEM(filters.shape, filters.dtype),
            pltpu.VMEM(filters.shape, jnp.bfloat16),
            pltpu.SemaphoreType.DMA((2,)),
        ]
    return call(
        kernel,
        "gate_near" if near else "gate_own",
        (*arrays, filters) if near else arrays,
        [near_shape, jax.ShapeDtypeStruct(filters.shape, jnp.bfloat16)] if near else [own_shape, own_shape],
        scratch,
    )


def exchange_own(even, odd, half_blocks):
    def swap(array, slot):
        return lax.ppermute(array, "ctx", [(i, i ^ slot) for i in range(2 * half_blocks)])

    odd = swap(odd, 1)
    groups = [([0], even[:1]), ([1], odd[:1])]
    for at in range(1, half_blocks // 2):
        pair = jnp.concatenate([even[at : at + 1], odd[at : at + 1]])
        groups.append(([2 * at, 2 * at + 1], swap(pair, 2 * at)))
    return groups


def finish(returned, arrays):
    half_blocks, _, repeats, sides, share, tokens = returned.shape
    count, rows = repeats * sides, half_blocks * share

    def kernel(recv_ref, pre_ref, value_ref, post_ref, cot_ref, *refs):
        out_refs, (held_ref, sems) = refs[:4], refs[4:]
        half, _ = place(half_blocks)
        sent = []
        for part in range(count):
            r, side = part // sides, part % sides
            at = pl.ds(part * rows, rows)
            conv = recv_ref[:, half, r, side].reshape(rows, tokens).astype(jnp.float32)
            grad = recv_ref[:, 1 - half, r, side].reshape(rows, tokens).astype(jnp.float32)
            for which, (factor_ref, result) in enumerate(
                ((post_ref, conv), (value_ref, grad), (pre_ref, grad), (cot_ref, conv))
            ):
                held_ref[which, part] = (factor_ref[at].astype(jnp.float32) * result).astype(jnp.bfloat16)
                sent += begin(
                    [pltpu.make_async_copy(held_ref.at[which, part], out_refs[which].at[at], sems.at[which, part])]
                )
        end(sent)

    shapes = [jax.ShapeDtypeStruct(arrays[0].shape, jnp.bfloat16)] * 4
    return pl.pallas_call(
        kernel,
        in_specs=[pl.BlockSpec(memory_space=pltpu.VMEM)] * 5,
        out_specs=[pl.BlockSpec(memory_space=pltpu.HBM)] * 4,
        out_shape=shapes,
        scratch_shapes=[
            pltpu.VMEM((4, count, rows, tokens), jnp.bfloat16),
            pltpu.SemaphoreType.DMA((4, count)),
        ],
        compiler_params=pltpu.CompilerParams(vmem_limit_bytes=VMEM_BYTES // 6),
        name="finish",
    )(returned, *arrays)


def pack_taps(taps, pair, half_blocks):
    share, lags = taps.shape

    def kernel(taps_ref, pair_ref, out_ref, held_ref, sems):
        half, _ = place(half_blocks)
        end(
            begin(
                [
                    pltpu.make_async_copy(taps_ref, held_ref.at[half], sems.at[0]),
                    pltpu.make_async_copy(pair_ref, held_ref.at[1 - half], sems.at[1]),
                ]
            )
        )
        end(begin([pltpu.make_async_copy(held_ref, out_ref, sems.at[2])]))

    return call(
        kernel,
        "pack_taps",
        (taps, pair),
        [jax.ShapeDtypeStruct((2, share, lags), jnp.bfloat16)],
        [pltpu.VMEM((2, share, lags), jnp.bfloat16), pltpu.SemaphoreType.DMA((3,))],
        weight=HEAVY,
        vmem=VMEM_BYTES // 12,
    )[0]


def transform_taps(here, there, half_blocks, groups, table):
    sides, share, lags = here.shape
    size = table.shape[0]
    count = groups * lags // size
    rows, width = sides * share, 2 * size

    def kernel(here_ref, there_ref, table_hbm, out_hbm, piece_ref, table_ref, stage_ref, out_ref, sems):
        sources = (here_ref, there_ref)
        loads = begin([pltpu.make_async_copy(ref, piece_ref.at[at], sems.at[at]) for at, ref in enumerate(sources)])
        tabled = begin([pltpu.make_async_copy(table_hbm, table_ref, sems.at[2])])
        half, _ = place(half_blocks)
        group = lax.axis_index("dp")
        end(loads)
        for at in range(2):
            first = (group if at == 0 else 1 - group) * (lags // size)
            for side in range(sides):
                for k in range(lags // size):
                    piece = piece_ref[at, side, :, k * size : (k + 1) * size]
                    stage_ref[first + k, side * share : (side + 1) * share] = piece
        end(tabled)
        spectrum = dot(stage_ref[...].reshape(count * rows, size), table_ref[...]).reshape(count, rows, width)
        turn = jnp.where(half == 0, 1.0, -1.0).astype(jnp.float32)
        sign = alternating()[:1]
        sent = []
        for k in range(count):
            for strip in range(size // LANES):
                re = slice(2 * strip * LANES, (2 * strip + 1) * LANES)
                im = slice((2 * strip + 1) * LANES, (2 * strip + 2) * LANES)
                real, imag = spectrum[k, :, re], spectrum[k, :, im]
                if k > 0:
                    real, imag = real - sign * spectrum[k - 1, :, im], imag + sign * spectrum[k - 1, :, re]
                out_ref[k, :, re] = real.astype(jnp.bfloat16)
                out_ref[k, :, im] = (turn * imag).astype(jnp.bfloat16)
            sent += begin([pltpu.make_async_copy(out_ref.at[k], out_hbm.at[k], sems.at[3 + k])])
        end(sent)

    return call(
        kernel,
        "taps",
        (here, there, table),
        [jax.ShapeDtypeStruct((count, rows, width), jnp.bfloat16)],
        [
            pltpu.VMEM((2, sides, share, lags), jnp.bfloat16),
            pltpu.VMEM((size, width), jnp.bfloat16),
            pltpu.VMEM((count, rows, size), jnp.bfloat16),
            pltpu.VMEM((count, rows, width), jnp.bfloat16),
            pltpu.SemaphoreType.DMA((3 + count,)),
        ],
        vmem=VMEM_BYTES // 6,
    )[0]


def add(total, term):
    return term if total is None else (total[0] + term[0], total[1] + term[1])


def times(a, b):
    return a[0] * b[0] - a[1] * b[1], a[0] * b[1] + a[1] * b[0]


def conj_times(a, b):
    return a[0] * b[0] + a[1] * b[1], a[0] * b[1] - a[1] * b[0]


def transform(stage_ref, table_ref, spec_ref):
    width = spec_ref.shape[-1]
    staged = stage_ref[...].reshape(-1, stage_ref.shape[-1])
    for strip in range(width // (2 * LANES)):
        columns = slice(2 * strip * LANES, 2 * (strip + 1) * LANES)
        spec_ref[..., columns] = dot(staged, table_ref[:, columns]).reshape(spec_ref.shape[:-1] + (2 * LANES,))


def stage_all(near_ref, own_refs, slots, stage_ref, half_blocks):
    _, count, _, size = stage_ref.shape
    tokens = near_ref.shape[2]
    merge = size // tokens
    half, me = place(half_blocks)
    for k in range(count):
        outer, inner = order(k, count, half, True), order(k, count, half, False)
        for q in range(merge):
            lanes = pl.ds(q * tokens, tokens)
            stage_ref[0, k, :, lanes] = near_ref[half * half_blocks + outer * merge + q]
            stage_ref[1, k, :, lanes] = near_ref[(1 - half) * half_blocks + inner * merge + q]
    for group, ref in zip(slots, own_refs):
        for at, slot in enumerate(group):
            position = jnp.bitwise_xor(me, slot)
            k = order(position // merge, count, half, False)
            start = pl.multiple_of(lax.rem(position, merge) * tokens, tokens)
            stage_ref[2, k, :, pl.ds(start, tokens)] = ref[at]


def order(k, count, half, outer):
    return jnp.where(half == (0 if outer else 1), k, count - 1 - k)


def tile_loop(rows, body):
    @pl.loop(0, rows // SUBLANES)
    def _(tile):
        body(pl.multiple_of(tile * SUBLANES, SUBLANES))


def parts(ref, k, row, strip):
    return ref[k, row, real_of(strip)], ref[k, row, imag_of(strip)]


def keep(ref, k, row, strip, value):
    ref[k, row, real_of(strip)], ref[k, row, imag_of(strip)] = value


def give_back(prod_ref, table_ref, held_ref, out_ref, sems, outer, half_blocks):
    count, rows, width = prod_ref.shape
    merge, tokens = held_ref.shape[1], held_ref.shape[3]
    half, _ = place(half_blocks)
    sent = []
    spectrum = prod_ref[...].astype(jnp.bfloat16).reshape(count * rows, width)
    for q in range(merge):
        result = back(spectrum, table_ref[q * tokens : (q + 1) * tokens])
        held_ref[:, q] = result.astype(jnp.bfloat16).reshape(count, rows, tokens)
        for k in range(count):
            block = order(k, count, half, outer)
            sent += begin(
                [pltpu.make_async_copy(held_ref.at[k, q], out_ref.at[block * merge + q], sems.at[k, q])]
            )
    end(sent)


def results(near, own, filt, half_blocks, table):
    slots = [group for group, _ in own]
    _, rows, tokens = near.shape
    size, width = table.shape
    merge = size // tokens
    count = half_blocks // merge
    filters = filt.shape[1]

    def kernel(near_ref, *refs):
        own_refs, (filt_in, table_ref, out_hbm) = refs[: len(own)], refs[len(own) : len(own) + 3]
        stage_ref, filt_ref, spec_ref, prod_ref, held_ref, out_sems = refs[len(own) + 3 :]
        stage_all(near_ref, own_refs, slots, stage_ref, half_blocks)
        filt_ref[...] = filt_in[...].astype(jnp.float32)
        transform(stage_ref, table_ref, spec_ref)
        half, _ = place(half_blocks)

        def tile(first):
            row = pl.ds(first, SUBLANES)
            tap_row = pl.ds(pl.multiple_of(lax.rem(first, filters), SUBLANES), SUBLANES)
            for strip in range(size // LANES):
                taps = [parts(filt_ref, k, tap_row, strip) for k in range(2 * count)]
                near, far, own = ([parts(spec_ref.at[which], k, row, strip) for k in range(count)] for which in range(3))
                for out in range(count):
                    total = None
                    for k in range(out + 1):
                        total = add(total, times(taps[out - k], near[k]))
                    keep(prod_ref.at[0], out, row, strip, total)
                for out in range(count):
                    total = None
                    for k in range(out + 1):
                        total = add(total, conj_times(taps[out - k], own[k]))
                    for k in range(count):
                        total = add(total, conj_times(taps[count + out - k], far[k]))
                    keep(prod_ref.at[1], out, row, strip, total)

        tile_loop(rows, tile)
        spectrum = prod_ref[...].astype(jnp.bfloat16).reshape(2 * count * rows, width)
        sent = []
        for q in range(merge):
            result = back(spectrum, table_ref[q * tokens : (q + 1) * tokens]).astype(jnp.bfloat16)
            held_ref[:, :, q] = result.reshape(2, count, rows, tokens)
            for which in range(2):
                for k in range(count):
                    position = order(k, count, half, which == 0) * merge + q
                    copy = pltpu.make_async_copy(
                        held_ref.at[which, k, q], out_hbm.at[position, which], out_sems.at[which, k, q]
                    )
                    sent += begin([copy])
        end(sent)

    return call(
        kernel,
        "results",
        (near, *[array for _, array in own], filt, table),
        [jax.ShapeDtypeStruct((half_blocks, 2, rows, tokens), jnp.bfloat16)],
        [
            pltpu.VMEM((3, count, rows, size), jnp.bfloat16),
            pltpu.VMEM((2 * count, filters, width), jnp.float32),
            pltpu.VMEM((3, count, rows, width), jnp.float32),
            pltpu.VMEM((2, count, rows, width), jnp.float32),
            pltpu.VMEM((2, count, merge, rows, tokens), jnp.bfloat16),
            pltpu.SemaphoreType.DMA((2, count, merge)),
        ],
        vmem=VMEM_BYTES // 2,
        weight=HEAVY,
        space=pltpu.VMEM,
    )[0]


def lag_products(near_ref, other_ref, row_at, strip, repeats, filters, totals):
    count = near_ref.shape[0]
    sums = [None] * len(totals)
    for repeat in range(repeats):
        row = pl.ds(pl.multiple_of(repeat * filters + row_at, SUBLANES), SUBLANES)
        near = [parts(near_ref, k, row, strip) for k in range(count)]
        other = [parts(other_ref, k, row, strip) for k in range(count)]
        for at, total in enumerate(totals):
            for a in range(count):
                if 0 <= total - a < count:
                    sums[at] = add(sums[at], conj_times(near[a], other[total - a]))
    return sums


def join_lags(ref, row, joint_ref, base):
    lags, size = ref.shape[0], ref.shape[2] // 2
    sign = alternating()[:1]
    for k in range(lags):
        for strip in range(size // LANES):
            real, imag = parts(ref, k, row, strip)
            if k + 1 < lags:
                next_real, next_imag = parts(ref, k + 1, row, strip)
                real, imag = real + sign * next_imag, imag - sign * next_real
            keep(joint_ref, base + k, slice(None), strip, (real.astype(jnp.bfloat16), imag.astype(jnp.bfloat16)))


def filter_terms(near, own, filters, half_blocks, table):
    slots = [group for group, _ in own]
    _, rows, tokens = near.shape
    size, width = table.shape
    merge = size // tokens
    count = half_blocks // merge
    kept, lags = filters // 2, count * size
    repeats = rows // filters

    def kernel(near_ref, *refs):
        own_refs, refs = refs[: len(own)], refs[len(own) :]
        table_ref, give_hbm, mine_hbm, theirs_hbm, stage_ref, spec_ref, local_ref, cross_ref, joint_ref = refs[:9]
        held_ref, give_ref, mine_ref, theirs_ref, sems = refs[9:]
        half, _ = place(half_blocks)
        group = lax.axis_index("dp")
        turn = jnp.where(half == 0, 1.0, -1.0).astype(jnp.float32)
        stage_all(near_ref, own_refs, slots, stage_ref, half_blocks)
        transform(stage_ref, table_ref, spec_ref)
        near_spec, far_spec, own_spec = (spec_ref.at[which] for which in range(3))

        def local_tile(first):
            for strip in range(size // LANES):
                sums = lag_products(near_spec, own_spec, first, strip, repeats, filters, [count - 1 - k for k in range(count)])
                for k, (real, imag) in enumerate(sums):
                    keep(local_ref, k, pl.ds(first, SUBLANES), strip, (real, turn * imag))

        tile_loop(filters, local_tile)
        mine = pl.multiple_of(half * kept, SUBLANES)
        other = pl.multiple_of((1 - half) * kept, SUBLANES)
        join_lags(local_ref, pl.ds(other, kept), joint_ref, 0)
        result = back(joint_ref[:count].reshape(count * kept, width), table_ref[...]).reshape(count, kept, size)
        for k in range(count):
            give_ref[:, k * size : (k + 1) * size] = result[k].astype(jnp.bfloat16)
        sent = begin([pltpu.make_async_copy(give_ref, give_hbm, sems.at[1])])

        def cross_tile(first):
            row = pl.ds(first, SUBLANES)
            at = pl.ds(pl.multiple_of(mine + first, SUBLANES), SUBLANES)
            for strip in range(size // LANES):
                totals = [2 * count - 1 - k for k in range(1, 2 * count)]
                sums = lag_products(near_spec, far_spec, mine + first, strip, repeats, filters, totals)
                keep(cross_ref, 0, row, strip, parts(local_ref, 0, at, strip))
                for k, (real, imag) in enumerate(sums, 1):
                    value = (real, turn * imag)
                    keep(cross_ref, k, row, strip, add(value, parts(local_ref, k, at, strip)) if k < count else value)

        tile_loop(kept, cross_tile)
        join_lags(cross_ref, slice(None), joint_ref, 0)
        result = back(joint_ref[...].reshape(2 * count * kept, width), table_ref[...])
        held_ref[...] = result.reshape(2, count, kept, size)
        for k in range(count):
            columns = slice(k * size, (k + 1) * size)
            mine_ref[:, columns] = held_ref[group, k]
            theirs_ref[:, columns] = held_ref[1 - group, k].astype(jnp.bfloat16)
        sent += begin(
            [
                pltpu.make_async_copy(theirs_ref, theirs_hbm, sems.at[2]),
                pltpu.make_async_copy(mine_ref, mine_hbm, sems.at[3]),
            ]
        )
        end(sent)

    return call(
        kernel,
        "filter_terms",
        (near, *[array for _, array in own], table),
        [
            jax.ShapeDtypeStruct((kept, lags), jnp.bfloat16),
            jax.ShapeDtypeStruct((kept, lags), jnp.float32),
            jax.ShapeDtypeStruct((kept, lags), jnp.bfloat16),
        ],
        [
            pltpu.VMEM((3, count, rows, size), jnp.bfloat16),
            pltpu.VMEM((3, count, rows, width), jnp.float32),
            pltpu.VMEM((count, filters, width), jnp.float32),
            pltpu.VMEM((2 * count, kept, width), jnp.float32),
            pltpu.VMEM((2 * count, kept, width), jnp.bfloat16),
            pltpu.VMEM((2, count, kept, size), jnp.float32),
            pltpu.VMEM((kept, lags), jnp.bfloat16),
            pltpu.VMEM((kept, lags), jnp.float32),
            pltpu.VMEM((kept, lags), jnp.bfloat16),
            pltpu.SemaphoreType.DMA((4,)),
        ],
        vmem=VMEM_BYTES - (5 << 20),
        space=pltpu.VMEM,
    )


def body(pre_gate, values, post_gate, filters, cotangent):
    blocks = lax.axis_size("ctx")
    groups = lax.axis_size("dp")
    half_blocks = blocks // 2
    local_rows, tokens = pre_gate.shape
    local_filters = filters.shape[0]
    repeats = local_rows // (local_filters * blocks)
    rows = 2 * local_filters * repeats
    table = dft_table(2 * tokens)
    arrays = (pre_gate, values, post_gate, cotangent)
    sides = [list(range(half_blocks)), list(range(half_blocks, blocks))]

    def swap(array):
        return lax.ppermute(array, "ctx", [(i, i ^ half_blocks) for i in range(blocks)])

    def other_group(array):
        return lax.ppermute(array, "dp", [(0, 1), (1, 0)])

    near, taps = gate(True, arrays, filters, repeats, half_blocks)
    even, odd = gate(False, arrays, filters, repeats, half_blocks)
    here = pack_taps(taps, swap(taps), half_blocks)
    odd, here = lax.optimization_barrier((odd, here))
    near = lax.all_to_all(near.reshape(blocks, rows, tokens), "ctx", split_axis=0, concat_axis=0, tiled=True)
    shape = (half_blocks // 2, rows, tokens)
    own = exchange_own(even.reshape(shape), odd.reshape(shape), half_blocks)
    filt = transform_taps(here, other_group(here), half_blocks, groups, table)

    result = results(near, own, filt, half_blocks, table)
    result, near = lax.optimization_barrier((result, near))
    returned = lax.all_to_all(
        result, "ctx", split_axis=0, concat_axis=0, tiled=True, axis_index_groups=sides
    )
    give, mine, theirs = filter_terms(near, own, 2 * local_filters, half_blocks, table)
    halves = tuple(
        lax.ppermute(give, ("dp", "ctx"), [(g * blocks + i, i ^ half_blocks) for i in range(blocks)]) for g in range(groups)
    )
    theirs = other_group(theirs)
    outputs = finish(returned.reshape(half_blocks, 2, repeats, 2, local_filters, tokens), arrays)
    mine, mixed, pre_grad, value_grad, post_grad = lax.optimization_barrier((mine, *outputs))
    filter_grad = mine + (halves[1].astype(jnp.float32) + halves[0].astype(jnp.float32)) + theirs.astype(jnp.float32)
    return (mixed, pre_grad, value_grad, post_grad, filter_grad)


def matmul(left, right):
    return jnp.dot(left, right, precision=lax.Precision.HIGHEST, preferred_element_type=jnp.float32)


def contract(form, left, right):
    return jnp.einsum(
        form, left, right, precision=lax.Precision.HIGHEST, preferred_element_type=jnp.float32
    )


def phases(height, width, modulus):
    product = lax.broadcasted_iota(jnp.int32, (height, width), 0) * lax.broadcasted_iota(
        jnp.int32, (height, width), 1
    )
    return (product % modulus).astype(jnp.float32) * (2.0 * math.pi / modulus)


def build_tables(blocks, tokens):
    factor = 1
    for candidate in range(1, tokens + 1):
        if tokens % candidate == 0 and candidate * candidate <= tokens:
            factor = candidate
    second = tokens // factor
    rows = blocks + 1
    total = 2 * blocks * tokens
    first_angle = phases(rows, blocks, 2 * blocks)
    twist_angle = phases(rows, tokens, total)
    inner_angle = phases(factor, factor, factor)
    middle_angle = phases(factor, second, tokens)
    outer_angle = phases(second, second, second)
    back_angle = phases(blocks, rows, 2 * blocks)
    column = lax.broadcasted_iota(jnp.int32, (blocks, rows), 1)
    weight = jnp.where((column == 0) | (column == blocks), 1.0, 2.0).astype(jnp.float32) / total
    return {
        "first_cos": jnp.cos(first_angle),
        "first_nsin": -jnp.sin(first_angle),
        "twist_cos": jnp.cos(twist_angle),
        "twist_sin": jnp.sin(twist_angle),
        "inner_cos": jnp.cos(inner_angle),
        "inner_sin": jnp.sin(inner_angle),
        "middle_cos": jnp.cos(middle_angle),
        "middle_sin": jnp.sin(middle_angle),
        "outer_cos": jnp.cos(outer_angle),
        "outer_sin": jnp.sin(outer_angle),
        "back_cos": weight * jnp.cos(back_angle),
        "back_sin": weight * jnp.sin(back_angle),
    }


def expand(table, ndim):
    return table.reshape((table.shape[0],) + (1,) * (ndim - 2) + (table.shape[1],))


def block_table(cos_part, sin_part):
    return jnp.stack([jnp.stack([cos_part, sin_part]), jnp.stack([-sin_part, cos_part])])


def wave(real_part, imag_part, tables, sign):
    shape = real_part.shape
    factor = tables["inner_cos"].shape[0]
    second = tables["outer_cos"].shape[0]
    stacked = jnp.stack(
        [real_part.reshape(-1, factor, second), imag_part.reshape(-1, factor, second)]
    )
    inner_table = block_table(tables["inner_cos"], sign * tables["inner_sin"])
    middle = contract("prab,pqac->qrcb", stacked, inner_table)
    middle_cos = tables["middle_cos"]
    middle_sin = sign * tables["middle_sin"]
    real_turn = middle[0] * middle_cos - middle[1] * middle_sin
    imag_turn = middle[0] * middle_sin + middle[1] * middle_cos
    turned = jnp.stack([real_turn, imag_turn])
    outer_table = block_table(tables["outer_cos"], sign * tables["outer_sin"])
    result = contract("prcb,pqbd->qrdc", turned, outer_table)
    return (result[0].reshape(shape), result[1].reshape(shape))


def finish_forward(real_first, imag_first, tables):
    ndim = real_first.ndim
    twist_cos = expand(tables["twist_cos"], ndim)
    twist_sin = expand(tables["twist_sin"], ndim)
    real_twist = real_first * twist_cos + imag_first * twist_sin
    imag_twist = imag_first * twist_cos - real_first * twist_sin
    return wave(real_twist, imag_twist, tables, -1.0)


def spectrum(signal, tables):
    flat = signal.reshape(signal.shape[0], -1)
    shape = (tables["first_cos"].shape[0],) + signal.shape[1:]
    real_first = matmul(tables["first_cos"], flat).reshape(shape)
    imag_first = matmul(tables["first_nsin"], flat).reshape(shape)
    return finish_forward(real_first, imag_first, tables)


def inverse_prepare(real_spec, imag_spec, tables):
    ndim = real_spec.ndim
    real_wave, imag_wave = wave(real_spec, imag_spec, tables, 1.0)
    twist_cos = expand(tables["twist_cos"], ndim)
    twist_sin = expand(tables["twist_sin"], ndim)
    real_twist = real_wave * twist_cos - imag_wave * twist_sin
    imag_twist = real_wave * twist_sin + imag_wave * twist_cos
    rows = real_spec.shape[0]
    return (real_twist.reshape(rows, -1), imag_twist.reshape(rows, -1))


def inverse_full(real_spec, imag_spec, tables):
    real_flat, imag_flat = inverse_prepare(real_spec, imag_spec, tables)
    signal = matmul(tables["back_cos"], real_flat) - matmul(tables["back_sin"], imag_flat)
    return signal.reshape((tables["back_cos"].shape[0],) + real_spec.shape[1:])


def plain_body(pre_gate, values, post_gate, filters, cotangent):
    blocks = lax.axis_size("ctx")
    groups = lax.axis_size("dp")
    local_rows = pre_gate.shape[0]
    tokens = pre_gate.shape[1]
    local_filters = filters.shape[0]
    repeats = local_rows // (local_filters * blocks)
    share = blocks // groups
    tables = build_tables(blocks, tokens)
    gated = (pre_gate.astype(jnp.float32) * values.astype(jnp.float32)).astype(jnp.bfloat16)
    conv_grad = (cotangent.astype(jnp.float32) * post_gate.astype(jnp.float32)).astype(jnp.bfloat16)
    gated_blocks = gated.reshape(repeats, blocks, local_filters, tokens)
    grad_blocks = conv_grad.reshape(repeats, blocks, local_filters, tokens)
    tap_local = jnp.transpose(filters.reshape(local_filters, share, tokens), (1, 0, 2))
    piece = lax.all_gather(tap_local, "dp", axis=0, tiled=True)
    count = piece.shape[0]
    flat = piece.reshape(count, -1)
    cos_cols = tables["first_cos"]
    sin_cols = tables["first_nsin"]
    real_first = matmul(cos_cols, flat)
    imag_first = matmul(sin_cols, flat)
    spec_shape = (blocks + 1, 1, local_filters, tokens)
    filt_real, filt_imag = finish_forward(
        real_first.reshape(spec_shape), imag_first.reshape(spec_shape), tables
    )

    def single_spectrum(received):
        signal = received.reshape(blocks, -1, received.shape[2], received.shape[3])
        return spectrum(signal.astype(jnp.float32), tables)

    gated_real, gated_imag = single_spectrum(
        lax.all_to_all(gated_blocks, "ctx", split_axis=1, concat_axis=0, tiled=True)
    )
    prod_real = gated_real * filt_real - gated_imag * filt_imag
    prod_imag = gated_real * filt_imag + gated_imag * filt_real
    result = inverse_full(prod_real, prod_imag, tables).astype(jnp.bfloat16)
    conv_chan = result.reshape(blocks * repeats, 1, local_filters, tokens)
    conv_seq = lax.all_to_all(conv_chan, "ctx", split_axis=0, concat_axis=1, tiled=True)
    grad_real, grad_imag = single_spectrum(
        lax.all_to_all(grad_blocks, "ctx", split_axis=1, concat_axis=0, tiled=True)
    )
    prod_real = filt_real * grad_real + filt_imag * grad_imag
    prod_imag = filt_real * grad_imag - filt_imag * grad_real
    result = inverse_full(prod_real, prod_imag, tables).astype(jnp.bfloat16)
    gated_chan_grad = result.reshape(blocks * repeats, 1, local_filters, tokens)
    gated_seq_grad = lax.all_to_all(gated_chan_grad, "ctx", split_axis=0, concat_axis=1, tiled=True)
    cross_real = jnp.sum(gated_real * grad_real + gated_imag * grad_imag, axis=1)
    cross_imag = jnp.sum(gated_real * grad_imag - gated_imag * grad_real, axis=1)
    wave_real, wave_imag = inverse_prepare(cross_real, cross_imag, tables)
    cos_rows = tables["back_cos"]
    sin_rows = tables["back_sin"]
    term = matmul(cos_rows, wave_real) - matmul(sin_rows, wave_imag)
    summed = lax.psum_scatter(
        term.reshape(lax.axis_size("dp") * share, local_filters, tokens).astype(jnp.bfloat16),
        "dp",
        scatter_dimension=0,
        tiled=True,
    ).astype(jnp.float32)
    filter_grad = jnp.transpose(summed, (1, 0, 2)).reshape(local_filters, share * tokens)
    conv_full = conv_seq.reshape(pre_gate.shape).astype(jnp.float32)
    gated_grad = gated_seq_grad.reshape(pre_gate.shape).astype(jnp.float32)
    mixed = (post_gate.astype(jnp.float32) * conv_full).astype(jnp.bfloat16)
    post_grad = (cotangent.astype(jnp.float32) * conv_full).astype(jnp.bfloat16)
    pre_grad = (gated_grad * values.astype(jnp.float32)).astype(jnp.bfloat16)
    value_grad = (gated_grad * pre_gate.astype(jnp.float32)).astype(jnp.bfloat16)
    return (mixed, pre_grad, value_grad, post_grad, filter_grad)


def solution(mesh):
    placed = (P("dp", "ctx"), P("dp", "ctx"), P("dp", "ctx"), P("ctx", "dp"), P("dp", "ctx"))
    groups, blocks = mesh.shape["dp"], mesh.shape["ctx"]

    def program(pre_gate, values, post_gate, filters, cotangent):
        kernels = groups == 2 and blocks >= 8 and blocks & (blocks - 1) == 0 and filters.shape[0] % 16 == 0
        return (body if kernels else plain_body)(pre_gate, values, post_gate, filters, cotangent)

    return jax.shard_map(
        program,
        mesh=mesh,
        in_specs=placed,
        out_specs=(P("dp", "ctx"), P("dp", "ctx"), P("dp", "ctx"), P("dp", "ctx"), P("ctx", "dp")),
        check_vma=False,
    )
```

```python
import math

import jax
import jax.numpy as jnp
import numpy as np
from jax import lax
from jax.experimental import pallas as pl
from jax.experimental.pallas import tpu as pltpu
from jax.sharding import PartitionSpec as P


LANES = 128
SUBLANES = 8
VMEM_BYTES = 60 * 1024 * 1024
HEAVY = 1 << 37


def dft_table(size):
    angle = np.arange(size)[:, None] * (2.0 * np.arange(size)[None, :] + 1.0) * (math.pi / (2 * size))
    strips = size // LANES
    cos, sin = (part.reshape(size, strips, 1, LANES) for part in (np.cos(angle), np.sin(angle)))
    return jnp.asarray(np.concatenate([cos, -sin], axis=2).reshape(size, 2 * size), jnp.bfloat16)


def dot(left, right):
    return jnp.dot(left, right, preferred_element_type=jnp.float32)


def back(spectrum, table):
    result = lax.dot_general(spectrum, table, (((1,), (1,)), ((), ())), preferred_element_type=jnp.float32)
    return result * (2.0 / table.shape[1])


def alternating():
    odd = lax.broadcasted_iota(jnp.int32, (SUBLANES, LANES), 1) % 2
    return 1.0 - 2.0 * odd.astype(jnp.float32)


def place(half_blocks):
    index = lax.axis_index("ctx")
    return index // half_blocks, lax.rem(index, half_blocks)


def real_of(strip):
    return pl.ds(2 * strip * LANES, LANES)


def imag_of(strip):
    return pl.ds((2 * strip + 1) * LANES, LANES)


def begin(copies):
    for copy in copies:
        copy.start()
    return copies


def end(copies):
    for copy in copies:
        copy.wait()


def call(kernel, name, operands, outputs, scratch, weight=1, vmem=VMEM_BYTES, space=pltpu.HBM):
    hbm = pl.BlockSpec(memory_space=pltpu.HBM)
    return pl.pallas_call(
        kernel,
        in_specs=[pl.BlockSpec(memory_space=space)] * len(operands),
        out_specs=[hbm] * len(outputs),
        out_shape=outputs,
        scratch_shapes=scratch,
        compiler_params=pltpu.CompilerParams(vmem_limit_bytes=vmem),
        cost_estimate=pl.CostEstimate(flops=weight, bytes_accessed=weight, transcendentals=0),
        name=name,
    )(*operands)


def gate(near, arrays, filters, repeats, half_blocks):
    rows_all, tokens = arrays[0].shape
    rows = rows_all // repeats
    share = rows // (2 * half_blocks)
    piece = (repeats, 2, share, tokens)

    def kernel(pre_ref, value_ref, post_ref, cot_ref, *refs):
        if near:
            filt_ref, out_ref, taps_ref, left_ref, right_ref, result_ref, in_sems, out_sems, filt_in, taps_out, taps_sems = refs
            loaded = begin([pltpu.make_async_copy(filt_ref, filt_in, taps_sems.at[0])])
        else:
            even_ref, odd_ref, left_ref, right_ref, result_ref, in_sems, out_sems = refs
        half, me = place(half_blocks)
        use_gated = half == 0 if near else half != 0

        def fetch(r, left, right):
            at = pl.ds(r * rows, rows)
            return (
                pltpu.make_async_copy(left.at[at], left_ref.at[r], in_sems.at[0, r]),
                pltpu.make_async_copy(right.at[at], right_ref.at[r], in_sems.at[1, r]),
            )

        @pl.when(use_gated)
        def _():
            for r in range(repeats):
                begin(fetch(r, pre_ref, value_ref))

        @pl.when(jnp.logical_not(use_gated))
        def _():
            for r in range(repeats):
                begin(fetch(r, cot_ref, post_ref))

        sent = []
        for r in range(repeats):
            end(fetch(r, pre_ref, value_ref))
            product = left_ref[r].astype(jnp.float32) * right_ref[r].astype(jnp.float32)
            product = product.astype(jnp.bfloat16).reshape(2, half_blocks, share, tokens)
            for side in range(2):
                result_ref[:, r, side] = product[side]
            for to in range(2 if near else 0):
                sent += begin([pltpu.make_async_copy(result_ref.at[:, r], out_ref.at[to, :, r], out_sems.at[to, r])])
        if near:
            end(loaded)
            taps_out[...] = filt_in[...].astype(jnp.bfloat16)
            sent += begin([pltpu.make_async_copy(taps_out, taps_ref, taps_sems.at[1])])
        else:
            for at in range(half_blocks // 2):
                for odd, target in enumerate((even_ref, odd_ref)):
                    source = result_ref.at[jnp.bitwise_xor(me, 2 * at + odd)]
                    sent += begin([pltpu.make_async_copy(source, target.at[at], out_sems.at[odd, at])])
        end(sent)

    own_shape = jax.ShapeDtypeStruct((half_blocks // 2, *piece), jnp.bfloat16)
    near_shape = jax.ShapeDtypeStruct((2, half_blocks, *piece), jnp.bfloat16)
    scratch = [
        pltpu.VMEM((repeats, rows, tokens), jnp.bfloat16),
        pltpu.VMEM((repeats, rows, tokens), jnp.bfloat16),
        pltpu.VMEM((half_blocks, *piece), jnp.bfloat16),
        pltpu.SemaphoreType.DMA((2, repeats)),
        pltpu.SemaphoreType.DMA((2, repeats if near else half_blocks // 2)),
    ]
    if near:
        scratch += [
            pltpu.VMEM(filters.shape, filters.dtype),
            pltpu.VMEM(filters.shape, jnp.bfloat16),
            pltpu.SemaphoreType.DMA((2,)),
        ]
    return call(
        kernel,
        "gate_near" if near else "gate_own",
        (*arrays, filters) if near else arrays,
        [near_shape, jax.ShapeDtypeStruct(filters.shape, jnp.bfloat16)] if near else [own_shape, own_shape],
        scratch,
    )


def exchange_own(even, odd, half_blocks):
    def swap(array, slot):
        return lax.ppermute(array, "ctx", [(i, i ^ slot) for i in range(2 * half_blocks)])

    odd = swap(odd, 1)
    groups = [([0], even[:1]), ([1], odd[:1])]
    for at in range(1, half_blocks // 2):
        pair = jnp.concatenate([even[at : at + 1], odd[at : at + 1]])
        groups.append(([2 * at, 2 * at + 1], swap(pair, 2 * at)))
    return groups


def finish(returned, arrays):
    half_blocks, _, repeats, sides, share, tokens = returned.shape
    count, rows = repeats * sides, half_blocks * share

    def kernel(recv_ref, pre_ref, value_ref, post_ref, cot_ref, *refs):
        out_refs, (held_ref, sems) = refs[:4], refs[4:]
        half, _ = place(half_blocks)
        sent = []
        for part in range(count):
            r, side = part // sides, part % sides
            at = pl.ds(part * rows, rows)
            conv = recv_ref[:, half, r, side].reshape(rows, tokens).astype(jnp.float32)
            grad = recv_ref[:, 1 - half, r, side].reshape(rows, tokens).astype(jnp.float32)
            for which, (factor_ref, result) in enumerate(
                ((post_ref, conv), (value_ref, grad), (pre_ref, grad), (cot_ref, conv))
            ):
                held_ref[which, part] = (factor_ref[at].astype(jnp.float32) * result).astype(jnp.bfloat16)
                sent += begin(
                    [pltpu.make_async_copy(held_ref.at[which, part], out_refs[which].at[at], sems.at[which, part])]
                )
        end(sent)

    shapes = [jax.ShapeDtypeStruct(arrays[0].shape, jnp.bfloat16)] * 4
    return pl.pallas_call(
        kernel,
        in_specs=[pl.BlockSpec(memory_space=pltpu.VMEM)] * 5,
        out_specs=[pl.BlockSpec(memory_space=pltpu.HBM)] * 4,
        out_shape=shapes,
        scratch_shapes=[
            pltpu.VMEM((4, count, rows, tokens), jnp.bfloat16),
            pltpu.SemaphoreType.DMA((4, count)),
        ],
        compiler_params=pltpu.CompilerParams(vmem_limit_bytes=VMEM_BYTES // 6),
        name="finish",
    )(returned, *arrays)


def pack_taps(taps, pair, half_blocks):
    share, lags = taps.shape

    def kernel(taps_ref, pair_ref, out_ref, held_ref, sems):
        half, _ = place(half_blocks)
        end(
            begin(
                [
                    pltpu.make_async_copy(taps_ref, held_ref.at[half], sems.at[0]),
                    pltpu.make_async_copy(pair_ref, held_ref.at[1 - half], sems.at[1]),
                ]
            )
        )
        end(begin([pltpu.make_async_copy(held_ref, out_ref, sems.at[2])]))

    return call(
        kernel,
        "pack_taps",
        (taps, pair),
        [jax.ShapeDtypeStruct((2, share, lags), jnp.bfloat16)],
        [pltpu.VMEM((2, share, lags), jnp.bfloat16), pltpu.SemaphoreType.DMA((3,))],
        weight=HEAVY,
        vmem=VMEM_BYTES // 12,
    )[0]


def transform_taps(here, there, half_blocks, groups, table):
    sides, share, lags = here.shape
    size = table.shape[0]
    count = groups * lags // size
    rows, width = sides * share, 2 * size

    def kernel(here_ref, there_ref, table_hbm, out_hbm, piece_ref, table_ref, stage_ref, out_ref, sems):
        sources = (here_ref, there_ref)
        loads = begin([pltpu.make_async_copy(ref, piece_ref.at[at], sems.at[at]) for at, ref in enumerate(sources)])
        tabled = begin([pltpu.make_async_copy(table_hbm, table_ref, sems.at[2])])
        half, _ = place(half_blocks)
        group = lax.axis_index("dp")
        end(loads)
        for at in range(2):
            first = (group if at == 0 else 1 - group) * (lags // size)
            for side in range(sides):
                for k in range(lags // size):
                    piece = piece_ref[at, side, :, k * size : (k + 1) * size]
                    stage_ref[first + k, side * share : (side + 1) * share] = piece
        end(tabled)
        spectrum = dot(stage_ref[...].reshape(count * rows, size), table_ref[...]).reshape(count, rows, width)
        turn = jnp.where(half == 0, 1.0, -1.0).astype(jnp.float32)
        sign = alternating()[:1]
        sent = []
        for k in range(count):
            for strip in range(size // LANES):
                re = slice(2 * strip * LANES, (2 * strip + 1) * LANES)
                im = slice((2 * strip + 1) * LANES, (2 * strip + 2) * LANES)
                real, imag = spectrum[k, :, re], spectrum[k, :, im]
                if k > 0:
                    real, imag = real - sign * spectrum[k - 1, :, im], imag + sign * spectrum[k - 1, :, re]
                out_ref[k, :, re] = real.astype(jnp.bfloat16)
                out_ref[k, :, im] = (turn * imag).astype(jnp.bfloat16)
            sent += begin([pltpu.make_async_copy(out_ref.at[k], out_hbm.at[k], sems.at[3 + k])])
        end(sent)

    return call(
        kernel,
        "taps",
        (here, there, table),
        [jax.ShapeDtypeStruct((count, rows, width), jnp.bfloat16)],
        [
            pltpu.VMEM((2, sides, share, lags), jnp.bfloat16),
            pltpu.VMEM((size, width), jnp.bfloat16),
            pltpu.VMEM((count, rows, size), jnp.bfloat16),
            pltpu.VMEM((count, rows, width), jnp.bfloat16),
            pltpu.SemaphoreType.DMA((3 + count,)),
        ],
        vmem=VMEM_BYTES // 6,
    )[0]


def add(total, term):
    return term if total is None else (total[0] + term[0], total[1] + term[1])


def times(a, b):
    return a[0] * b[0] - a[1] * b[1], a[0] * b[1] + a[1] * b[0]


def conj_times(a, b):
    return a[0] * b[0] + a[1] * b[1], a[0] * b[1] - a[1] * b[0]


def transform(stage_ref, table_ref, spec_ref):
    width = spec_ref.shape[-1]
    staged = stage_ref[...].reshape(-1, stage_ref.shape[-1])
    for strip in range(width // (2 * LANES)):
        columns = slice(2 * strip * LANES, 2 * (strip + 1) * LANES)
        spec_ref[..., columns] = dot(staged, table_ref[:, columns]).reshape(spec_ref.shape[:-1] + (2 * LANES,))


def stage_all(near_ref, own_refs, slots, near_stage, far_stage, own_stage, half_blocks, far_rows):
    count, _, size = near_stage.shape
    tokens = near_ref.shape[2]
    merge = size // tokens
    half, me = place(half_blocks)
    for k in range(count):
        outer, inner = order(k, count, half, True), order(k, count, half, False)
        for q in range(merge):
            lanes = pl.ds(q * tokens, tokens)
            near_stage[k, :, lanes] = near_ref[half * half_blocks + outer * merge + q]
            at = 0
            for first, rows in far_rows:
                far = near_ref[(1 - half) * half_blocks + inner * merge + q, pl.ds(first, rows)]
                far_stage[k, at : at + rows, lanes] = far
                at += rows
    for group, ref in zip(slots, own_refs):
        for at, slot in enumerate(group):
            position = jnp.bitwise_xor(me, slot)
            k = order(position // merge, count, half, False)
            start = pl.multiple_of(lax.rem(position, merge) * tokens, tokens)
            own_stage[k, :, pl.ds(start, tokens)] = ref[at]


def order(k, count, half, outer):
    return jnp.where(half == (0 if outer else 1), k, count - 1 - k)


def tile_loop(rows, body):
    @pl.loop(0, rows // SUBLANES)
    def _(tile):
        body(pl.multiple_of(tile * SUBLANES, SUBLANES))


def parts(ref, k, row, strip):
    return ref[k, row, real_of(strip)], ref[k, row, imag_of(strip)]


def keep(ref, k, row, strip, value):
    ref[k, row, real_of(strip)], ref[k, row, imag_of(strip)] = value


def give_back(prod_ref, table_ref, held_ref, out_ref, sems, outer, half_blocks):
    count, rows, width = prod_ref.shape
    merge, tokens = held_ref.shape[1], held_ref.shape[3]
    half, _ = place(half_blocks)
    sent = []
    spectrum = prod_ref[...].astype(jnp.bfloat16).reshape(count * rows, width)
    for q in range(merge):
        result = back(spectrum, table_ref[q * tokens : (q + 1) * tokens])
        held_ref[:, q] = result.astype(jnp.bfloat16).reshape(count, rows, tokens)
        for k in range(count):
            block = order(k, count, half, outer)
            sent += begin(
                [pltpu.make_async_copy(held_ref.at[k, q], out_ref.at[block * merge + q], sems.at[k, q])]
            )
    end(sent)


def results(near, own, filt, half_blocks, table):
    slots = [group for group, _ in own]
    _, rows, tokens = near.shape
    size, width = table.shape
    merge = size // tokens
    count = half_blocks // merge
    filters = filt.shape[1]

    def kernel(near_ref, *refs):
        own_refs, (filt_in, table_ref, out_hbm) = refs[: len(own)], refs[len(own) : len(own) + 3]
        stage_ref, filt_ref, spec_ref, prod_ref, held_ref, out_sems = refs[len(own) + 3 :]
        near_stage, far_stage, own_stage = (stage_ref.at[which] for which in range(3))
        stage_all(near_ref, own_refs, slots, near_stage, far_stage, own_stage, half_blocks, [(0, rows)])
        filt_ref[...] = filt_in[...].astype(jnp.float32)
        transform(stage_ref, table_ref, spec_ref)
        half, _ = place(half_blocks)

        def tile(first):
            row = pl.ds(first, SUBLANES)
            tap_row = pl.ds(pl.multiple_of(lax.rem(first, filters), SUBLANES), SUBLANES)
            for strip in range(size // LANES):
                taps = [parts(filt_ref, k, tap_row, strip) for k in range(2 * count)]
                near, far, own = ([parts(spec_ref.at[which], k, row, strip) for k in range(count)] for which in range(3))
                for out in range(count):
                    total = None
                    for k in range(out + 1):
                        total = add(total, times(taps[out - k], near[k]))
                    keep(prod_ref.at[0], out, row, strip, total)
                for out in range(count):
                    total = None
                    for k in range(out + 1):
                        total = add(total, conj_times(taps[out - k], own[k]))
                    for k in range(count):
                        total = add(total, conj_times(taps[count + out - k], far[k]))
                    keep(prod_ref.at[1], out, row, strip, total)

        tile_loop(rows, tile)
        spectrum = prod_ref[...].astype(jnp.bfloat16).reshape(2 * count * rows, width)
        sent = []
        for q in range(merge):
            result = back(spectrum, table_ref[q * tokens : (q + 1) * tokens]).astype(jnp.bfloat16)
            held_ref[:, :, q] = result.reshape(2, count, rows, tokens)
            for which in range(2):
                for k in range(count):
                    position = order(k, count, half, which == 0) * merge + q
                    copy = pltpu.make_async_copy(
                        held_ref.at[which, k, q], out_hbm.at[position, which], out_sems.at[which, k, q]
                    )
                    sent += begin([copy])
        end(sent)

    return call(
        kernel,
        "results",
        (near, *[array for _, array in own], filt, table),
        [jax.ShapeDtypeStruct((half_blocks, 2, rows, tokens), jnp.bfloat16)],
        [
            pltpu.VMEM((3, count, rows, size), jnp.bfloat16),
            pltpu.VMEM((2 * count, filters, width), jnp.float32),
            pltpu.VMEM((3, count, rows, width), jnp.float32),
            pltpu.VMEM((2, count, rows, width), jnp.float32),
            pltpu.VMEM((2, count, merge, rows, tokens), jnp.bfloat16),
            pltpu.SemaphoreType.DMA((2, count, merge)),
        ],
        vmem=VMEM_BYTES // 2,
        weight=HEAVY,
        space=pltpu.VMEM,
    )[0]


def lag_products(near_ref, near_rows, other_ref, other_rows, strip, totals):
    count = near_ref.shape[0]
    sums = [None] * len(totals)
    for near_row, other_row in zip(near_rows, other_rows):
        near = [parts(near_ref, k, pl.ds(near_row, SUBLANES), strip) for k in range(count)]
        other = [parts(other_ref, k, pl.ds(other_row, SUBLANES), strip) for k in range(count)]
        for at, total in enumerate(totals):
            for a in range(count):
                if 0 <= total - a < count:
                    sums[at] = add(sums[at], conj_times(near[a], other[total - a]))
    return sums


def repeat_rows(first, step, repeats):
    return [pl.multiple_of(r * step + first, SUBLANES) for r in range(repeats)]


def join_lags(ref, row, joint_ref, base):
    lags, size = ref.shape[0], ref.shape[2] // 2
    sign = alternating()[:1]
    for k in range(lags):
        for strip in range(size // LANES):
            real, imag = parts(ref, k, row, strip)
            if k + 1 < lags:
                next_real, next_imag = parts(ref, k + 1, row, strip)
                real, imag = real + sign * next_imag, imag - sign * next_real
            keep(joint_ref, base + k, slice(None), strip, (real.astype(jnp.bfloat16), imag.astype(jnp.bfloat16)))


def filter_terms(near, own, filters, half_blocks, table):
    slots = [group for group, _ in own]
    _, rows, tokens = near.shape
    size, width = table.shape
    merge = size // tokens
    count = half_blocks // merge
    kept, lags = filters // 2, count * size
    repeats = rows // filters

    def kernel(near_ref, *refs):
        own_refs, refs = refs[: len(own)], refs[len(own) :]
        table_ref, give_hbm, mine_hbm, theirs_hbm, stage_ref, far_stage, spec_ref, far_ref, local_ref, cross_ref, joint_ref = refs[:11]
        held_ref, give_ref, mine_ref, theirs_ref, sems = refs[11:]
        half, _ = place(half_blocks)
        group = lax.axis_index("dp")
        turn = jnp.where(half == 0, 1.0, -1.0).astype(jnp.float32)
        mine = pl.multiple_of(half * kept, SUBLANES)
        other = pl.multiple_of((1 - half) * kept, SUBLANES)
        far_rows = [(pl.multiple_of(r * filters + half * kept, kept), kept) for r in range(repeats)]
        stage_all(near_ref, own_refs, slots, stage_ref.at[0], far_stage, stage_ref.at[1], half_blocks, far_rows)
        transform(stage_ref, table_ref, spec_ref)
        transform(far_stage, table_ref, far_ref)
        near_spec, own_spec = spec_ref.at[0], spec_ref.at[1]

        def local_tile(first):
            rows_at = repeat_rows(first, filters, repeats)
            for strip in range(size // LANES):
                totals = [count - 1 - k for k in range(count)]
                sums = lag_products(near_spec, rows_at, own_spec, rows_at, strip, totals)
                for k, (real, imag) in enumerate(sums):
                    keep(local_ref, k, pl.ds(first, SUBLANES), strip, (real, turn * imag))

        tile_loop(filters, local_tile)

        def cross_tile(first):
            row = pl.ds(first, SUBLANES)
            at = pl.ds(pl.multiple_of(mine + first, SUBLANES), SUBLANES)
            near_at, far_at = repeat_rows(mine + first, filters, repeats), repeat_rows(first, kept, repeats)
            for strip in range(size // LANES):
                totals = [2 * count - 1 - k for k in range(1, 2 * count)]
                sums = lag_products(near_spec, near_at, far_ref, far_at, strip, totals)
                keep(cross_ref, 0, row, strip, parts(local_ref, 0, at, strip))
                for k, (real, imag) in enumerate(sums, 1):
                    value = (real, turn * imag)
                    keep(cross_ref, k, row, strip, add(value, parts(local_ref, k, at, strip)) if k < count else value)

        tile_loop(kept, cross_tile)
        join_lags(cross_ref, slice(None), joint_ref, 0)
        join_lags(local_ref, pl.ds(other, kept), joint_ref, 2 * count)
        result = back(joint_ref[...].reshape(3 * count * kept, width), table_ref[...]).reshape(3, count, kept, size)
        held_ref[...] = result[:2]
        for k in range(count):
            give_ref[:, k * size : (k + 1) * size] = result[2, k].astype(jnp.bfloat16)
        sent = begin([pltpu.make_async_copy(give_ref, give_hbm, sems.at[1])])
        for k in range(count):
            columns = slice(k * size, (k + 1) * size)
            mine_ref[:, columns] = held_ref[group, k]
            theirs_ref[:, columns] = held_ref[1 - group, k].astype(jnp.bfloat16)
        sent += begin(
            [
                pltpu.make_async_copy(theirs_ref, theirs_hbm, sems.at[2]),
                pltpu.make_async_copy(mine_ref, mine_hbm, sems.at[3]),
            ]
        )
        end(sent)

    return call(
        kernel,
        "filter_terms",
        (near, *[array for _, array in own], table),
        [
            jax.ShapeDtypeStruct((kept, lags), jnp.bfloat16),
            jax.ShapeDtypeStruct((kept, lags), jnp.float32),
            jax.ShapeDtypeStruct((kept, lags), jnp.bfloat16),
        ],
        [
            pltpu.VMEM((2, count, rows, size), jnp.bfloat16),
            pltpu.VMEM((count, rows // 2, size), jnp.bfloat16),
            pltpu.VMEM((2, count, rows, width), jnp.float32),
            pltpu.VMEM((count, rows // 2, width), jnp.float32),
            pltpu.VMEM((count, filters, width), jnp.float32),
            pltpu.VMEM((2 * count, kept, width), jnp.float32),
            pltpu.VMEM((3 * count, kept, width), jnp.bfloat16),
            pltpu.VMEM((2, count, kept, size), jnp.float32),
            pltpu.VMEM((kept, lags), jnp.bfloat16),
            pltpu.VMEM((kept, lags), jnp.float32),
            pltpu.VMEM((kept, lags), jnp.bfloat16),
            pltpu.SemaphoreType.DMA((4,)),
        ],
        vmem=VMEM_BYTES - (5 << 20),
        space=pltpu.VMEM,
    )


def body(pre_gate, values, post_gate, filters, cotangent):
    blocks = lax.axis_size("ctx")
    groups = lax.axis_size("dp")
    half_blocks = blocks // 2
    local_rows, tokens = pre_gate.shape
    local_filters = filters.shape[0]
    repeats = local_rows // (local_filters * blocks)
    rows = 2 * local_filters * repeats
    table = dft_table(2 * tokens)
    arrays = (pre_gate, values, post_gate, cotangent)
    sides = [list(range(half_blocks)), list(range(half_blocks, blocks))]

    def swap(array):
        return lax.ppermute(array, "ctx", [(i, i ^ half_blocks) for i in range(blocks)])

    def other_group(array):
        return lax.ppermute(array, "dp", [(0, 1), (1, 0)])

    near, taps = gate(True, arrays, filters, repeats, half_blocks)
    even, odd = gate(False, arrays, filters, repeats, half_blocks)
    here = pack_taps(taps, swap(taps), half_blocks)
    odd, here = lax.optimization_barrier((odd, here))
    near = lax.all_to_all(near.reshape(blocks, rows, tokens), "ctx", split_axis=0, concat_axis=0, tiled=True)
    shape = (half_blocks // 2, rows, tokens)
    own = exchange_own(even.reshape(shape), odd.reshape(shape), half_blocks)
    filt = transform_taps(here, other_group(here), half_blocks, groups, table)

    result = results(near, own, filt, half_blocks, table)
    result, near = lax.optimization_barrier((result, near))
    returned = lax.all_to_all(
        result, "ctx", split_axis=0, concat_axis=0, tiled=True, axis_index_groups=sides
    )
    give, mine, theirs = filter_terms(near, own, 2 * local_filters, half_blocks, table)
    halves = tuple(
        lax.ppermute(give, ("dp", "ctx"), [(g * blocks + i, i ^ half_blocks) for i in range(blocks)]) for g in range(groups)
    )
    theirs = other_group(theirs)
    outputs = finish(returned.reshape(half_blocks, 2, repeats, 2, local_filters, tokens), arrays)
    mine, mixed, pre_grad, value_grad, post_grad = lax.optimization_barrier((mine, *outputs))
    filter_grad = mine + (halves[1].astype(jnp.float32) + halves[0].astype(jnp.float32)) + theirs.astype(jnp.float32)
    return (mixed, pre_grad, value_grad, post_grad, filter_grad)


def matmul(left, right):
    return jnp.dot(left, right, precision=lax.Precision.HIGHEST, preferred_element_type=jnp.float32)


def contract(form, left, right):
    return jnp.einsum(
        form, left, right, precision=lax.Precision.HIGHEST, preferred_element_type=jnp.float32
    )


def phases(height, width, modulus):
    product = lax.broadcasted_iota(jnp.int32, (height, width), 0) * lax.broadcasted_iota(
        jnp.int32, (height, width), 1
    )
    return (product % modulus).astype(jnp.float32) * (2.0 * math.pi / modulus)


def build_tables(blocks, tokens):
    factor = 1
    for candidate in range(1, tokens + 1):
        if tokens % candidate == 0 and candidate * candidate <= tokens:
            factor = candidate
    second = tokens // factor
    rows = blocks + 1
    total = 2 * blocks * tokens
    first_angle = phases(rows, blocks, 2 * blocks)
    twist_angle = phases(rows, tokens, total)
    inner_angle = phases(factor, factor, factor)
    middle_angle = phases(factor, second, tokens)
    outer_angle = phases(second, second, second)
    back_angle = phases(blocks, rows, 2 * blocks)
    column = lax.broadcasted_iota(jnp.int32, (blocks, rows), 1)
    weight = jnp.where((column == 0) | (column == blocks), 1.0, 2.0).astype(jnp.float32) / total
    return {
        "first_cos": jnp.cos(first_angle),
        "first_nsin": -jnp.sin(first_angle),
        "twist_cos": jnp.cos(twist_angle),
        "twist_sin": jnp.sin(twist_angle),
        "inner_cos": jnp.cos(inner_angle),
        "inner_sin": jnp.sin(inner_angle),
        "middle_cos": jnp.cos(middle_angle),
        "middle_sin": jnp.sin(middle_angle),
        "outer_cos": jnp.cos(outer_angle),
        "outer_sin": jnp.sin(outer_angle),
        "back_cos": weight * jnp.cos(back_angle),
        "back_sin": weight * jnp.sin(back_angle),
    }


def expand(table, ndim):
    return table.reshape((table.shape[0],) + (1,) * (ndim - 2) + (table.shape[1],))


def block_table(cos_part, sin_part):
    return jnp.stack([jnp.stack([cos_part, sin_part]), jnp.stack([-sin_part, cos_part])])


def wave(real_part, imag_part, tables, sign):
    shape = real_part.shape
    factor = tables["inner_cos"].shape[0]
    second = tables["outer_cos"].shape[0]
    stacked = jnp.stack(
        [real_part.reshape(-1, factor, second), imag_part.reshape(-1, factor, second)]
    )
    inner_table = block_table(tables["inner_cos"], sign * tables["inner_sin"])
    middle = contract("prab,pqac->qrcb", stacked, inner_table)
    middle_cos = tables["middle_cos"]
    middle_sin = sign * tables["middle_sin"]
    real_turn = middle[0] * middle_cos - middle[1] * middle_sin
    imag_turn = middle[0] * middle_sin + middle[1] * middle_cos
    turned = jnp.stack([real_turn, imag_turn])
    outer_table = block_table(tables["outer_cos"], sign * tables["outer_sin"])
    result = contract("prcb,pqbd->qrdc", turned, outer_table)
    return (result[0].reshape(shape), result[1].reshape(shape))


def finish_forward(real_first, imag_first, tables):
    ndim = real_first.ndim
    twist_cos = expand(tables["twist_cos"], ndim)
    twist_sin = expand(tables["twist_sin"], ndim)
    real_twist = real_first * twist_cos + imag_first * twist_sin
    imag_twist = imag_first * twist_cos - real_first * twist_sin
    return wave(real_twist, imag_twist, tables, -1.0)


def spectrum(signal, tables):
    flat = signal.reshape(signal.shape[0], -1)
    shape = (tables["first_cos"].shape[0],) + signal.shape[1:]
    real_first = matmul(tables["first_cos"], flat).reshape(shape)
    imag_first = matmul(tables["first_nsin"], flat).reshape(shape)
    return finish_forward(real_first, imag_first, tables)


def inverse_prepare(real_spec, imag_spec, tables):
    ndim = real_spec.ndim
    real_wave, imag_wave = wave(real_spec, imag_spec, tables, 1.0)
    twist_cos = expand(tables["twist_cos"], ndim)
    twist_sin = expand(tables["twist_sin"], ndim)
    real_twist = real_wave * twist_cos - imag_wave * twist_sin
    imag_twist = real_wave * twist_sin + imag_wave * twist_cos
    rows = real_spec.shape[0]
    return (real_twist.reshape(rows, -1), imag_twist.reshape(rows, -1))


def inverse_full(real_spec, imag_spec, tables):
    real_flat, imag_flat = inverse_prepare(real_spec, imag_spec, tables)
    signal = matmul(tables["back_cos"], real_flat) - matmul(tables["back_sin"], imag_flat)
    return signal.reshape((tables["back_cos"].shape[0],) + real_spec.shape[1:])


def plain_body(pre_gate, values, post_gate, filters, cotangent):
    blocks = lax.axis_size("ctx")
    groups = lax.axis_size("dp")
    local_rows = pre_gate.shape[0]
    tokens = pre_gate.shape[1]
    local_filters = filters.shape[0]
    repeats = local_rows // (local_filters * blocks)
    share = blocks // groups
    tables = build_tables(blocks, tokens)
    gated = (pre_gate.astype(jnp.float32) * values.astype(jnp.float32)).astype(jnp.bfloat16)
    conv_grad = (cotangent.astype(jnp.float32) * post_gate.astype(jnp.float32)).astype(jnp.bfloat16)
    gated_blocks = gated.reshape(repeats, blocks, local_filters, tokens)
    grad_blocks = conv_grad.reshape(repeats, blocks, local_filters, tokens)
    tap_local = jnp.transpose(filters.reshape(local_filters, share, tokens), (1, 0, 2))
    piece = lax.all_gather(tap_local, "dp", axis=0, tiled=True)
    count = piece.shape[0]
    flat = piece.reshape(count, -1)
    cos_cols = tables["first_cos"]
    sin_cols = tables["first_nsin"]
    real_first = matmul(cos_cols, flat)
    imag_first = matmul(sin_cols, flat)
    spec_shape = (blocks + 1, 1, local_filters, tokens)
    filt_real, filt_imag = finish_forward(
        real_first.reshape(spec_shape), imag_first.reshape(spec_shape), tables
    )

    def single_spectrum(received):
        signal = received.reshape(blocks, -1, received.shape[2], received.shape[3])
        return spectrum(signal.astype(jnp.float32), tables)

    gated_real, gated_imag = single_spectrum(
        lax.all_to_all(gated_blocks, "ctx", split_axis=1, concat_axis=0, tiled=True)
    )
    prod_real = gated_real * filt_real - gated_imag * filt_imag
    prod_imag = gated_real * filt_imag + gated_imag * filt_real
    result = inverse_full(prod_real, prod_imag, tables).astype(jnp.bfloat16)
    conv_chan = result.reshape(blocks * repeats, 1, local_filters, tokens)
    conv_seq = lax.all_to_all(conv_chan, "ctx", split_axis=0, concat_axis=1, tiled=True)
    grad_real, grad_imag = single_spectrum(
        lax.all_to_all(grad_blocks, "ctx", split_axis=1, concat_axis=0, tiled=True)
    )
    prod_real = filt_real * grad_real + filt_imag * grad_imag
    prod_imag = filt_real * grad_imag - filt_imag * grad_real
    result = inverse_full(prod_real, prod_imag, tables).astype(jnp.bfloat16)
    gated_chan_grad = result.reshape(blocks * repeats, 1, local_filters, tokens)
    gated_seq_grad = lax.all_to_all(gated_chan_grad, "ctx", split_axis=0, concat_axis=1, tiled=True)
    cross_real = jnp.sum(gated_real * grad_real + gated_imag * grad_imag, axis=1)
    cross_imag = jnp.sum(gated_real * grad_imag - gated_imag * grad_real, axis=1)
    wave_real, wave_imag = inverse_prepare(cross_real, cross_imag, tables)
    cos_rows = tables["back_cos"]
    sin_rows = tables["back_sin"]
    term = matmul(cos_rows, wave_real) - matmul(sin_rows, wave_imag)
    summed = lax.psum_scatter(
        term.reshape(lax.axis_size("dp") * share, local_filters, tokens).astype(jnp.bfloat16),
        "dp",
        scatter_dimension=0,
        tiled=True,
    ).astype(jnp.float32)
    filter_grad = jnp.transpose(summed, (1, 0, 2)).reshape(local_filters, share * tokens)
    conv_full = conv_seq.reshape(pre_gate.shape).astype(jnp.float32)
    gated_grad = gated_seq_grad.reshape(pre_gate.shape).astype(jnp.float32)
    mixed = (post_gate.astype(jnp.float32) * conv_full).astype(jnp.bfloat16)
    post_grad = (cotangent.astype(jnp.float32) * conv_full).astype(jnp.bfloat16)
    pre_grad = (gated_grad * values.astype(jnp.float32)).astype(jnp.bfloat16)
    value_grad = (gated_grad * pre_gate.astype(jnp.float32)).astype(jnp.bfloat16)
    return (mixed, pre_grad, value_grad, post_grad, filter_grad)


def solution(mesh):
    placed = (P("dp", "ctx"), P("dp", "ctx"), P("dp", "ctx"), P("ctx", "dp"), P("dp", "ctx"))
    groups, blocks = mesh.shape["dp"], mesh.shape["ctx"]

    def program(pre_gate, values, post_gate, filters, cotangent):
        kernels = groups == 2 and blocks >= 8 and blocks & (blocks - 1) == 0 and filters.shape[0] % 16 == 0
        return (body if kernels else plain_body)(pre_gate, values, post_gate, filters, cotangent)

    return jax.shard_map(
        program,
        mesh=mesh,
        in_specs=placed,
        out_specs=(P("dp", "ctx"), P("dp", "ctx"), P("dp", "ctx"), P("dp", "ctx"), P("ctx", "dp")),
        check_vma=False,
    )
```

```python
import math

import jax
import jax.numpy as jnp
import numpy as np
from jax import lax
from jax.experimental import pallas as pl
from jax.experimental.pallas import tpu as pltpu
from jax.sharding import PartitionSpec as P


LANES = 128
SUBLANES = 8
VMEM_BYTES = 60 * 1024 * 1024
HEAVY = 1 << 37


def dft_table(size):
    angle = np.arange(size)[:, None] * (2.0 * np.arange(size)[None, :] + 1.0) * (math.pi / (2 * size))
    strips = size // LANES
    cos, sin = (part.reshape(size, strips, 1, LANES) for part in (np.cos(angle), np.sin(angle)))
    return jnp.asarray(np.concatenate([cos, -sin], axis=2).reshape(size, 2 * size), jnp.bfloat16)


def dot(left, right):
    return jnp.dot(left, right, preferred_element_type=jnp.float32)


def back(spectrum, table):
    result = lax.dot_general(spectrum, table, (((1,), (1,)), ((), ())), preferred_element_type=jnp.float32)
    return result * (2.0 / table.shape[1])


def alternating():
    odd = lax.broadcasted_iota(jnp.int32, (SUBLANES, LANES), 1) % 2
    return 1.0 - 2.0 * odd.astype(jnp.float32)


def place(half_blocks):
    index = lax.axis_index("ctx")
    return index // half_blocks, lax.rem(index, half_blocks)


def real_of(strip):
    return pl.ds(2 * strip * LANES, LANES)


def imag_of(strip):
    return pl.ds((2 * strip + 1) * LANES, LANES)


def begin(copies):
    for copy in copies:
        copy.start()
    return copies


def end(copies):
    for copy in copies:
        copy.wait()


def call(kernel, name, operands, outputs, scratch, weight=1, vmem=VMEM_BYTES, space=pltpu.HBM):
    hbm = pl.BlockSpec(memory_space=pltpu.HBM)
    return pl.pallas_call(
        kernel,
        in_specs=[pl.BlockSpec(memory_space=space)] * len(operands),
        out_specs=[hbm] * len(outputs),
        out_shape=outputs,
        scratch_shapes=scratch,
        compiler_params=pltpu.CompilerParams(vmem_limit_bytes=vmem),
        cost_estimate=pl.CostEstimate(flops=weight, bytes_accessed=weight, transcendentals=0),
        name=name,
    )(*operands)


def gate(near, arrays, filters, repeats, half_blocks):
    rows_all, tokens = arrays[0].shape
    rows = rows_all // repeats
    share = rows // (2 * half_blocks)
    piece = (repeats, 2, share, tokens)

    def kernel(pre_ref, value_ref, post_ref, cot_ref, *refs):
        if near:
            filt_ref, out_ref, taps_ref, left_ref, right_ref, result_ref, in_sems, out_sems, filt_in, taps_out, taps_sems = refs
            loaded = begin([pltpu.make_async_copy(filt_ref, filt_in, taps_sems.at[0])])
        else:
            even_ref, odd_ref, left_ref, right_ref, result_ref, in_sems, out_sems = refs
        half, me = place(half_blocks)
        use_gated = half == 0 if near else half != 0

        def fetch(r, left, right):
            at = pl.ds(r * rows, rows)
            return (
                pltpu.make_async_copy(left.at[at], left_ref.at[r], in_sems.at[0, r]),
                pltpu.make_async_copy(right.at[at], right_ref.at[r], in_sems.at[1, r]),
            )

        @pl.when(use_gated)
        def _():
            for r in range(repeats):
                begin(fetch(r, pre_ref, value_ref))

        @pl.when(jnp.logical_not(use_gated))
        def _():
            for r in range(repeats):
                begin(fetch(r, cot_ref, post_ref))

        sent = []
        for r in range(repeats):
            end(fetch(r, pre_ref, value_ref))
            product = left_ref[r].astype(jnp.float32) * right_ref[r].astype(jnp.float32)
            product = product.astype(jnp.bfloat16).reshape(2, half_blocks, share, tokens)
            for side in range(2):
                result_ref[:, r, side] = product[side]
            for to in range(2 if near else 0):
                sent += begin([pltpu.make_async_copy(result_ref.at[:, r], out_ref.at[to, :, r], out_sems.at[to, r])])
        if near:
            end(loaded)
            taps_out[...] = filt_in[...].astype(jnp.bfloat16)
            sent += begin([pltpu.make_async_copy(taps_out, taps_ref, taps_sems.at[1])])
        else:
            for at in range(half_blocks // 2):
                for odd, target in enumerate((even_ref, odd_ref)):
                    source = result_ref.at[jnp.bitwise_xor(me, 2 * at + odd)]
                    sent += begin([pltpu.make_async_copy(source, target.at[at], out_sems.at[odd, at])])
        end(sent)

    own_shape = jax.ShapeDtypeStruct((half_blocks // 2, *piece), jnp.bfloat16)
    near_shape = jax.ShapeDtypeStruct((2, half_blocks, *piece), jnp.bfloat16)
    scratch = [
        pltpu.VMEM((repeats, rows, tokens), jnp.bfloat16),
        pltpu.VMEM((repeats, rows, tokens), jnp.bfloat16),
        pltpu.VMEM((half_blocks, *piece), jnp.bfloat16),
        pltpu.SemaphoreType.DMA((2, repeats)),
        pltpu.SemaphoreType.DMA((2, repeats if near else half_blocks // 2)),
    ]
    if near:
        scratch += [
            pltpu.VMEM(filters.shape, filters.dtype),
            pltpu.VMEM(filters.shape, jnp.bfloat16),
            pltpu.SemaphoreType.DMA((2,)),
        ]
    return call(
        kernel,
        "gate_near" if near else "gate_own",
        (*arrays, filters) if near else arrays,
        [near_shape, jax.ShapeDtypeStruct(filters.shape, jnp.bfloat16)] if near else [own_shape, own_shape],
        scratch,
    )


def exchange_own(even, odd, half_blocks):
    def swap(array, slot):
        return lax.ppermute(array, "ctx", [(i, i ^ slot) for i in range(2 * half_blocks)])

    far = half_blocks // 4
    groups = [([2 * at], swap(even[at : at + 1], 2 * at)) for at in reversed(range(far, half_blocks // 2))]
    odd = swap(odd, 1)
    groups += [([2 * at + 1], swap(odd[at : at + 1], 2 * at)) for at in reversed(range(far, half_blocks // 2))]
    for at in reversed(range(1, far)):
        pair = jnp.concatenate([even[at : at + 1], odd[at : at + 1]])
        groups.append(([2 * at, 2 * at + 1], swap(pair, 2 * at)))
    groups += [([0], even[:1]), ([1], odd[:1])]
    return groups


def finish(returned, arrays):
    half_blocks, _, repeats, sides, share, tokens = returned.shape
    count, rows = repeats * sides, half_blocks * share

    def kernel(recv_ref, pre_ref, value_ref, post_ref, cot_ref, *refs):
        out_refs, (held_ref, sems) = refs[:4], refs[4:]
        half, _ = place(half_blocks)
        sent = []
        for part in range(count):
            r, side = part // sides, part % sides
            at = pl.ds(part * rows, rows)
            conv = recv_ref[:, half, r, side].reshape(rows, tokens).astype(jnp.float32)
            grad = recv_ref[:, 1 - half, r, side].reshape(rows, tokens).astype(jnp.float32)
            for which, (factor_ref, result) in enumerate(
                ((post_ref, conv), (value_ref, grad), (pre_ref, grad), (cot_ref, conv))
            ):
                held_ref[which, part] = (factor_ref[at].astype(jnp.float32) * result).astype(jnp.bfloat16)
                sent += begin(
                    [pltpu.make_async_copy(held_ref.at[which, part], out_refs[which].at[at], sems.at[which, part])]
                )
        end(sent)

    shapes = [jax.ShapeDtypeStruct(arrays[0].shape, jnp.bfloat16)] * 4
    return pl.pallas_call(
        kernel,
        in_specs=[pl.BlockSpec(memory_space=pltpu.VMEM)] * 5,
        out_specs=[pl.BlockSpec(memory_space=pltpu.HBM)] * 4,
        out_shape=shapes,
        scratch_shapes=[
            pltpu.VMEM((4, count, rows, tokens), jnp.bfloat16),
            pltpu.SemaphoreType.DMA((4, count)),
        ],
        compiler_params=pltpu.CompilerParams(vmem_limit_bytes=VMEM_BYTES // 6),
        name="finish",
    )(returned, *arrays)


def pack_taps(taps, pair, half_blocks):
    share, lags = taps.shape

    def kernel(taps_ref, pair_ref, out_ref, held_ref, sems):
        half, _ = place(half_blocks)
        end(
            begin(
                [
                    pltpu.make_async_copy(taps_ref, held_ref.at[half], sems.at[0]),
                    pltpu.make_async_copy(pair_ref, held_ref.at[1 - half], sems.at[1]),
                ]
            )
        )
        end(begin([pltpu.make_async_copy(held_ref, out_ref, sems.at[2])]))

    return call(
        kernel,
        "pack_taps",
        (taps, pair),
        [jax.ShapeDtypeStruct((2, share, lags), jnp.bfloat16)],
        [pltpu.VMEM((2, share, lags), jnp.bfloat16), pltpu.SemaphoreType.DMA((3,))],
        weight=HEAVY,
        vmem=VMEM_BYTES // 12,
    )[0]


def transform_taps(here, there, half_blocks, groups, table):
    sides, share, lags = here.shape
    size = table.shape[0]
    count = groups * lags // size
    rows, width = sides * share, 2 * size

    def kernel(here_ref, there_ref, table_hbm, out_hbm, piece_ref, table_ref, stage_ref, out_ref, sems):
        sources = (here_ref, there_ref)
        loads = begin([pltpu.make_async_copy(ref, piece_ref.at[at], sems.at[at]) for at, ref in enumerate(sources)])
        tabled = begin([pltpu.make_async_copy(table_hbm, table_ref, sems.at[2])])
        half, _ = place(half_blocks)
        group = lax.axis_index("dp")
        end(loads)
        for at in range(2):
            first = (group if at == 0 else 1 - group) * (lags // size)
            for side in range(sides):
                for k in range(lags // size):
                    piece = piece_ref[at, side, :, k * size : (k + 1) * size]
                    stage_ref[first + k, side * share : (side + 1) * share] = piece
        end(tabled)
        spectrum = dot(stage_ref[...].reshape(count * rows, size), table_ref[...]).reshape(count, rows, width)
        turn = jnp.where(half == 0, 1.0, -1.0).astype(jnp.float32)
        sign = alternating()[:1]
        sent = []
        for k in range(count):
            for strip in range(size // LANES):
                re = slice(2 * strip * LANES, (2 * strip + 1) * LANES)
                im = slice((2 * strip + 1) * LANES, (2 * strip + 2) * LANES)
                real, imag = spectrum[k, :, re], spectrum[k, :, im]
                if k > 0:
                    real, imag = real - sign * spectrum[k - 1, :, im], imag + sign * spectrum[k - 1, :, re]
                out_ref[k, :, re] = real.astype(jnp.bfloat16)
                out_ref[k, :, im] = (turn * imag).astype(jnp.bfloat16)
            sent += begin([pltpu.make_async_copy(out_ref.at[k], out_hbm.at[k], sems.at[3 + k])])
        end(sent)

    return call(
        kernel,
        "taps",
        (here, there, table),
        [jax.ShapeDtypeStruct((count, rows, width), jnp.bfloat16)],
        [
            pltpu.VMEM((2, sides, share, lags), jnp.bfloat16),
            pltpu.VMEM((size, width), jnp.bfloat16),
            pltpu.VMEM((count, rows, size), jnp.bfloat16),
            pltpu.VMEM((count, rows, width), jnp.bfloat16),
            pltpu.SemaphoreType.DMA((3 + count,)),
        ],
        vmem=VMEM_BYTES // 6,
    )[0]


def add(total, term):
    return term if total is None else (total[0] + term[0], total[1] + term[1])


def times(a, b):
    return a[0] * b[0] - a[1] * b[1], a[0] * b[1] + a[1] * b[0]


def conj_times(a, b):
    return a[0] * b[0] + a[1] * b[1], a[0] * b[1] - a[1] * b[0]


def transform(stage_ref, table_ref, spec_ref):
    width = spec_ref.shape[-1]
    staged = stage_ref[...].reshape(-1, stage_ref.shape[-1])
    for strip in range(width // (2 * LANES)):
        columns = slice(2 * strip * LANES, 2 * (strip + 1) * LANES)
        spec_ref[..., columns] = dot(staged, table_ref[:, columns]).reshape(spec_ref.shape[:-1] + (2 * LANES,))


def stage_all(near_ref, own_refs, slots, near_stage, far_stage, own_stage, half_blocks, far_rows):
    count, _, size = near_stage.shape
    tokens = near_ref.shape[2]
    merge = size // tokens
    half, me = place(half_blocks)
    for k in range(count):
        outer, inner = order(k, count, half, True), order(k, count, half, False)
        for q in range(merge):
            lanes = pl.ds(q * tokens, tokens)
            near_stage[k, :, lanes] = near_ref[half * half_blocks + outer * merge + q]
            at = 0
            for first, rows in far_rows:
                far = near_ref[(1 - half) * half_blocks + inner * merge + q, pl.ds(first, rows)]
                far_stage[k, at : at + rows, lanes] = far
                at += rows
    for group, ref in zip(slots, own_refs):
        for at, slot in enumerate(group):
            position = jnp.bitwise_xor(me, slot)
            k = order(position // merge, count, half, False)
            start = pl.multiple_of(lax.rem(position, merge) * tokens, tokens)
            own_stage[k, :, pl.ds(start, tokens)] = ref[at]


def order(k, count, half, outer):
    return jnp.where(half == (0 if outer else 1), k, count - 1 - k)


def tile_loop(rows, body):
    @pl.loop(0, rows // SUBLANES)
    def _(tile):
        body(pl.multiple_of(tile * SUBLANES, SUBLANES))


def parts(ref, k, row, strip):
    return ref[k, row, real_of(strip)], ref[k, row, imag_of(strip)]


def keep(ref, k, row, strip, value):
    ref[k, row, real_of(strip)], ref[k, row, imag_of(strip)] = value


def give_back(prod_ref, table_ref, held_ref, out_ref, sems, outer, half_blocks):
    count, rows, width = prod_ref.shape
    merge, tokens = held_ref.shape[1], held_ref.shape[3]
    half, _ = place(half_blocks)
    sent = []
    spectrum = prod_ref[...].astype(jnp.bfloat16).reshape(count * rows, width)
    for q in range(merge):
        result = back(spectrum, table_ref[q * tokens : (q + 1) * tokens])
        held_ref[:, q] = result.astype(jnp.bfloat16).reshape(count, rows, tokens)
        for k in range(count):
            block = order(k, count, half, outer)
            sent += begin(
                [pltpu.make_async_copy(held_ref.at[k, q], out_ref.at[block * merge + q], sems.at[k, q])]
            )
    end(sent)


def results(near, own, filt, half_blocks, table):
    slots = [group for group, _ in own]
    _, rows, tokens = near.shape
    size, width = table.shape
    merge = size // tokens
    count = half_blocks // merge
    filters = filt.shape[1]

    def kernel(near_ref, filt_in, table_ref, *refs):
        own_refs, out_hbm = refs[: len(own)], refs[len(own)]
        stage_ref, filt_ref, spec_ref, prod_ref, held_ref, out_sems = refs[len(own) + 1 :]
        near_stage, far_stage, own_stage = (stage_ref.at[which] for which in range(3))
        stage_all(near_ref, own_refs, slots, near_stage, far_stage, own_stage, half_blocks, [(0, rows)])
        filt_ref[...] = filt_in[...].astype(jnp.float32)
        transform(stage_ref, table_ref, spec_ref)
        half, _ = place(half_blocks)

        def tile(first):
            row = pl.ds(first, SUBLANES)
            tap_row = pl.ds(pl.multiple_of(lax.rem(first, filters), SUBLANES), SUBLANES)
            for strip in range(size // LANES):
                taps = [parts(filt_ref, k, tap_row, strip) for k in range(2 * count)]
                near, far, own = ([parts(spec_ref.at[which], k, row, strip) for k in range(count)] for which in range(3))
                for out in range(count):
                    total = None
                    for k in range(out + 1):
                        total = add(total, times(taps[out - k], near[k]))
                    keep(prod_ref.at[0], out, row, strip, total)
                for out in range(count):
                    total = None
                    for k in range(out + 1):
                        total = add(total, conj_times(taps[out - k], own[k]))
                    for k in range(count):
                        total = add(total, conj_times(taps[count + out - k], far[k]))
                    keep(prod_ref.at[1], out, row, strip, total)

        tile_loop(rows, tile)
        spectrum = prod_ref[...].astype(jnp.bfloat16).reshape(2 * count * rows, width)
        sent = []
        for q in range(merge):
            result = back(spectrum, table_ref[q * tokens : (q + 1) * tokens]).astype(jnp.bfloat16)
            held_ref[:, :, q] = result.reshape(2, count, rows, tokens)
            for which in range(2):
                for k in range(count):
                    position = order(k, count, half, which == 0) * merge + q
                    copy = pltpu.make_async_copy(
                        held_ref.at[which, k, q], out_hbm.at[position, which], out_sems.at[which, k, q]
                    )
                    sent += begin([copy])
        end(sent)

    return call(
        kernel,
        "results",
        (near, filt, table, *[array for _, array in own]),
        [jax.ShapeDtypeStruct((half_blocks, 2, rows, tokens), jnp.bfloat16)],
        [
            pltpu.VMEM((3, count, rows, size), jnp.bfloat16),
            pltpu.VMEM((2 * count, filters, width), jnp.float32),
            pltpu.VMEM((3, count, rows, width), jnp.float32),
            pltpu.VMEM((2, count, rows, width), jnp.float32),
            pltpu.VMEM((2, count, merge, rows, tokens), jnp.bfloat16),
            pltpu.SemaphoreType.DMA((2, count, merge)),
        ],
        vmem=VMEM_BYTES // 2,
        weight=HEAVY,
        space=pltpu.VMEM,
    )[0]


def lag_products(near_ref, near_rows, other_ref, other_rows, strip, totals):
    count = near_ref.shape[0]
    sums = [None] * len(totals)
    for near_row, other_row in zip(near_rows, other_rows):
        near = [parts(near_ref, k, pl.ds(near_row, SUBLANES), strip) for k in range(count)]
        other = [parts(other_ref, k, pl.ds(other_row, SUBLANES), strip) for k in range(count)]
        for at, total in enumerate(totals):
            for a in range(count):
                if 0 <= total - a < count:
                    sums[at] = add(sums[at], conj_times(near[a], other[total - a]))
    return sums


def repeat_rows(first, step, repeats):
    return [pl.multiple_of(r * step + first, SUBLANES) for r in range(repeats)]


def join_lags(ref, row, joint_ref, base):
    lags, size = ref.shape[0], ref.shape[2] // 2
    sign = alternating()[:1]
    for k in range(lags):
        for strip in range(size // LANES):
            real, imag = parts(ref, k, row, strip)
            if k + 1 < lags:
                next_real, next_imag = parts(ref, k + 1, row, strip)
                real, imag = real + sign * next_imag, imag - sign * next_real
            keep(joint_ref, base + k, slice(None), strip, (real.astype(jnp.bfloat16), imag.astype(jnp.bfloat16)))


def filter_terms(near, own, filters, half_blocks, table):
    slots = [group for group, _ in own]
    _, rows, tokens = near.shape
    size, width = table.shape
    merge = size // tokens
    count = half_blocks // merge
    kept, lags = filters // 2, count * size
    repeats = rows // filters

    def kernel(near_ref, *refs):
        own_refs, refs = refs[: len(own)], refs[len(own) :]
        table_ref, give_hbm, mine_hbm, theirs_hbm, stage_ref, far_stage, spec_ref, far_ref, local_ref, cross_ref, joint_ref = refs[:11]
        held_ref, give_ref, mine_ref, theirs_ref, sems = refs[11:]
        half, _ = place(half_blocks)
        group = lax.axis_index("dp")
        turn = jnp.where(half == 0, 1.0, -1.0).astype(jnp.float32)
        mine = pl.multiple_of(half * kept, SUBLANES)
        other = pl.multiple_of((1 - half) * kept, SUBLANES)
        far_rows = [(pl.multiple_of(r * filters + half * kept, kept), kept) for r in range(repeats)]
        stage_all(near_ref, own_refs, slots, stage_ref.at[0], far_stage, stage_ref.at[1], half_blocks, far_rows)
        transform(stage_ref, table_ref, spec_ref)
        transform(far_stage, table_ref, far_ref)
        near_spec, own_spec = spec_ref.at[0], spec_ref.at[1]

        def local_tile(first):
            rows_at = repeat_rows(first, filters, repeats)
            for strip in range(size // LANES):
                totals = [count - 1 - k for k in range(count)]
                sums = lag_products(near_spec, rows_at, own_spec, rows_at, strip, totals)
                for k, (real, imag) in enumerate(sums):
                    keep(local_ref, k, pl.ds(first, SUBLANES), strip, (real, turn * imag))

        tile_loop(filters, local_tile)

        def cross_tile(first):
            row = pl.ds(first, SUBLANES)
            at = pl.ds(pl.multiple_of(mine + first, SUBLANES), SUBLANES)
            near_at, far_at = repeat_rows(mine + first, filters, repeats), repeat_rows(first, kept, repeats)
            for strip in range(size // LANES):
                totals = [2 * count - 1 - k for k in range(1, 2 * count)]
                sums = lag_products(near_spec, near_at, far_ref, far_at, strip, totals)
                keep(cross_ref, 0, row, strip, parts(local_ref, 0, at, strip))
                for k, (real, imag) in enumerate(sums, 1):
                    value = (real, turn * imag)
                    keep(cross_ref, k, row, strip, add(value, parts(local_ref, k, at, strip)) if k < count else value)

        tile_loop(kept, cross_tile)
        join_lags(cross_ref, slice(None), joint_ref, 0)
        join_lags(local_ref, pl.ds(other, kept), joint_ref, 2 * count)
        result = back(joint_ref[...].reshape(3 * count * kept, width), table_ref[...]).reshape(3, count, kept, size)
        held_ref[...] = result[:2]
        for k in range(count):
            give_ref[:, k * size : (k + 1) * size] = result[2, k].astype(jnp.bfloat16)
        sent = begin([pltpu.make_async_copy(give_ref, give_hbm, sems.at[1])])
        for k in range(count):
            columns = slice(k * size, (k + 1) * size)
            mine_ref[:, columns] = held_ref[group, k]
            theirs_ref[:, columns] = held_ref[1 - group, k].astype(jnp.bfloat16)
        sent += begin(
            [
                pltpu.make_async_copy(theirs_ref, theirs_hbm, sems.at[2]),
                pltpu.make_async_copy(mine_ref, mine_hbm, sems.at[3]),
            ]
        )
        end(sent)

    return call(
        kernel,
        "filter_terms",
        (near, *[array for _, array in own], table),
        [
            jax.ShapeDtypeStruct((kept, lags), jnp.bfloat16),
            jax.ShapeDtypeStruct((kept, lags), jnp.float32),
            jax.ShapeDtypeStruct((kept, lags), jnp.bfloat16),
        ],
        [
            pltpu.VMEM((2, count, rows, size), jnp.bfloat16),
            pltpu.VMEM((count, rows // 2, size), jnp.bfloat16),
            pltpu.VMEM((2, count, rows, width), jnp.float32),
            pltpu.VMEM((count, rows // 2, width), jnp.float32),
            pltpu.VMEM((count, filters, width), jnp.float32),
            pltpu.VMEM((2 * count, kept, width), jnp.float32),
            pltpu.VMEM((3 * count, kept, width), jnp.bfloat16),
            pltpu.VMEM((2, count, kept, size), jnp.float32),
            pltpu.VMEM((kept, lags), jnp.bfloat16),
            pltpu.VMEM((kept, lags), jnp.float32),
            pltpu.VMEM((kept, lags), jnp.bfloat16),
            pltpu.SemaphoreType.DMA((4,)),
        ],
        vmem=VMEM_BYTES - (5 << 20),
        space=pltpu.VMEM,
    )


def body(pre_gate, values, post_gate, filters, cotangent):
    blocks = lax.axis_size("ctx")
    groups = lax.axis_size("dp")
    half_blocks = blocks // 2
    local_rows, tokens = pre_gate.shape
    local_filters = filters.shape[0]
    repeats = local_rows // (local_filters * blocks)
    rows = 2 * local_filters * repeats
    table = dft_table(2 * tokens)
    arrays = (pre_gate, values, post_gate, cotangent)
    sides = [list(range(half_blocks)), list(range(half_blocks, blocks))]

    def swap(array):
        return lax.ppermute(array, "ctx", [(i, i ^ half_blocks) for i in range(blocks)])

    def other_group(array):
        return lax.ppermute(array, "dp", [(0, 1), (1, 0)])

    near, taps = gate(True, arrays, filters, repeats, half_blocks)
    even, odd = gate(False, arrays, filters, repeats, half_blocks)
    here = pack_taps(taps, swap(taps), half_blocks)
    odd, here = lax.optimization_barrier((odd, here))
    near = lax.all_to_all(near.reshape(blocks, rows, tokens), "ctx", split_axis=0, concat_axis=0, tiled=True)
    shape = (half_blocks // 2, rows, tokens)
    own = exchange_own(even.reshape(shape), odd.reshape(shape), half_blocks)
    filt = transform_taps(here, other_group(here), half_blocks, groups, table)

    result = results(near, own, filt, half_blocks, table)
    result, near = lax.optimization_barrier((result, near))
    returned = lax.all_to_all(
        result, "ctx", split_axis=0, concat_axis=0, tiled=True, axis_index_groups=sides
    )
    give, mine, theirs = filter_terms(near, own, 2 * local_filters, half_blocks, table)
    halves = tuple(
        lax.ppermute(give, ("dp", "ctx"), [(g * blocks + i, i ^ half_blocks) for i in range(blocks)]) for g in range(groups)
    )
    theirs = other_group(theirs)
    outputs = finish(returned.reshape(half_blocks, 2, repeats, 2, local_filters, tokens), arrays)
    mine, mixed, pre_grad, value_grad, post_grad = lax.optimization_barrier((mine, *outputs))
    filter_grad = mine + (halves[1].astype(jnp.float32) + halves[0].astype(jnp.float32)) + theirs.astype(jnp.float32)
    return (mixed, pre_grad, value_grad, post_grad, filter_grad)


def matmul(left, right):
    return jnp.dot(left, right, precision=lax.Precision.HIGHEST, preferred_element_type=jnp.float32)


def contract(form, left, right):
    return jnp.einsum(
        form, left, right, precision=lax.Precision.HIGHEST, preferred_element_type=jnp.float32
    )


def phases(height, width, modulus):
    product = lax.broadcasted_iota(jnp.int32, (height, width), 0) * lax.broadcasted_iota(
        jnp.int32, (height, width), 1
    )
    return (product % modulus).astype(jnp.float32) * (2.0 * math.pi / modulus)


def build_tables(blocks, tokens):
    factor = 1
    for candidate in range(1, tokens + 1):
        if tokens % candidate == 0 and candidate * candidate <= tokens:
            factor = candidate
    second = tokens // factor
    rows = blocks + 1
    total = 2 * blocks * tokens
    first_angle = phases(rows, blocks, 2 * blocks)
    twist_angle = phases(rows, tokens, total)
    inner_angle = phases(factor, factor, factor)
    middle_angle = phases(factor, second, tokens)
    outer_angle = phases(second, second, second)
    back_angle = phases(blocks, rows, 2 * blocks)
    column = lax.broadcasted_iota(jnp.int32, (blocks, rows), 1)
    weight = jnp.where((column == 0) | (column == blocks), 1.0, 2.0).astype(jnp.float32) / total
    return {
        "first_cos": jnp.cos(first_angle),
        "first_nsin": -jnp.sin(first_angle),
        "twist_cos": jnp.cos(twist_angle),
        "twist_sin": jnp.sin(twist_angle),
        "inner_cos": jnp.cos(inner_angle),
        "inner_sin": jnp.sin(inner_angle),
        "middle_cos": jnp.cos(middle_angle),
        "middle_sin": jnp.sin(middle_angle),
        "outer_cos": jnp.cos(outer_angle),
        "outer_sin": jnp.sin(outer_angle),
        "back_cos": weight * jnp.cos(back_angle),
        "back_sin": weight * jnp.sin(back_angle),
    }


def expand(table, ndim):
    return table.reshape((table.shape[0],) + (1,) * (ndim - 2) + (table.shape[1],))


def block_table(cos_part, sin_part):
    return jnp.stack([jnp.stack([cos_part, sin_part]), jnp.stack([-sin_part, cos_part])])


def wave(real_part, imag_part, tables, sign):
    shape = real_part.shape
    factor = tables["inner_cos"].shape[0]
    second = tables["outer_cos"].shape[0]
    stacked = jnp.stack(
        [real_part.reshape(-1, factor, second), imag_part.reshape(-1, factor, second)]
    )
    inner_table = block_table(tables["inner_cos"], sign * tables["inner_sin"])
    middle = contract("prab,pqac->qrcb", stacked, inner_table)
    middle_cos = tables["middle_cos"]
    middle_sin = sign * tables["middle_sin"]
    real_turn = middle[0] * middle_cos - middle[1] * middle_sin
    imag_turn = middle[0] * middle_sin + middle[1] * middle_cos
    turned = jnp.stack([real_turn, imag_turn])
    outer_table = block_table(tables["outer_cos"], sign * tables["outer_sin"])
    result = contract("prcb,pqbd->qrdc", turned, outer_table)
    return (result[0].reshape(shape), result[1].reshape(shape))


def finish_forward(real_first, imag_first, tables):
    ndim = real_first.ndim
    twist_cos = expand(tables["twist_cos"], ndim)
    twist_sin = expand(tables["twist_sin"], ndim)
    real_twist = real_first * twist_cos + imag_first * twist_sin
    imag_twist = imag_first * twist_cos - real_first * twist_sin
    return wave(real_twist, imag_twist, tables, -1.0)


def spectrum(signal, tables):
    flat = signal.reshape(signal.shape[0], -1)
    shape = (tables["first_cos"].shape[0],) + signal.shape[1:]
    real_first = matmul(tables["first_cos"], flat).reshape(shape)
    imag_first = matmul(tables["first_nsin"], flat).reshape(shape)
    return finish_forward(real_first, imag_first, tables)


def inverse_prepare(real_spec, imag_spec, tables):
    ndim = real_spec.ndim
    real_wave, imag_wave = wave(real_spec, imag_spec, tables, 1.0)
    twist_cos = expand(tables["twist_cos"], ndim)
    twist_sin = expand(tables["twist_sin"], ndim)
    real_twist = real_wave * twist_cos - imag_wave * twist_sin
    imag_twist = real_wave * twist_sin + imag_wave * twist_cos
    rows = real_spec.shape[0]
    return (real_twist.reshape(rows, -1), imag_twist.reshape(rows, -1))


def inverse_full(real_spec, imag_spec, tables):
    real_flat, imag_flat = inverse_prepare(real_spec, imag_spec, tables)
    signal = matmul(tables["back_cos"], real_flat) - matmul(tables["back_sin"], imag_flat)
    return signal.reshape((tables["back_cos"].shape[0],) + real_spec.shape[1:])


def plain_body(pre_gate, values, post_gate, filters, cotangent):
    blocks = lax.axis_size("ctx")
    groups = lax.axis_size("dp")
    local_rows = pre_gate.shape[0]
    tokens = pre_gate.shape[1]
    local_filters = filters.shape[0]
    repeats = local_rows // (local_filters * blocks)
    share = blocks // groups
    tables = build_tables(blocks, tokens)
    gated = (pre_gate.astype(jnp.float32) * values.astype(jnp.float32)).astype(jnp.bfloat16)
    conv_grad = (cotangent.astype(jnp.float32) * post_gate.astype(jnp.float32)).astype(jnp.bfloat16)
    gated_blocks = gated.reshape(repeats, blocks, local_filters, tokens)
    grad_blocks = conv_grad.reshape(repeats, blocks, local_filters, tokens)
    tap_local = jnp.transpose(filters.reshape(local_filters, share, tokens), (1, 0, 2))
    piece = lax.all_gather(tap_local, "dp", axis=0, tiled=True)
    count = piece.shape[0]
    flat = piece.reshape(count, -1)
    cos_cols = tables["first_cos"]
    sin_cols = tables["first_nsin"]
    real_first = matmul(cos_cols, flat)
    imag_first = matmul(sin_cols, flat)
    spec_shape = (blocks + 1, 1, local_filters, tokens)
    filt_real, filt_imag = finish_forward(
        real_first.reshape(spec_shape), imag_first.reshape(spec_shape), tables
    )

    def single_spectrum(received):
        signal = received.reshape(blocks, -1, received.shape[2], received.shape[3])
        return spectrum(signal.astype(jnp.float32), tables)

    gated_real, gated_imag = single_spectrum(
        lax.all_to_all(gated_blocks, "ctx", split_axis=1, concat_axis=0, tiled=True)
    )
    prod_real = gated_real * filt_real - gated_imag * filt_imag
    prod_imag = gated_real * filt_imag + gated_imag * filt_real
    result = inverse_full(prod_real, prod_imag, tables).astype(jnp.bfloat16)
    conv_chan = result.reshape(blocks * repeats, 1, local_filters, tokens)
    conv_seq = lax.all_to_all(conv_chan, "ctx", split_axis=0, concat_axis=1, tiled=True)
    grad_real, grad_imag = single_spectrum(
        lax.all_to_all(grad_blocks, "ctx", split_axis=1, concat_axis=0, tiled=True)
    )
    prod_real = filt_real * grad_real + filt_imag * grad_imag
    prod_imag = filt_real * grad_imag - filt_imag * grad_real
    result = inverse_full(prod_real, prod_imag, tables).astype(jnp.bfloat16)
    gated_chan_grad = result.reshape(blocks * repeats, 1, local_filters, tokens)
    gated_seq_grad = lax.all_to_all(gated_chan_grad, "ctx", split_axis=0, concat_axis=1, tiled=True)
    cross_real = jnp.sum(gated_real * grad_real + gated_imag * grad_imag, axis=1)
    cross_imag = jnp.sum(gated_real * grad_imag - gated_imag * grad_real, axis=1)
    wave_real, wave_imag = inverse_prepare(cross_real, cross_imag, tables)
    cos_rows = tables["back_cos"]
    sin_rows = tables["back_sin"]
    term = matmul(cos_rows, wave_real) - matmul(sin_rows, wave_imag)
    summed = lax.psum_scatter(
        term.reshape(lax.axis_size("dp") * share, local_filters, tokens).astype(jnp.bfloat16),
        "dp",
        scatter_dimension=0,
        tiled=True,
    ).astype(jnp.float32)
    filter_grad = jnp.transpose(summed, (1, 0, 2)).reshape(local_filters, share * tokens)
    conv_full = conv_seq.reshape(pre_gate.shape).astype(jnp.float32)
    gated_grad = gated_seq_grad.reshape(pre_gate.shape).astype(jnp.float32)
    mixed = (post_gate.astype(jnp.float32) * conv_full).astype(jnp.bfloat16)
    post_grad = (cotangent.astype(jnp.float32) * conv_full).astype(jnp.bfloat16)
    pre_grad = (gated_grad * values.astype(jnp.float32)).astype(jnp.bfloat16)
    value_grad = (gated_grad * pre_gate.astype(jnp.float32)).astype(jnp.bfloat16)
    return (mixed, pre_grad, value_grad, post_grad, filter_grad)


def solution(mesh):
    placed = (P("dp", "ctx"), P("dp", "ctx"), P("dp", "ctx"), P("ctx", "dp"), P("dp", "ctx"))
    groups, blocks = mesh.shape["dp"], mesh.shape["ctx"]

    def program(pre_gate, values, post_gate, filters, cotangent):
        kernels = groups == 2 and blocks >= 8 and blocks & (blocks - 1) == 0 and filters.shape[0] % 16 == 0
        return (body if kernels else plain_body)(pre_gate, values, post_gate, filters, cotangent)

    return jax.shard_map(
        program,
        mesh=mesh,
        in_specs=placed,
        out_specs=(P("dp", "ctx"), P("dp", "ctx"), P("dp", "ctx"), P("dp", "ctx"), P("ctx", "dp")),
        check_vma=False,
    )
```
